32 devices in a mesh: row: 2 (over core), ax: 2 (over x), az: 8 (over z, y).
Axes of the slice: x: 2, y: 2, z: 4, core: 2. Of those that a mesh axis runs over, the one named last changes fastest.
Arguments:
- density: float32 [2, 4, 256, 512], P('row', 'ax', 'az'), may hold values from 0.8 to 1.6
- velocity: float32 [2, 3, 4, 256, 512], P('row', None, 'ax', 'az'), may hold values from -1.5 to 1.5
- pressure: float32 [2, 4, 256, 512], P('row', 'ax', 'az'), may hold values from 0.4 to 1.2
- offsets: int32 [3], replicated, may hold values from 0 to 255
Outputs:
- final_state: float32 [2, 5, 4, 256, 512], P('row', None, 'ax', 'az')
The draws below stay inside these ranges and needn't reach their ends.
All inputs are finite; a program needn't handle non-finite values.
Results may differ from the reference program's by a relative error of at most 0.00002.
Values sent between devices are 32-bit elements; how exact they have to be, the bound alone decides.
A program may use at most 128 MiB of HBM per device.

```python
import math
import jax
import jax.numpy as jnp
from jax import lax

CR = 512
SUBSTEPS = 3
NT = 256
NZ = 4


def draw_velocity(key, part):
    noise_key = jax.random.fold_in(key, 11)
    phase_key = jax.random.fold_in(key, 12)
    size_key = jax.random.fold_in(key, 13)
    noise_field = jnp.clip(0.3 * jax.random.normal(noise_key, (2, 3, NZ, NT, CR), jnp.float32), -1.2, 1.2)
    phase_shift = jax.random.randint(phase_key, (2, 1, NZ, 1, 1), 0, 4)
    azimuth = jnp.arange(NT, dtype=jnp.int32).reshape(1, 1, 1, NT, 1)
    sign_pattern = jnp.where((azimuth + phase_shift) % 4 < 2, 1.0, -1.0).astype(jnp.float32)
    magnitude = 1.2 + 0.3 * jax.random.uniform(size_key, (2, 1, NZ, NT, CR), jnp.float32)
    radial_index = jnp.arange(CR, dtype=jnp.int32).reshape(1, 1, 1, 1, CR)
    component = jnp.arange(3, dtype=jnp.int32).reshape(1, 3, 1, 1, 1)
    inner_band = (radial_index < CR // 4) & (component == 1)
    return jnp.where(inner_band, sign_pattern * magnitude, noise_field).astype(jnp.float32)


def level_of(key, dims, split, low, high):
    gain = 1.0
    for position, parts in split:
        draws = jax.random.uniform(jax.random.fold_in(jax.random.fold_in(key, 6), position), (parts,), jnp.float32, low / len(split), high / len(split))
        gain = gain * jnp.repeat(jnp.exp(draws), dims[position] // parts).reshape((-1,) + (1,) * (len(dims) - 1 - position))
    return gain


def setup_inputs(seed: int = 0) -> dict:
    streams_of = jax.random.split(jax.random.key(seed), 5)
    return {
        "density": jnp.clip(0.8 + 0.8 * jax.random.uniform(streams_of[0], (2, NZ, NT, CR), jnp.float32) ** level_of(streams_of[0], (2, NZ, NT, CR), ((0, 2), (1, 2), (2, 8)), -0.2, 0.2), 0.8, 1.6),
        "velocity": draw_velocity(jax.random.fold_in(streams_of[4], 71), 0),
        "pressure": jnp.clip(0.4 + 0.800000042 * jax.random.uniform(streams_of[2], (2, NZ, NT, CR), jnp.float32) ** level_of(streams_of[2], (2, NZ, NT, CR), ((0, 2), (1, 2), (2, 8)), -0.2, 0.2), 0.4, 1.2),
        "offsets": jax.random.randint(streams_of[3], (SUBSTEPS,), 0, NT).astype(jnp.int32),
    }


HEAT_RATIO = 1.4
VISCOSITY = 0.8
CONDUCTION = 0.6
TIME_STEP = 0.1
AXIAL_FLUX = 1.0
AXIAL_CURVE = 4.0


def conserved(density, velocity, pressure):
    momentum = density[:, None] * velocity
    energy = pressure / (HEAT_RATIO - 1.0) + 0.5 * density * jnp.sum(velocity * velocity, axis=1)
    return jnp.concatenate([density[:, None], momentum, energy[:, None]], axis=1)


def primitive(state):
    vel_theta = state[:, 1] / state[:, 0]
    vel_radial = state[:, 2] / state[:, 0]
    vel_axial = state[:, 3] / state[:, 0]
    press = (HEAT_RATIO - 1.0) * (state[:, 4] - 0.5 * (state[:, 1] * vel_theta + state[:, 2] * vel_radial + state[:, 3] * vel_axial))
    return (vel_theta, vel_radial, vel_axial, press / state[:, 0], press)


def fluxes(state, values, direction):
    normal_vel = values[direction]
    press = values[4]
    flux_terms = [state[:, 0] * normal_vel, state[:, 1] * normal_vel, state[:, 2] * normal_vel, state[:, 3] * normal_vel, (state[:, 4] + press) * normal_vel]
    flux_terms[1 + direction] = flux_terms[1 + direction] + press
    return flux_terms


def laplace(center, theta_lo, theta_hi, radial_lo, radial_hi, axial_lo, axial_hi, radius, dtheta):
    beside_all = (theta_hi - 2.0 * center + theta_lo) / (radius * dtheta) ** 2
    across = ((radius + 0.5) * (radial_hi - center) - (radius - 0.5) * (center - radial_lo)) / radius
    return beside_all + across + AXIAL_CURVE * (axial_hi - 2.0 * center + axial_lo)


def tendency(center, theta_lo, theta_hi, radial_lo, radial_hi, axial_lo, axial_hi, radius, dtheta):
    values_c = primitive(center)
    values_tl = primitive(theta_lo)
    values_th = primitive(theta_hi)
    values_rl = primitive(radial_lo)
    values_rh = primitive(radial_hi)
    values_zl = primitive(axial_lo)
    values_zh = primitive(axial_hi)
    flux_tl = fluxes(theta_lo, values_tl, 0)
    flux_th = fluxes(theta_hi, values_th, 0)
    flux_rl = fluxes(radial_lo, values_rl, 1)
    flux_rh = fluxes(radial_hi, values_rh, 1)
    flux_zl = fluxes(axial_lo, values_zl, 2)
    flux_zh = fluxes(axial_hi, values_zh, 2)
    result = []
    for field_index in range(5):
        divergence = -(flux_th[field_index] - flux_tl[field_index]) / (2.0 * radius * dtheta)
        divergence = divergence - ((radius + 1.0) * flux_rh[field_index] - (radius - 1.0) * flux_rl[field_index]) / (2.0 * radius)
        divergence = divergence - AXIAL_FLUX * (flux_zh[field_index] - flux_zl[field_index])
        result.append(divergence)

    def viscous(which):
        return laplace(values_c[which], values_tl[which], values_th[which], values_rl[which], values_rh[which], values_zl[which], values_zh[which], radius, dtheta)

    density_now = center[:, 0]
    result[1] = result[1] - density_now * values_c[0] * values_c[1] / radius + VISCOSITY * (viscous(0) - values_c[0] / radius ** 2 + (values_th[1] - values_tl[1]) / (radius ** 2 * dtheta))
    result[2] = result[2] + (density_now * values_c[0] * values_c[0] + values_c[4]) / radius + VISCOSITY * (viscous(1) - values_c[1] / radius ** 2 - (values_th[0] - values_tl[0]) / (radius ** 2 * dtheta))
    result[3] = result[3] + VISCOSITY * viscous(2)
    result[4] = result[4] + CONDUCTION * viscous(3)
    return jnp.stack(result, axis=1)


def full_rate(state, shift, radius, dtheta):
    axial_sign = jnp.array([1.0, 1.0, 1.0, -1.0, 1.0], dtype=jnp.float32).reshape(5, 1, 1)
    wall_sign = jnp.array([1.0, -1.0, -1.0, -1.0, 1.0], dtype=jnp.float32).reshape(5, 1, 1)
    top_plane = state[:, :, -1] * axial_sign
    partner = top_plane[::-1]
    ghost_rotor = jnp.roll(partner[0], -shift, axis=1)
    ghost_stator = jnp.roll(partner[1], shift, axis=1)
    upper_ghost = jnp.stack([ghost_rotor, ghost_stator])[:, :, None]
    padded = jnp.concatenate([state[:, :, :1], state, upper_ghost], axis=2)

    def plane_rate(section):
        plane_block = lax.dynamic_slice_in_dim(padded, section, 3, 2)
        center = plane_block[:, :, 1]
        theta_lo = jnp.roll(center, 1, axis=2)
        theta_hi = jnp.roll(center, -1, axis=2)
        radial_lo = jnp.concatenate([center[..., :1] * wall_sign, center[..., :-1]], axis=3)
        radial_hi = jnp.concatenate([center[..., 1:], center[..., -1:] * wall_sign], axis=3)
        return tendency(center, theta_lo, theta_hi, radial_lo, radial_hi, plane_block[:, :, 0], plane_block[:, :, 2], radius, dtheta)

    planes = lax.map(plane_rate, jnp.arange(NZ, dtype=jnp.int32))
    return jnp.moveaxis(planes, 0, 2)


def reference(density, velocity, pressure, offsets):
    dtheta = 2.0 * math.pi / NT
    radius = NT / (2.0 * math.pi) + jnp.arange(CR, dtype=jnp.float32) + 0.5
    state0 = conserved(density, velocity, pressure)
    state1 = state0 + TIME_STEP * full_rate(state0, offsets[0], radius, dtheta)
    state2 = 0.75 * state0 + 0.25 * (state1 + TIME_STEP * full_rate(state1, offsets[1], radius, dtheta))
    return state0 / 3.0 + (2.0 / 3.0) * (state2 + TIME_STEP * full_rate(state2, offsets[2], radius, dtheta))
```

```python
import functools
import math

import jax
import jax.numpy as jnp
from jax import lax
from jax.experimental import pallas as pl
from jax.experimental.pallas import tpu as pltpu
from jax.sharding import PartitionSpec as P

HEAT_RATIO = 1.4
VISCOSITY = 0.8
CONDUCTION = 0.6
TIME_STEP = 0.1
AXIAL_FLUX = 1.0
AXIAL_CURVE = 4.0


def partner_2(value, axis, bit):
    mask = 2**bit
    pairs = [(source, source ^ mask) for source in range(lax.axis_size(axis))]
    return lax.ppermute(value, axis, pairs)


def padded(cells, sides, width, closed):
    for axis, dim in sides:
        count = lax.axis_size(axis)
        ends = count if closed else count - 1
        head = lax.slice_in_dim(cells, 0, width, axis=dim)
        tail = lax.slice_in_dim(cells, cells.shape[dim] - width, cells.shape[dim], axis=dim)
        cells = jnp.concatenate(
            [
                lax.ppermute(tail, axis, [(i, (i + 1) % count) for i in range(ends)]),
                cells,
                lax.ppermute(head, axis, [((i + 1) % count, i) for i in range(ends)]),
            ],
            axis=dim,
        )
    return cells


def conserved(density, velocity, pressure):
    momentum = density[:, None] * velocity
    energy = pressure / (HEAT_RATIO - 1.0) + 0.5 * density * jnp.sum(velocity * velocity, axis=1)
    return jnp.concatenate([density[:, None], momentum, energy[:, None]], axis=1)


def primitive(state):
    vel_theta = state[:, 1] / state[:, 0]
    vel_radial = state[:, 2] / state[:, 0]
    vel_axial = state[:, 3] / state[:, 0]
    press = (HEAT_RATIO - 1.0) * (
        state[:, 4]
        - 0.5 * (state[:, 1] * vel_theta + state[:, 2] * vel_radial + state[:, 3] * vel_axial)
    )
    return (vel_theta, vel_radial, vel_axial, press / state[:, 0], press)


def fluxes(state, values, direction):
    normal_vel = values[direction]
    press = values[4]
    flux_terms = [
        state[:, 0] * normal_vel,
        state[:, 1] * normal_vel,
        state[:, 2] * normal_vel,
        state[:, 3] * normal_vel,
        (state[:, 4] + press) * normal_vel,
    ]
    flux_terms[1 + direction] = flux_terms[1 + direction] + press
    return flux_terms


def extended(state, values_c, lower, upper, axis_pos):
    values_lo = primitive(lower)
    values_hi = primitive(upper)
    ext_state = jnp.concatenate([lower, state, upper], axis=axis_pos)
    ext_values = tuple(
        (
            jnp.concatenate([values_lo[k], values_c[k], values_hi[k]], axis=axis_pos - 1)
            for k in range(5)
        )
    )
    return (ext_state, ext_values)


def side_slices(items, axis_pos):
    size_now = items[0].shape[axis_pos] - 2
    lows = [lax.slice_in_dim(item, 0, size_now, axis=axis_pos) for item in items]
    highs = [lax.slice_in_dim(item, 2, size_now + 2, axis=axis_pos) for item in items]
    return (lows, highs)


def tendency(state, theta_ghosts, radial_ghosts, axial_ghosts, radius, dtheta):
    values_c = primitive(state)
    directions = [(theta_ghosts, 3), (radial_ghosts, 4), (axial_ghosts, 2)]
    flux_lo = []
    flux_hi = []
    value_lo = []
    value_hi = []
    for direction_index in range(3):
        ghosts, axis_pos = directions[direction_index]
        ext_state, ext_values = extended(state, values_c, ghosts[0], ghosts[1], axis_pos)
        flux_all = fluxes(ext_state, ext_values, direction_index)
        lows, highs = side_slices(flux_all, axis_pos - 1)
        flux_lo.append(lows)
        flux_hi.append(highs)
        vlows, vhighs = side_slices(list(ext_values), axis_pos - 1)
        value_lo.append(vlows)
        value_hi.append(vhighs)
    result = []
    for field_index in range(5):
        divergence = -(flux_hi[0][field_index] - flux_lo[0][field_index]) / (2.0 * radius * dtheta)
        divergence = divergence - (
            (radius + 1.0) * flux_hi[1][field_index] - (radius - 1.0) * flux_lo[1][field_index]
        ) / (2.0 * radius)
        divergence = divergence - AXIAL_FLUX * (flux_hi[2][field_index] - flux_lo[2][field_index])
        result.append(divergence)

    def viscous(which):
        center = values_c[which]
        beside_all = (value_hi[0][which] - 2.0 * center + value_lo[0][which]) / (
            radius * dtheta
        ) ** 2
        across = (
            (radius + 0.5) * (value_hi[1][which] - center)
            - (radius - 0.5) * (center - value_lo[1][which])
        ) / radius
        return (
            beside_all
            + across
            + AXIAL_CURVE * (value_hi[2][which] - 2.0 * center + value_lo[2][which])
        )

    density_now = state[:, 0]
    result[1] = (
        result[1]
        - density_now * values_c[0] * values_c[1] / radius
        + VISCOSITY
        * (
            viscous(0)
            - values_c[0] / radius**2
            + (value_hi[0][1] - value_lo[0][1]) / (radius**2 * dtheta)
        )
    )
    result[2] = (
        result[2]
        + (density_now * values_c[0] * values_c[0] + values_c[4]) / radius
        + VISCOSITY
        * (
            viscous(1)
            - values_c[1] / radius**2
            - (value_hi[0][0] - value_lo[0][0]) / (radius**2 * dtheta)
        )
    )
    result[3] = result[3] + VISCOSITY * viscous(2)
    result[4] = result[4] + CONDUCTION * viscous(3)
    return jnp.stack(result, axis=1)


def body(density, velocity, pressure, offsets):
    state0 = conserved(density, velocity, pressure)
    tile_cells = state0.shape[3]
    radial_cells = state0.shape[4]
    cycle_size = lax.axis_size("az")
    cycle_cells = tile_cells * cycle_size
    dtheta = 2.0 * math.pi / cycle_cells
    radius = cycle_cells / (2.0 * math.pi) + jnp.arange(radial_cells, dtype=jnp.float32) + 0.5
    at_outer = lax.axis_index("ax") == 0
    at_plane = lax.axis_index("ax") == lax.axis_size("ax") - 1
    is_rotor = lax.axis_index("row") == 0
    axial_sign = jnp.array([1.0, 1.0, 1.0, -1.0, 1.0], dtype=jnp.float32).reshape(5, 1, 1)
    wall_sign = jnp.array([1.0, -1.0, -1.0, -1.0, 1.0], dtype=jnp.float32).reshape(5, 1, 1, 1)

    def rotate_plane(partner, turn_cells):
        band = lax.all_to_all(partner, "az", split_axis=2, concat_axis=1, tiled=True)
        doubled = jnp.concatenate([band, band], axis=1)
        rolled = lax.dynamic_slice_in_dim(doubled, turn_cells, cycle_cells, 1)
        return lax.all_to_all(rolled, "az", split_axis=1, concat_axis=2, tiled=True)

    def full_rate(state, shift):
        top_plane = state[0, :, -1] * axial_sign
        partner = partner_2(top_plane, "row", 0)
        turn_cells = jnp.where(is_rotor, shift, (cycle_cells - shift) % cycle_cells)
        ghost_plane = rotate_plane(partner, turn_cells)
        cycle_pad = padded(state, (("az", 3),), 1, True)
        theta_lo = cycle_pad[:, :, :, :1]
        theta_hi = cycle_pad[:, :, :, -1:]
        plane_pad = padded(state, (("ax", 2),), 1, False)
        lower_ghost = plane_pad[:, :, :1]
        upper_ghost = plane_pad[:, :, -1:]
        lower_ghost = jnp.where(at_outer, state[:, :, :1], lower_ghost)
        upper_ghost = jnp.where(at_plane, ghost_plane[None, :, None], upper_ghost)
        radial_lo = state[..., :1] * wall_sign
        radial_hi = state[..., -1:] * wall_sign
        return tendency(
            state,
            (theta_lo, theta_hi),
            (radial_lo, radial_hi),
            (lower_ghost, upper_ghost),
            radius,
            dtheta,
        )

    state1 = state0 + TIME_STEP * full_rate(state0, offsets[0])
    state2 = 0.75 * state0 + 0.25 * (state1 + TIME_STEP * full_rate(state1, offsets[1]))
    return state0 / 3.0 + 2.0 / 3.0 * (state2 + TIME_STEP * full_rate(state2, offsets[2]))


LANES = 128
TILE = 8
PEER = pl.DeviceIdType.MESH
RUNGE_KUTTA = ((0.0, 1.0), (0.75, 0.25), (1.0 / 3.0, 2.0 / 3.0))


def band_of(ax, az, wide):
    deep, side = az // 2, az % 2
    column = side + ax * (3 - 2 * side)
    return column * wide + deep + (column % 2) * (wide - 1 - 2 * deep)


def chip_of(band, wide):
    column, step = band // wide, band % wide
    ax = column // 2
    side = (column + ax) % 2
    deep = step + (column % 2) * (wide - 1 - 2 * step)
    return ax, deep * 2 + side


def kernel(
    az_count, planes, width,
    off_ref, den_ref, vel_ref, pre_ref, out_ref,
    send1, recv1, send2, recv2, base, now, prim, halo_out, halo_in, halo, plane_out, plane_in, ghost,
    s1, r1, s2, r2, sh, rh, sp, rp,
):
    chips = 2 * az_count
    wide = az_count // 2
    turn_cells = 32 * az_count
    tiles = 4
    row = lax.axis_index("row")
    ax = lax.axis_index("ax")
    az = lax.axis_index("az")
    me = ax * az_count + az
    band = band_of(ax, az, wide)

    def chip_id(flat):
        return (row, flat // az_count, flat % az_count)

    def band_id(which):
        return (row,) + chip_of(which, wide)

    barrier = pltpu.get_barrier_semaphore()
    for i in range(1, chips):
        pl.semaphore_signal(barrier, inc=1, device_id=chip_id((me + i) % chips), device_id_type=PEER)
    pl.semaphore_signal(barrier, inc=1, device_id=(1 - row, ax, az), device_id_type=PEER)

    lane = lax.broadcasted_iota(jnp.int32, (TILE, LANES), 1)
    part = lane // 32
    inner = lane % 32

    for f in range(5):
        for i in range(2):
            for col in range(4):
                source = []
                for h in range(2):
                    for k in range(2):
                        rows = pl.ds(16 * h + 8 * i, 8)
                        cols = pl.ds(128 * col, 128)
                        if f == 0:
                            tile = den_ref[0, k, rows, cols]
                        elif f == 4:
                            tile = pre_ref[0, k, rows, cols] / den_ref[0, k, rows, cols]
                        else:
                            tile = vel_ref[0, f - 1, k, rows, cols]
                        source.append(tile)
                for sub in range(4):
                    mixed = None
                    for q in range(4):
                        turn = (32 * (q - sub)) % 128
                        moved = pltpu.roll(source[q], turn, axis=1) if turn else source[q]
                        mixed = moved if mixed is None else jnp.where(part == q, moved, mixed)
                    send1[4 * col + sub, f, 8 * i:8 * i + 8, :] = mixed

    pl.semaphore_wait(barrier, chips)

    def first_copy(i):
        flat = (me + i) % chips
        to_ax, to_az = flat // az_count, flat % az_count
        return pltpu.make_async_remote_copy(
            src_ref=send1.at[band_of(to_ax, to_az, wide)],
            dst_ref=recv1.at[me],
            send_sem=s1.at[i],
            recv_sem=r1.at[i],
            device_id=(row, to_ax, to_az),
            device_id_type=PEER,
        )

    for i in range(1, chips):
        first_copy(i).start()
    recv1[me] = send1[band]

    dtheta = 2.0 * math.pi / turn_cells
    radius = turn_cells / (2.0 * math.pi) + (band * 32 + inner).astype(jnp.float32) + 0.5
    inverse = 1.0 / radius
    c_turn = inverse * (0.5 / dtheta)
    c_out = 0.5 * (radius + 1.0) * inverse
    c_in = 0.5 * (radius - 1.0) * inverse
    l_turn = (inverse * (1.0 / dtheta)) * (inverse * (1.0 / dtheta))
    l_out = (radius + 0.5) * inverse
    l_in = (radius - 0.5) * inverse
    l_mid = 2.0 * l_turn + (2.0 + 2.0 * AXIAL_CURVE)
    inverse2 = inverse * inverse
    c_cross = inverse2 * (VISCOSITY / dtheta)

    def pack(w, tile_index, row0, group, slot, packed):
        low, high = packed
        low = [jnp.where(inner == tile_index, pltpu.roll(w[f], tile_index + 97, axis=1), low[f]) for f in range(5)]
        high = [jnp.where(inner == tile_index, pltpu.roll(w[f], tile_index, axis=1), high[f]) for f in range(5)]
        for f in range(5):
            moved = pltpu.roll(w[f], (32 * group + 32) % 128, axis=1)
            rows = pl.ds(pl.multiple_of(row0, 8), 8)
            plane_out[slot, f, rows, :] = jnp.where(part == group, moved, plane_out[slot, f, rows, :])
        return low, high

    def close(slot, which, packed):
        low, high = packed
        for f in range(5):
            halo_out[slot, 0, f] = low[f]
            halo_out[slot, 1, f] = high[f]
            prim[which, f, 0:8, :] = prim[which, f, turn_cells:turn_cells + 8, :]
            prim[which, f, turn_cells + 8:turn_cells + 16, :] = prim[which, f, 8:16, :]

    def neighbour_copies(slot):
        copies = []
        for side, to in ((0, (band + 1) % chips), (1, (band + chips - 1) % chips)):
            copies.append(pltpu.make_async_remote_copy(
                src_ref=halo_out.at[slot, side],
                dst_ref=halo_in.at[slot, side],
                send_sem=sh.at[slot, side],
                recv_sem=rh.at[slot, side],
                device_id=band_id(to),
                device_id_type=PEER,
            ))
        copies.append(pltpu.make_async_remote_copy(
            src_ref=plane_out.at[slot],
            dst_ref=plane_in.at[slot],
            send_sem=sp.at[slot],
            recv_sem=rp.at[slot],
            device_id=(1 - row, ax, az),
            device_id_type=PEER,
        ))
        return copies

    quarter = az_count // 4
    empty = ([jnp.zeros((TILE, LANES), jnp.float32)] * 5, [jnp.zeros((TILE, LANES), jnp.float32)] * 5)

    for i in range(1, chips):
        first_copy(i).wait()

    def unpack(a, packed):
        for t in range(tiles):
            h, i = t // 2, t % 2
            w = []
            for f in range(5):
                c0 = recv1[a, f, 8 * i:8 * i + 8, :]
                c1 = recv1[az_count + a, f, 8 * i:8 * i + 8, :]
                if h == 0:
                    w.append(jnp.where(part < 2, c0, pltpu.roll(c1, 64, axis=1)))
                else:
                    w.append(jnp.where(part < 2, pltpu.roll(c0, 64, axis=1), c1))
            rho, vt, vr, vz, temp = w
            rows = pl.ds(pl.multiple_of(a * 32 + t * 8, 8), 8)
            rows_pad = pl.ds(pl.multiple_of(a * 32 + t * 8 + 8, 8), 8)
            state = (rho, rho * vt, rho * vr, rho * vz,
                     rho * (temp / (HEAT_RATIO - 1.0) + 0.5 * (vt * vt + vr * vr + vz * vz)))
            for f in range(5):
                base[f, rows, :] = state[f]
                now[f, rows, :] = state[f]
                prim[0, f, rows_pad, :] = w[f]
            packed = pack(w, a * 4 + t, (a % quarter) * 32 + t * 8, a // quarter, 0, packed)
        return packed

    close(0, 0, lax.fori_loop(0, az_count, unpack, empty))

    def second_copy(flat):
        return pltpu.make_async_remote_copy(
            src_ref=send2.at[flat],
            dst_ref=recv2.at[band],
            send_sem=s2.at[flat],
            recv_sem=r2.at[band],
            device_id=chip_id(flat),
            device_id_type=PEER,
        )

    signs = (1.0, -1.0, -1.0, -1.0, 1.0)
    for step in range(3):
        copies = neighbour_copies(step)
        for copy in copies:
            copy.start()
        for copy in copies:
            copy.wait()
        which = step % 2
        first_band = band == 0
        last_band = band == chips - 1
        for f in range(5):
            halo[0, f] = jnp.where(first_band, signs[f] * halo_out[step, 1, f], halo_in[step, 0, f])
            halo[1, f] = jnp.where(last_band, signs[f] * halo_out[step, 0, f], halo_in[step, 1, f])
        span = 32 * quarter
        for f in range(5):
            for g in range(4):
                moved = plane_in[step, f]
                if g != 3:
                    moved = pltpu.roll(moved, 96 - 32 * g, axis=1)
                if f == 3:
                    moved = -moved
                ghost[f, span * g:span * (g + 1), :] = moved
                ghost[f, turn_cells + span * g:turn_cells + span * (g + 1), :] = moved
        shift = off_ref[step]
        shift = jnp.where(row == 0, shift, turn_cells - shift)
        keep, fresh = RUNGE_KUTTA[step]

        def rate(j, packed, step=step, which=which, shift=shift, keep=keep, fresh=fresh):
            a = j if step < 2 else (az + j) % az_count
            result = []
            for t in range(tiles):
                tile_index = a * 4 + t
                row0 = a * 32 + t * 8
                mid, tl, th, rl, rr, zl, zh = [], [], [], [], [], [], []
                for f in range(5):
                    c = prim[which, f, pl.ds(pl.multiple_of(row0 + 8, 8), 8), :]
                    mid.append(c)
                    tl.append(prim[which, f, pl.ds(row0 + 7, 8), :])
                    th.append(prim[which, f, pl.ds(row0 + 9, 8), :])
                    rl.append(jnp.where(inner == 0, pltpu.roll(halo[0, f], 128 - tile_index, axis=1), pltpu.roll(c, 1, axis=1)))
                    rr.append(jnp.where(inner == 31, pltpu.roll(halo[1, f], 128 + 31 - tile_index, axis=1), pltpu.roll(c, 127, axis=1)))
                    zl.append(jnp.where(part == 0, c, pltpu.roll(c, 32, axis=1)))
                    zh.append(jnp.where(part == 3, ghost[f, pl.ds(row0 + shift, 8), :], pltpu.roll(c, 96, axis=1)))

                def flux(w, d):
                    rho, vt, vr, vz, temp = w
                    m = rho * w[1 + d]
                    terms = [m, m * vt, m * vr, m * vz,
                             m * (3.5 * temp + 0.5 * (vt * vt + vr * vr + vz * vz))]
                    terms[1 + d] = terms[1 + d] + rho * temp
                    return terms

                ftl, fth = flux(tl, 0), flux(th, 0)
                frl, frh = flux(rl, 1), flux(rr, 1)
                fzl, fzh = flux(zl, 2), flux(zh, 2)
                total = [
                    c_turn * (ftl[f] - fth[f]) + (c_in * frl[f] - c_out * frh[f]) + (fzl[f] - fzh[f])
                    for f in range(5)
                ]

                def lap(n):
                    return (l_turn * (th[n] + tl[n]) + (l_out * rr[n] + l_in * rl[n])
                            + AXIAL_CURVE * (zh[n] + zl[n]) - l_mid * mid[n])

                rho, vt, vr, vz, temp = mid
                total[1] = (total[1] - rho * vt * vr * inverse
                            + VISCOSITY * (lap(1) - vt * inverse2) + c_cross * (th[2] - tl[2]))
                total[2] = (total[2] + rho * (vt * vt + temp) * inverse
                            + VISCOSITY * (lap(2) - vr * inverse2) - c_cross * (th[1] - tl[1]))
                total[3] = total[3] + VISCOSITY * lap(3)
                total[4] = total[4] + CONDUCTION * lap(4)
                rows = pl.ds(pl.multiple_of(row0, 8), 8)
                state = []
                for f in range(5):
                    value = fresh * (now[f, rows, :] + TIME_STEP * total[f])
                    if keep:
                        value = value + keep * base[f, rows, :]
                    state.append(value)
                if step < 2:
                    inv = 1.0 / state[0]
                    vt, vr, vz = state[1] * inv, state[2] * inv, state[3] * inv
                    press = (HEAT_RATIO - 1.0) * (
                        state[4] - 0.5 * (state[1] * vt + state[2] * vr + state[3] * vz))
                    w = [state[0], vt, vr, vz, press * inv]
                    rows_pad = pl.ds(pl.multiple_of(row0 + 8, 8), 8)
                    for f in range(5):
                        now[f, rows, :] = state[f]
                        prim[1 - which, f, rows_pad, :] = w[f]
                    packed = pack(w, tile_index, (a % quarter) * 32 + t * 8, a // quarter, step + 1, packed)
                else:
                    result.append(state)
            if step == 2:
                for f in range(5):
                    for i in range(2):
                        upper, lower = result[i][f], result[2 + i][f]
                        send2[a, f, 8 * i:8 * i + 8, :] = jnp.where(part < 2, upper, pltpu.roll(lower, 64, axis=1))
                        send2[az_count + a, f, 8 * i:8 * i + 8, :] = jnp.where(
                            part < 2, pltpu.roll(upper, 64, axis=1), lower)
                for x in range(2):
                    flat = x * az_count + a

                    @pl.when(flat != me)
                    def _():
                        second_copy(flat).start()

                    @pl.when(flat == me)
                    def _():
                        recv2[band] = send2[me]
            return packed

        if step < 2:
            close(step + 1, 1 - which, lax.fori_loop(0, az_count, rate, empty))
        else:
            lax.fori_loop(0, az_count, rate, 0)

    def finish(i, carry):
        flat = (me + i) % chips
        from_band = band_of(flat // az_count, flat % az_count, wide)
        second_copy(flat).wait_send()
        pltpu.make_async_remote_copy(
            src_ref=send2.at[flat],
            dst_ref=recv2.at[from_band],
            send_sem=s2.at[flat],
            recv_sem=r2.at[from_band],
            device_id=chip_id(flat),
            device_id_type=PEER,
        ).wait_recv()
        return carry

    lax.fori_loop(1, chips, finish, 0)

    for f in range(5):
        for i in range(2):
            for col in range(4):
                source = [recv2[4 * col + sub, f, 8 * i:8 * i + 8, :] for sub in range(4)]
                for q in range(4):
                    h, k = q // 2, q % 2
                    mixed = None
                    for sub in range(4):
                        turn = (32 * (sub - q)) % 128
                        moved = pltpu.roll(source[sub], turn, axis=1) if turn else source[sub]
                        mixed = moved if mixed is None else jnp.where(part == sub, moved, mixed)
                    out_ref[0, f, k, 16 * h + 8 * i:16 * h + 8 * i + 8, 128 * col:128 * col + 128] = mixed


def banded(az_count, density, velocity, pressure, offsets):
    chips = 2 * az_count
    cells = 32 * az_count
    planes, width = 4, 32
    f32 = jnp.float32
    dma = pltpu.SemaphoreType.DMA
    vmem = pl.BlockSpec(memory_space=pltpu.VMEM)
    return pl.pallas_call(
        functools.partial(kernel, az_count, planes, width),
        out_shape=jax.ShapeDtypeStruct((1, 5) + density.shape[1:], f32),
        in_specs=[pl.BlockSpec(memory_space=pltpu.SMEM), vmem, vmem, vmem],
        out_specs=vmem,
        scratch_shapes=[
            pltpu.VMEM((chips, 5, 16, LANES), f32),
            pltpu.VMEM((chips, 5, 16, LANES), f32),
            pltpu.VMEM((chips, 5, 16, LANES), f32),
            pltpu.VMEM((chips, 5, 16, LANES), f32),
            pltpu.VMEM((5, cells, LANES), f32),
            pltpu.VMEM((5, cells, LANES), f32),
            pltpu.VMEM((2, 5, cells + 16, LANES), f32),
            pltpu.VMEM((3, 2, 5, TILE, LANES), f32),
            pltpu.VMEM((3, 2, 5, TILE, LANES), f32),
            pltpu.VMEM((2, 5, TILE, LANES), f32),
            pltpu.VMEM((3, 5, cells // 4, LANES), f32),
            pltpu.VMEM((3, 5, cells // 4, LANES), f32),
            pltpu.VMEM((5, 2 * cells + 8, LANES), f32),
            dma((chips,)), dma((chips,)), dma((chips,)), dma((chips,)),
            dma((3, 2)), dma((3, 2)), dma((3,)), dma((3,)),
        ],
        compiler_params=pltpu.CompilerParams(
            collective_id=0, has_side_effects=True, vmem_limit_bytes=40 * 2**20
        ),
    )(offsets, density, velocity, pressure)


def whole_step(density, velocity, pressure, offsets):
    ax_count, az_count = lax.axis_size("ax"), lax.axis_size("az")
    if ax_count == 2 and az_count == 8 and density.shape == (1, 2, 32, 512):
        return banded(az_count, density, velocity, pressure, offsets)
    return body(density, velocity, pressure, offsets)


def solution(mesh):
    placed = (
        P("row", "ax", "az", None),
        P("row", None, "ax", "az", None),
        P("row", "ax", "az", None),
        P(),
    )
    return jax.shard_map(
        whole_step,
        mesh=mesh,
        in_specs=placed,
        out_specs=P("row", None, "ax", "az", None),
        check_vma=False,
    )
```

```python
import functools
import math

import jax
import jax.numpy as jnp
from jax import lax
from jax.experimental import pallas as pl
from jax.experimental.pallas import tpu as pltpu
from jax.sharding import PartitionSpec as P

HEAT_RATIO = 1.4
VISCOSITY = 0.8
CONDUCTION = 0.6
TIME_STEP = 0.1
AXIAL_FLUX = 1.0
AXIAL_CURVE = 4.0


def partner_2(value, axis, bit):
    mask = 2**bit
    pairs = [(source, source ^ mask) for source in range(lax.axis_size(axis))]
    return lax.ppermute(value, axis, pairs)


def padded(cells, sides, width, closed):
    for axis, dim in sides:
        count = lax.axis_size(axis)
        ends = count if closed else count - 1
        head = lax.slice_in_dim(cells, 0, width, axis=dim)
        tail = lax.slice_in_dim(cells, cells.shape[dim] - width, cells.shape[dim], axis=dim)
        cells = jnp.concatenate(
            [
                lax.ppermute(tail, axis, [(i, (i + 1) % count) for i in range(ends)]),
                cells,
                lax.ppermute(head, axis, [((i + 1) % count, i) for i in range(ends)]),
            ],
            axis=dim,
        )
    return cells


def conserved(density, velocity, pressure):
    momentum = density[:, None] * velocity
    energy = pressure / (HEAT_RATIO - 1.0) + 0.5 * density * jnp.sum(velocity * velocity, axis=1)
    return jnp.concatenate([density[:, None], momentum, energy[:, None]], axis=1)


def primitive(state):
    vel_theta = state[:, 1] / state[:, 0]
    vel_radial = state[:, 2] / state[:, 0]
    vel_axial = state[:, 3] / state[:, 0]
    press = (HEAT_RATIO - 1.0) * (
        state[:, 4]
        - 0.5 * (state[:, 1] * vel_theta + state[:, 2] * vel_radial + state[:, 3] * vel_axial)
    )
    return (vel_theta, vel_radial, vel_axial, press / state[:, 0], press)


def fluxes(state, values, direction):
    normal_vel = values[direction]
    press = values[4]
    flux_terms = [
        state[:, 0] * normal_vel,
        state[:, 1] * normal_vel,
        state[:, 2] * normal_vel,
        state[:, 3] * normal_vel,
        (state[:, 4] + press) * normal_vel,
    ]
    flux_terms[1 + direction] = flux_terms[1 + direction] + press
    return flux_terms


def extended(state, values_c, lower, upper, axis_pos):
    values_lo = primitive(lower)
    values_hi = primitive(upper)
    ext_state = jnp.concatenate([lower, state, upper], axis=axis_pos)
    ext_values = tuple(
        (
            jnp.concatenate([values_lo[k], values_c[k], values_hi[k]], axis=axis_pos - 1)
            for k in range(5)
        )
    )
    return (ext_state, ext_values)


def side_slices(items, axis_pos):
    size_now = items[0].shape[axis_pos] - 2
    lows = [lax.slice_in_dim(item, 0, size_now, axis=axis_pos) for item in items]
    highs = [lax.slice_in_dim(item, 2, size_now + 2, axis=axis_pos) for item in items]
    return (lows, highs)


def tendency(state, theta_ghosts, radial_ghosts, axial_ghosts, radius, dtheta):
    values_c = primitive(state)
    directions = [(theta_ghosts, 3), (radial_ghosts, 4), (axial_ghosts, 2)]
    flux_lo = []
    flux_hi = []
    value_lo = []
    value_hi = []
    for direction_index in range(3):
        ghosts, axis_pos = directions[direction_index]
        ext_state, ext_values = extended(state, values_c, ghosts[0], ghosts[1], axis_pos)
        flux_all = fluxes(ext_state, ext_values, direction_index)
        lows, highs = side_slices(flux_all, axis_pos - 1)
        flux_lo.append(lows)
        flux_hi.append(highs)
        vlows, vhighs = side_slices(list(ext_values), axis_pos - 1)
        value_lo.append(vlows)
        value_hi.append(vhighs)
    result = []
    for field_index in range(5):
        divergence = -(flux_hi[0][field_index] - flux_lo[0][field_index]) / (2.0 * radius * dtheta)
        divergence = divergence - (
            (radius + 1.0) * flux_hi[1][field_index] - (radius - 1.0) * flux_lo[1][field_index]
        ) / (2.0 * radius)
        divergence = divergence - AXIAL_FLUX * (flux_hi[2][field_index] - flux_lo[2][field_index])
        result.append(divergence)

    def viscous(which):
        center = values_c[which]
        beside_all = (value_hi[0][which] - 2.0 * center + value_lo[0][which]) / (
            radius * dtheta
        ) ** 2
        across = (
            (radius + 0.5) * (value_hi[1][which] - center)
            - (radius - 0.5) * (center - value_lo[1][which])
        ) / radius
        return (
            beside_all
            + across
            + AXIAL_CURVE * (value_hi[2][which] - 2.0 * center + value_lo[2][which])
        )

    density_now = state[:, 0]
    result[1] = (
        result[1]
        - density_now * values_c[0] * values_c[1] / radius
        + VISCOSITY
        * (
            viscous(0)
            - values_c[0] / radius**2
            + (value_hi[0][1] - value_lo[0][1]) / (radius**2 * dtheta)
        )
    )
    result[2] = (
        result[2]
        + (density_now * values_c[0] * values_c[0] + values_c[4]) / radius
        + VISCOSITY
        * (
            viscous(1)
            - values_c[1] / radius**2
            - (value_hi[0][0] - value_lo[0][0]) / (radius**2 * dtheta)
        )
    )
    result[3] = result[3] + VISCOSITY * viscous(2)
    result[4] = result[4] + CONDUCTION * viscous(3)
    return jnp.stack(result, axis=1)


def body(density, velocity, pressure, offsets):
    state0 = conserved(density, velocity, pressure)
    tile_cells = state0.shape[3]
    radial_cells = state0.shape[4]
    cycle_size = lax.axis_size("az")
    cycle_cells = tile_cells * cycle_size
    dtheta = 2.0 * math.pi / cycle_cells
    radius = cycle_cells / (2.0 * math.pi) + jnp.arange(radial_cells, dtype=jnp.float32) + 0.5
    at_outer = lax.axis_index("ax") == 0
    at_plane = lax.axis_index("ax") == lax.axis_size("ax") - 1
    is_rotor = lax.axis_index("row") == 0
    axial_sign = jnp.array([1.0, 1.0, 1.0, -1.0, 1.0], dtype=jnp.float32).reshape(5, 1, 1)
    wall_sign = jnp.array([1.0, -1.0, -1.0, -1.0, 1.0], dtype=jnp.float32).reshape(5, 1, 1, 1)

    def rotate_plane(partner, turn_cells):
        band = lax.all_to_all(partner, "az", split_axis=2, concat_axis=1, tiled=True)
        doubled = jnp.concatenate([band, band], axis=1)
        rolled = lax.dynamic_slice_in_dim(doubled, turn_cells, cycle_cells, 1)
        return lax.all_to_all(rolled, "az", split_axis=1, concat_axis=2, tiled=True)

    def full_rate(state, shift):
        top_plane = state[0, :, -1] * axial_sign
        partner = partner_2(top_plane, "row", 0)
        turn_cells = jnp.where(is_rotor, shift, (cycle_cells - shift) % cycle_cells)
        ghost_plane = rotate_plane(partner, turn_cells)
        cycle_pad = padded(state, (("az", 3),), 1, True)
        theta_lo = cycle_pad[:, :, :, :1]
        theta_hi = cycle_pad[:, :, :, -1:]
        plane_pad = padded(state, (("ax", 2),), 1, False)
        lower_ghost = plane_pad[:, :, :1]
        upper_ghost = plane_pad[:, :, -1:]
        lower_ghost = jnp.where(at_outer, state[:, :, :1], lower_ghost)
        upper_ghost = jnp.where(at_plane, ghost_plane[None, :, None], upper_ghost)
        radial_lo = state[..., :1] * wall_sign
        radial_hi = state[..., -1:] * wall_sign
        return tendency(
            state,
            (theta_lo, theta_hi),
            (radial_lo, radial_hi),
            (lower_ghost, upper_ghost),
            radius,
            dtheta,
        )

    state1 = state0 + TIME_STEP * full_rate(state0, offsets[0])
    state2 = 0.75 * state0 + 0.25 * (state1 + TIME_STEP * full_rate(state1, offsets[1]))
    return state0 / 3.0 + 2.0 / 3.0 * (state2 + TIME_STEP * full_rate(state2, offsets[2]))


LANES = 128
TILE = 8
PEER = pl.DeviceIdType.MESH
RUNGE_KUTTA = ((0.0, 1.0), (0.75, 0.25), (1.0 / 3.0, 2.0 / 3.0))


def band_of(ax, az, wide):
    deep, side = az // 2, az % 2
    column = side + ax * (3 - 2 * side)
    return column * wide + deep + (column % 2) * (wide - 1 - 2 * deep)


def chip_of(band, wide):
    column, step = band // wide, band % wide
    ax = column // 2
    side = (column + ax) % 2
    deep = step + (column % 2) * (wide - 1 - 2 * step)
    return ax, deep * 2 + side


def kernel(
    az_count,
    off_hbm, den_hbm, vel_hbm, pre_hbm, out_hbm,
    off_ref, den_ref, vel_ref, pre_ref, out_ref,
    send1, recv1, send2, recv2, base, now, prim, halo_out, halo_in, halo, plane_out, plane_in, ghost,
    s1, r1, s2, r2, sh, rh, sp, rp, s_in, s_out,
):
    chips = 2 * az_count
    wide = az_count // 2
    turn_cells = 32 * az_count
    tiles = 4
    row = lax.axis_index("row")
    ax = lax.axis_index("ax")
    az = lax.axis_index("az")
    me = ax * az_count + az
    band = band_of(ax, az, wide)

    def chip_id(flat):
        return (row, flat // az_count, flat % az_count)

    def band_id(which):
        return (row,) + chip_of(which, wide)

    loads = [
        pltpu.make_async_copy(src, dst, s_in.at[n])
        for n, (src, dst) in enumerate((
            (den_hbm, den_ref), (pre_hbm, pre_ref), (vel_hbm, vel_ref), (off_hbm, off_ref)))
    ]
    for load in loads:
        load.start()
    barrier = pltpu.get_barrier_semaphore()
    for i in range(1, chips):
        pl.semaphore_signal(barrier, inc=1, device_id=chip_id((me + i) % chips), device_id_type=PEER)
    pl.semaphore_signal(barrier, inc=1, device_id=(1 - row, ax, az), device_id_type=PEER)

    lane = lax.broadcasted_iota(jnp.int32, (TILE, LANES), 1)
    part = lane // 32
    inner = lane % 32

    for load in loads:
        load.wait()

    for f in range(5):
        for i in range(2):
            for col in range(4):
                source = []
                for h in range(2):
                    for k in range(2):
                        rows = pl.ds(16 * h + 8 * i, 8)
                        cols = pl.ds(128 * col, 128)
                        if f == 0:
                            tile = den_ref[0, k, rows, cols]
                        elif f == 4:
                            tile = pre_ref[0, k, rows, cols] / den_ref[0, k, rows, cols]
                        else:
                            tile = vel_ref[0, f - 1, k, rows, cols]
                        source.append(tile)
                for sub in range(4):
                    mixed = None
                    for q in range(4):
                        turn = (32 * (q - sub)) % 128
                        moved = pltpu.roll(source[q], turn, axis=1) if turn else source[q]
                        mixed = moved if mixed is None else jnp.where(part == q, moved, mixed)
                    send1[4 * col + sub, f, 8 * i:8 * i + 8, :] = mixed

    pl.semaphore_wait(barrier, chips)

    def first_copy(flat):
        return pltpu.make_async_remote_copy(
            src_ref=send1.at[band_of(flat // az_count, flat % az_count, wide)],
            dst_ref=recv1.at[me],
            send_sem=s1.at[flat],
            recv_sem=r1.at[me],
            device_id=chip_id(flat),
            device_id_type=PEER,
        )

    def others():
        for j in range(az_count):
            for x in range(2):
                if j or x:
                    yield ((ax + x) % 2) * az_count + (az + az_count - j) % az_count

    for flat in others():
        first_copy(flat).start()
    recv1[me] = send1[band]

    dtheta = 2.0 * math.pi / turn_cells
    radius = turn_cells / (2.0 * math.pi) + (band * 32 + inner).astype(jnp.float32) + 0.5
    inverse = 1.0 / radius
    c_turn = inverse * (0.5 / dtheta)
    c_out = 0.5 * (radius + 1.0) * inverse
    c_in = 0.5 * (radius - 1.0) * inverse
    l_turn = (inverse * (1.0 / dtheta)) * (inverse * (1.0 / dtheta))
    l_out = (radius + 0.5) * inverse
    l_in = (radius - 0.5) * inverse
    l_mid = 2.0 * l_turn + (2.0 + 2.0 * AXIAL_CURVE)
    inverse2 = inverse * inverse
    c_cross = inverse2 * (VISCOSITY / dtheta)
    r_low = turn_cells / (2.0 * math.pi) + (lane * 0 + band * 32).astype(jnp.float32) + 0.5
    r_high = r_low + 31.0
    edge_c = (0.5 * (r_low - 1.0) / r_low, -0.5 * (r_high + 1.0) / r_high)
    edge_l = ((r_low - 0.5) / r_low, (r_high + 0.5) / r_high)
    zero = jnp.zeros((TILE, LANES), jnp.float32)
    c_in = jnp.where(inner == 0, zero, c_in)
    l_in = jnp.where(inner == 0, zero, l_in)
    c_out = jnp.where(inner == 31, zero, c_out)
    l_out = jnp.where(inner == 31, zero, l_out)

    def pack(tiles_of, a, slot):
        group = a // quarter
        for f in range(5):
            low, high = halo_out[slot, 0, f], halo_out[slot, 1, f]
            for t in range(tiles):
                w, tile_index = tiles_of[t][f], a * 4 + t
                low = jnp.where(inner == tile_index, pltpu.roll(w, tile_index + 97, axis=1), low)
                high = jnp.where(inner == tile_index, pltpu.roll(w, tile_index, axis=1), high)
                moved = pltpu.roll(w, (32 * group + 32) % 128, axis=1)
                rows = pl.ds(pl.multiple_of((a % quarter) * 32 + t * 8, 8), 8)
                plane_out[slot, f, rows, :] = jnp.where(part == group, moved, plane_out[slot, f, rows, :])
            halo_out[slot, 0, f], halo_out[slot, 1, f] = low, high

    def wrap(which, a, tiles_of):
        @pl.when(a == 0)
        def _():
            for f in range(5):
                prim[which, f, turn_cells + 8:turn_cells + 16, :] = tiles_of[0][f]

        @pl.when(a == az_count - 1)
        def _():
            for f in range(5):
                prim[which, f, 0:8, :] = tiles_of[tiles - 1][f]

    def neighbour_copies(slot):
        copies = []
        for side, to in ((0, (band + 1) % chips), (1, (band + chips - 1) % chips)):
            copies.append(pltpu.make_async_remote_copy(
                src_ref=halo_out.at[slot, side],
                dst_ref=halo_in.at[slot, side],
                send_sem=sh.at[slot, side],
                recv_sem=rh.at[slot, side],
                device_id=band_id(to),
                device_id_type=PEER,
            ))
        copies.append(pltpu.make_async_remote_copy(
            src_ref=plane_out.at[slot],
            dst_ref=plane_in.at[slot],
            send_sem=sp.at[slot],
            recv_sem=rp.at[slot],
            device_id=(1 - row, ax, az),
            device_id_type=PEER,
        ))
        return copies

    quarter = az_count // 4
    drag = (0.0, VISCOSITY, VISCOSITY, VISCOSITY, CONDUCTION)

    def flux(w, d):
        rho, vt, vr, vz, temp = w
        m = rho * w[1 + d]
        terms = [m, m * vt, m * vr, m * vz,
                 m * (3.5 * temp + 0.5 * (vt * vt + vr * vr + vz * vz))]
        terms[1 + d] = terms[1 + d] + rho * temp
        return terms

    def inside(a, step):
        which = step % 2
        keep, fresh = RUNGE_KUTTA[step]
        for t in range(tiles):
            row0 = a * 32 + t * 8
            mid, tl, th, rl, rr, zl, zh = [], [], [], [], [], [], []
            for f in range(5):
                c = prim[which, f, pl.ds(pl.multiple_of(row0 + 8, 8), 8), :]
                mid.append(c)
                tl.append(prim[which, f, pl.ds(row0 + 7, 8), :])
                th.append(prim[which, f, pl.ds(row0 + 9, 8), :])
                rl.append(pltpu.roll(c, 1, axis=1))
                rr.append(pltpu.roll(c, 127, axis=1))
                zl.append(jnp.where(part == 0, c, pltpu.roll(c, 32, axis=1)))
                zh.append(jnp.where(part == 3, zero, pltpu.roll(c, 96, axis=1)))
            ftl, fth = flux(tl, 0), flux(th, 0)
            frl, frh = flux(rl, 1), flux(rr, 1)
            fzl, fzh = flux(zl, 2), flux(zh, 2)
            total = [
                c_turn * (ftl[f] - fth[f]) + (c_in * frl[f] - c_out * frh[f]) + (fzl[f] - fzh[f])
                for f in range(5)
            ]

            def lap(n):
                return (l_turn * (th[n] + tl[n]) + (l_out * rr[n] + l_in * rl[n])
                        + AXIAL_CURVE * (zh[n] + zl[n]) - l_mid * mid[n])

            rho, vt, vr, vz, temp = mid
            total[1] = (total[1] - rho * vt * vr * inverse
                        + VISCOSITY * (lap(1) - vt * inverse2) + c_cross * (th[2] - tl[2]))
            total[2] = (total[2] + rho * (vt * vt + temp) * inverse
                        + VISCOSITY * (lap(2) - vr * inverse2) - c_cross * (th[1] - tl[1]))
            total[3] = total[3] + VISCOSITY * lap(3)
            total[4] = total[4] + CONDUCTION * lap(4)
            rows = pl.ds(pl.multiple_of(row0, 8), 8)
            for f in range(5):
                value = fresh * (now[f, rows, :] + TIME_STEP * total[f])
                if keep:
                    value = value + keep * base[f, rows, :]
                now[f, rows, :] = value

    def unpack(a):
        tiles_of = []
        for t in range(tiles):
            h, i = t // 2, t % 2
            w = []
            for f in range(5):
                c0 = recv1[a, f, 8 * i:8 * i + 8, :]
                c1 = recv1[az_count + a, f, 8 * i:8 * i + 8, :]
                if h == 0:
                    w.append(jnp.where(part < 2, c0, pltpu.roll(c1, 64, axis=1)))
                else:
                    w.append(jnp.where(part < 2, pltpu.roll(c0, 64, axis=1), c1))
            rho, vt, vr, vz, temp = w
            rows = pl.ds(pl.multiple_of(a * 32 + t * 8, 8), 8)
            rows_pad = pl.ds(pl.multiple_of(a * 32 + t * 8 + 8, 8), 8)
            state = (rho, rho * vt, rho * vr, rho * vz,
                     rho * (temp / (HEAT_RATIO - 1.0) + 0.5 * (vt * vt + vr * vr + vz * vz)))
            for f in range(5):
                base[f, rows, :] = state[f]
                now[f, rows, :] = state[f]
                prim[0, f, rows_pad, :] = w[f]
            tiles_of.append(w)
        wrap(0, a, tiles_of)
        pack(tiles_of, a, 0)

    def arrive(j, carry):
        a = (az + j) % az_count
        for x in range(2):
            flat = x * az_count + a

            @pl.when(flat != me)
            def _():
                pltpu.make_async_remote_copy(
                    src_ref=send1.at[flat],
                    dst_ref=recv1.at[flat],
                    send_sem=s1.at[flat],
                    recv_sem=r1.at[flat],
                    device_id=chip_id(flat),
                    device_id_type=PEER,
                ).wait_recv()

        unpack(a)

        @pl.when(j >= 2)
        def _():
            inside((a + az_count - 1) % az_count, 0)

        return carry

    lax.fori_loop(0, az_count, arrive, 0)

    def second_copy(flat):
        return pltpu.make_async_remote_copy(
            src_ref=send2.at[flat],
            dst_ref=recv2.at[band],
            send_sem=s2.at[flat],
            recv_sem=r2.at[band],
            device_id=chip_id(flat),
            device_id_type=PEER,
        )

    signs = (1.0, -1.0, -1.0, -1.0, 1.0)
    for step in range(3):
        copies = neighbour_copies(step)
        for copy in copies:
            copy.start()
        if step == 0:
            def rest(j, carry):
                inside((az + az_count - 1 + j) % az_count, 0)
                return carry

            lax.fori_loop(0, 2, rest, 0)
        else:
            def sweep(a, carry, step=step):
                inside(a, step)
                return carry

            lax.fori_loop(0, az_count, sweep, 0)
        for copy in copies:
            copy.wait()
        weight = TIME_STEP * RUNGE_KUTTA[step][1]
        walls = (band == 0, band == chips - 1)
        for side in range(2):
            w = [
                jnp.where(walls[side], signs[f] * halo_out[step, 1 - side, f], halo_in[step, side, f])
                for f in range(5)
            ]
            terms = flux(w, 1)
            for f in range(5):
                value = edge_c[side] * terms[f]
                if f:
                    value = value + drag[f] * edge_l[side] * w[f]
                halo[side, f] = weight * value

        def slide(n, carry, step=step, weight=weight):
            rows = pl.ds(pl.multiple_of(n * 8, 8), 8)
            w = [plane_in[step, f, rows, :] for f in range(5)]
            w[3] = -w[3]
            terms = flux(w, 2)
            for f in range(5):
                value = -terms[f]
                if f:
                    value = value + (AXIAL_CURVE * drag[f]) * w[f]
                value = weight * value
                for g in range(4):
                    moved = pltpu.roll(value, 96 - 32 * g, axis=1) if g != 3 else value
                    place = 32 * quarter * g + n * 8
                    ghost[f, pl.ds(pl.multiple_of(place, 8), 8), :] = moved
                    ghost[f, pl.ds(pl.multiple_of(turn_cells + place, 8), 8), :] = moved
            return carry

        lax.fori_loop(0, 4 * quarter, slide, 0)
        shift = off_ref[step]
        shift = jnp.where(row == 0, shift, turn_cells - shift)

        def edges(j, carry, step=step, shift=shift):
            which = step % 2
            a = j if step < 2 else (az + j) % az_count
            states, prims = [], []
            for t in range(tiles):
                tile_index = a * 4 + t
                row0 = a * 32 + t * 8
                rows = pl.ds(pl.multiple_of(row0, 8), 8)
                state = []
                for f in range(5):
                    low = pltpu.roll(halo[0, f], 128 - tile_index, axis=1)
                    high = pltpu.roll(halo[1, f], 128 + 31 - tile_index, axis=1)
                    extra = jnp.where(inner == 0, low, jnp.where(inner == 31, high, zero))
                    extra = extra + jnp.where(part == 3, ghost[f, pl.ds(row0 + shift, 8), :], zero)
                    state.append(now[f, rows, :] + extra)
                if step < 2:
                    inv = 1.0 / state[0]
                    vt, vr, vz = state[1] * inv, state[2] * inv, state[3] * inv
                    press = (HEAT_RATIO - 1.0) * (
                        state[4] - 0.5 * (state[1] * vt + state[2] * vr + state[3] * vz))
                    w = [state[0], vt, vr, vz, press * inv]
                    rows_pad = pl.ds(pl.multiple_of(row0 + 8, 8), 8)
                    for f in range(5):
                        now[f, rows, :] = state[f]
                        prim[1 - which, f, rows_pad, :] = w[f]
                    prims.append(w)
                else:
                    states.append(state)
            if step < 2:
                wrap(1 - which, a, prims)
                pack(prims, a, step + 1)
                return carry
            for f in range(5):
                for i in range(2):
                    upper, lower = states[i][f], states[2 + i][f]
                    send2[a, f, 8 * i:8 * i + 8, :] = jnp.where(part < 2, upper, pltpu.roll(lower, 64, axis=1))
                    send2[az_count + a, f, 8 * i:8 * i + 8, :] = jnp.where(
                        part < 2, pltpu.roll(upper, 64, axis=1), lower)
            for x in range(2):
                flat = x * az_count + a

                @pl.when(flat != me)
                def _():
                    second_copy(flat).start()

                @pl.when(flat == me)
                def _():
                    recv2[band] = send2[me]
            return carry

        lax.fori_loop(0, az_count, edges, 0)

    stores = []
    for col in range(4):
        for sub in range(4):
            from_band = 4 * col + sub
            from_ax, from_az = chip_of(from_band, wide)
            flat = from_ax * az_count + from_az

            @pl.when(flat != me)
            def _():
                pltpu.make_async_remote_copy(
                    src_ref=send2.at[flat],
                    dst_ref=recv2.at[from_band],
                    send_sem=s2.at[flat],
                    recv_sem=r2.at[from_band],
                    device_id=chip_id(flat),
                    device_id_type=PEER,
                ).wait_recv()

        for f in range(5):
            for i in range(2):
                source = [recv2[4 * col + sub, f, 8 * i:8 * i + 8, :] for sub in range(4)]
                for q in range(4):
                    h, k = q // 2, q % 2
                    mixed = None
                    for sub in range(4):
                        turn = (32 * (sub - q)) % 128
                        moved = pltpu.roll(source[sub], turn, axis=1) if turn else source[sub]
                        mixed = moved if mixed is None else jnp.where(part == sub, moved, mixed)
                    out_ref[col, f, k, 16 * h + 8 * i:16 * h + 8 * i + 8, :] = mixed
        store = pltpu.make_async_copy(
            out_ref.at[col], out_hbm.at[0, :, :, :, pl.ds(128 * col, 128)], s_out.at[col])
        store.start()
        stores.append(store)

    for flat in others():
        first_copy(flat).wait_send()
        second_copy(flat).wait_send()
    for store in stores:
        store.wait()


def banded(az_count, density, velocity, pressure, offsets):
    chips = 2 * az_count
    cells = 32 * az_count
    f32 = jnp.float32
    dma = pltpu.SemaphoreType.DMA
    anywhere = pl.BlockSpec(memory_space=pl.ANY)
    return pl.pallas_call(
        functools.partial(kernel, az_count),
        out_shape=jax.ShapeDtypeStruct((1, 5) + density.shape[1:], f32),
        in_specs=[anywhere] * 4,
        out_specs=anywhere,
        scratch_shapes=[
            pltpu.SMEM(offsets.shape, jnp.int32),
            pltpu.VMEM(density.shape, f32),
            pltpu.VMEM(velocity.shape, f32),
            pltpu.VMEM(pressure.shape, f32),
            pltpu.VMEM((4, 5, 2, 32, LANES), f32),
            pltpu.VMEM((chips, 5, 16, LANES), f32),
            pltpu.VMEM((chips, 5, 16, LANES), f32),
            pltpu.VMEM((chips, 5, 16, LANES), f32),
            pltpu.VMEM((chips, 5, 16, LANES), f32),
            pltpu.VMEM((5, cells, LANES), f32),
            pltpu.VMEM((5, cells, LANES), f32),
            pltpu.VMEM((2, 5, cells + 16, LANES), f32),
            pltpu.VMEM((3, 2, 5, TILE, LANES), f32),
            pltpu.VMEM((3, 2, 5, TILE, LANES), f32),
            pltpu.VMEM((2, 5, TILE, LANES), f32),
            pltpu.VMEM((3, 5, cells // 4, LANES), f32),
            pltpu.VMEM((3, 5, cells // 4, LANES), f32),
            pltpu.VMEM((5, 2 * cells + 8, LANES), f32),
            dma((chips,)), dma((chips,)), dma((chips,)), dma((chips,)),
            dma((3, 2)), dma((3, 2)), dma((3,)), dma((3,)), dma((4,)), dma((4,)),
        ],
        compiler_params=pltpu.CompilerParams(
            collective_id=0, has_side_effects=True, vmem_limit_bytes=56 * 2**20
        ),
    )(offsets, density, velocity, pressure)


def whole_step(density, velocity, pressure, offsets):
    ax_count, az_count = lax.axis_size("ax"), lax.axis_size("az")
    if ax_count == 2 and az_count == 8 and density.shape == (1, 2, 32, 512):
        return banded(az_count, density, velocity, pressure, offsets)
    return body(density, velocity, pressure, offsets)


def solution(mesh):
    placed = (
        P("row", "ax", "az", None),
        P("row", None, "ax", "az", None),
        P("row", "ax", "az", None),
        P(),
    )
    return jax.shard_map(
        whole_step,
        mesh=mesh,
        in_specs=placed,
        out_specs=P("row", None, "ax", "az", None),
        check_vma=False,
    )
```

```python
import functools
import math

import jax
import jax.numpy as jnp
from jax import lax
from jax.experimental import pallas as pl
from jax.experimental.pallas import tpu as pltpu
from jax.sharding import PartitionSpec as P

HEAT_RATIO = 1.4
VISCOSITY = 0.8
CONDUCTION = 0.6
TIME_STEP = 0.1
AXIAL_FLUX = 1.0
AXIAL_CURVE = 4.0


def partner_2(value, axis, bit):
    mask = 2**bit
    pairs = [(source, source ^ mask) for source in range(lax.axis_size(axis))]
    return lax.ppermute(value, axis, pairs)


def padded(cells, sides, width, closed):
    for axis, dim in sides:
        count = lax.axis_size(axis)
        ends = count if closed else count - 1
        head = lax.slice_in_dim(cells, 0, width, axis=dim)
        tail = lax.slice_in_dim(cells, cells.shape[dim] - width, cells.shape[dim], axis=dim)
        cells = jnp.concatenate(
            [
                lax.ppermute(tail, axis, [(i, (i + 1) % count) for i in range(ends)]),
                cells,
                lax.ppermute(head, axis, [((i + 1) % count, i) for i in range(ends)]),
            ],
            axis=dim,
        )
    return cells


def conserved(density, velocity, pressure):
    momentum = density[:, None] * velocity
    energy = pressure / (HEAT_RATIO - 1.0) + 0.5 * density * jnp.sum(velocity * velocity, axis=1)
    return jnp.concatenate([density[:, None], momentum, energy[:, None]], axis=1)


def primitive(state):
    vel_theta = state[:, 1] / state[:, 0]
    vel_radial = state[:, 2] / state[:, 0]
    vel_axial = state[:, 3] / state[:, 0]
    press = (HEAT_RATIO - 1.0) * (
        state[:, 4]
        - 0.5 * (state[:, 1] * vel_theta + state[:, 2] * vel_radial + state[:, 3] * vel_axial)
    )
    return (vel_theta, vel_radial, vel_axial, press / state[:, 0], press)


def fluxes(state, values, direction):
    normal_vel = values[direction]
    press = values[4]
    flux_terms = [
        state[:, 0] * normal_vel,
        state[:, 1] * normal_vel,
        state[:, 2] * normal_vel,
        state[:, 3] * normal_vel,
        (state[:, 4] + press) * normal_vel,
    ]
    flux_terms[1 + direction] = flux_terms[1 + direction] + press
    return flux_terms


def extended(state, values_c, lower, upper, axis_pos):
    values_lo = primitive(lower)
    values_hi = primitive(upper)
    ext_state = jnp.concatenate([lower, state, upper], axis=axis_pos)
    ext_values = tuple(
        (
            jnp.concatenate([values_lo[k], values_c[k], values_hi[k]], axis=axis_pos - 1)
            for k in range(5)
        )
    )
    return (ext_state, ext_values)


def side_slices(items, axis_pos):
    size_now = items[0].shape[axis_pos] - 2
    lows = [lax.slice_in_dim(item, 0, size_now, axis=axis_pos) for item in items]
    highs = [lax.slice_in_dim(item, 2, size_now + 2, axis=axis_pos) for item in items]
    return (lows, highs)


def tendency(state, theta_ghosts, radial_ghosts, axial_ghosts, radius, dtheta):
    values_c = primitive(state)
    directions = [(theta_ghosts, 3), (radial_ghosts, 4), (axial_ghosts, 2)]
    flux_lo = []
    flux_hi = []
    value_lo = []
    value_hi = []
    for direction_index in range(3):
        ghosts, axis_pos = directions[direction_index]
        ext_state, ext_values = extended(state, values_c, ghosts[0], ghosts[1], axis_pos)
        flux_all = fluxes(ext_state, ext_values, direction_index)
        lows, highs = side_slices(flux_all, axis_pos - 1)
        flux_lo.append(lows)
        flux_hi.append(highs)
        vlows, vhighs = side_slices(list(ext_values), axis_pos - 1)
        value_lo.append(vlows)
        value_hi.append(vhighs)
    result = []
    for field_index in range(5):
        divergence = -(flux_hi[0][field_index] - flux_lo[0][field_index]) / (2.0 * radius * dtheta)
        divergence = divergence - (
            (radius + 1.0) * flux_hi[1][field_index] - (radius - 1.0) * flux_lo[1][field_index]
        ) / (2.0 * radius)
        divergence = divergence - AXIAL_FLUX * (flux_hi[2][field_index] - flux_lo[2][field_index])
        result.append(divergence)

    def viscous(which):
        center = values_c[which]
        beside_all = (value_hi[0][which] - 2.0 * center + value_lo[0][which]) / (
            radius * dtheta
        ) ** 2
        across = (
            (radius + 0.5) * (value_hi[1][which] - center)
            - (radius - 0.5) * (center - value_lo[1][which])
        ) / radius
        return (
            beside_all
            + across
            + AXIAL_CURVE * (value_hi[2][which] - 2.0 * center + value_lo[2][which])
        )

    density_now = state[:, 0]
    result[1] = (
        result[1]
        - density_now * values_c[0] * values_c[1] / radius
        + VISCOSITY
        * (
            viscous(0)
            - values_c[0] / radius**2
            + (value_hi[0][1] - value_lo[0][1]) / (radius**2 * dtheta)
        )
    )
    result[2] = (
        result[2]
        + (density_now * values_c[0] * values_c[0] + values_c[4]) / radius
        + VISCOSITY
        * (
            viscous(1)
            - values_c[1] / radius**2
            - (value_hi[0][0] - value_lo[0][0]) / (radius**2 * dtheta)
        )
    )
    result[3] = result[3] + VISCOSITY * viscous(2)
    result[4] = result[4] + CONDUCTION * viscous(3)
    return jnp.stack(result, axis=1)


def body(density, velocity, pressure, offsets):
    state0 = conserved(density, velocity, pressure)
    tile_cells = state0.shape[3]
    radial_cells = state0.shape[4]
    cycle_size = lax.axis_size("az")
    cycle_cells = tile_cells * cycle_size
    dtheta = 2.0 * math.pi / cycle_cells
    radius = cycle_cells / (2.0 * math.pi) + jnp.arange(radial_cells, dtype=jnp.float32) + 0.5
    at_outer = lax.axis_index("ax") == 0
    at_plane = lax.axis_index("ax") == lax.axis_size("ax") - 1
    is_rotor = lax.axis_index("row") == 0
    axial_sign = jnp.array([1.0, 1.0, 1.0, -1.0, 1.0], dtype=jnp.float32).reshape(5, 1, 1)
    wall_sign = jnp.array([1.0, -1.0, -1.0, -1.0, 1.0], dtype=jnp.float32).reshape(5, 1, 1, 1)

    def rotate_plane(partner, turn_cells):
        band = lax.all_to_all(partner, "az", split_axis=2, concat_axis=1, tiled=True)
        doubled = jnp.concatenate([band, band], axis=1)
        rolled = lax.dynamic_slice_in_dim(doubled, turn_cells, cycle_cells, 1)
        return lax.all_to_all(rolled, "az", split_axis=1, concat_axis=2, tiled=True)

    def full_rate(state, shift):
        top_plane = state[0, :, -1] * axial_sign
        partner = partner_2(top_plane, "row", 0)
        turn_cells = jnp.where(is_rotor, shift, (cycle_cells - shift) % cycle_cells)
        ghost_plane = rotate_plane(partner, turn_cells)
        cycle_pad = padded(state, (("az", 3),), 1, True)
        theta_lo = cycle_pad[:, :, :, :1]
        theta_hi = cycle_pad[:, :, :, -1:]
        plane_pad = padded(state, (("ax", 2),), 1, False)
        lower_ghost = plane_pad[:, :, :1]
        upper_ghost = plane_pad[:, :, -1:]
        lower_ghost = jnp.where(at_outer, state[:, :, :1], lower_ghost)
        upper_ghost = jnp.where(at_plane, ghost_plane[None, :, None], upper_ghost)
        radial_lo = state[..., :1] * wall_sign
        radial_hi = state[..., -1:] * wall_sign
        return tendency(
            state,
            (theta_lo, theta_hi),
            (radial_lo, radial_hi),
            (lower_ghost, upper_ghost),
            radius,
            dtheta,
        )

    state1 = state0 + TIME_STEP * full_rate(state0, offsets[0])
    state2 = 0.75 * state0 + 0.25 * (state1 + TIME_STEP * full_rate(state1, offsets[1]))
    return state0 / 3.0 + 2.0 / 3.0 * (state2 + TIME_STEP * full_rate(state2, offsets[2]))


LANES = 128
TILE = 8
PEER = pl.DeviceIdType.MESH
RUNGE_KUTTA = ((0.0, 1.0), (0.75, 0.25), (1.0 / 3.0, 2.0 / 3.0))


def band_of(ax, az, wide):
    deep, side = az // 2, az % 2
    column = side + ax * (3 - 2 * side)
    return column * wide + deep + (column % 2) * (wide - 1 - 2 * deep)


def chip_of(band, wide):
    column, step = band // wide, band % wide
    ax = column // 2
    side = (column + ax) % 2
    deep = step + (column % 2) * (wide - 1 - 2 * step)
    return ax, deep * 2 + side


def spread(j, half):
    return half + (j % 2) * ((j + 1) // 2) - (1 - j % 2) * (j // 2)


def kernel(
    az_count,
    off_hbm, den_hbm, vel_hbm, pre_hbm, out_ref,
    off_ref, den_ref, vel_ref, pre_ref,
    send1, recv1, send2, recv2, base, now, prim, halo_out, halo_in, halo, plane_out, plane_in, ghost,
    s1, r1, s2, r2, sh, rh, sp, rp, s_in,
):
    chips = 2 * az_count
    half = az_count // 2
    wide = az_count // 2
    turn_cells = 32 * az_count
    tiles = 4
    row = lax.axis_index("row")
    ax = lax.axis_index("ax")
    az = lax.axis_index("az")
    me = ax * az_count + az
    band = band_of(ax, az, wide)

    def chip_id(flat):
        return (row, flat // az_count, flat % az_count)

    def band_id(which):
        return (row,) + chip_of(which, wide)

    loads = [
        pltpu.make_async_copy(src, dst, s_in.at[n])
        for n, (src, dst) in enumerate((
            (den_hbm, den_ref), (pre_hbm, pre_ref), (vel_hbm, vel_ref), (off_hbm, off_ref)))
    ]
    for load in loads:
        load.start()
    barrier = pltpu.get_barrier_semaphore()
    for i in range(1, chips):
        pl.semaphore_signal(barrier, inc=1, device_id=chip_id((me + i) % chips), device_id_type=PEER)
    pl.semaphore_signal(barrier, inc=1, device_id=(1 - row, ax, az), device_id_type=PEER)

    lane = lax.broadcasted_iota(jnp.int32, (TILE, LANES), 1)
    part = lane // 32
    inner = lane % 32

    for load in loads:
        load.wait()

    for f in range(5):
        for i in range(2):
            for col in range(4):
                source = []
                for h in range(2):
                    for k in range(2):
                        rows = pl.ds(16 * h + 8 * i, 8)
                        cols = pl.ds(128 * col, 128)
                        if f == 0:
                            tile = den_ref[0, k, rows, cols]
                        elif f == 4:
                            tile = pre_ref[0, k, rows, cols] / den_ref[0, k, rows, cols]
                        else:
                            tile = vel_ref[0, f - 1, k, rows, cols]
                        source.append(tile)
                for sub in range(4):
                    mixed = None
                    for q in range(4):
                        turn = (32 * (q - sub)) % 128
                        moved = pltpu.roll(source[q], turn, axis=1) if turn else source[q]
                        mixed = moved if mixed is None else jnp.where(part == q, moved, mixed)
                    send1[4 * col + sub, f, 8 * i:8 * i + 8, :] = mixed

    pl.semaphore_wait(barrier, chips)

    def first_copy(flat):
        return pltpu.make_async_remote_copy(
            src_ref=send1.at[band_of(flat // az_count, flat % az_count, wide)],
            dst_ref=recv1.at[me],
            send_sem=s1.at[flat],
            recv_sem=r1.at[me],
            device_id=chip_id(flat),
            device_id_type=PEER,
        )

    def others():
        for j in range(az_count):
            for x in range(2):
                offset = spread(j, half) % az_count
                if offset or x:
                    yield ((ax + x) % 2) * az_count + (az + az_count - offset) % az_count

    for flat in others():
        first_copy(flat).start()
    recv1[me] = send1[band]

    dtheta = 2.0 * math.pi / turn_cells
    radius = turn_cells / (2.0 * math.pi) + (band * 32 + inner).astype(jnp.float32) + 0.5
    inverse = 1.0 / radius
    c_turn = inverse * (0.5 / dtheta)
    c_out = 0.5 * (radius + 1.0) * inverse
    c_in = 0.5 * (radius - 1.0) * inverse
    l_turn = (inverse * (1.0 / dtheta)) * (inverse * (1.0 / dtheta))
    l_out = (radius + 0.5) * inverse
    l_in = (radius - 0.5) * inverse
    l_mid = 2.0 * l_turn + (2.0 + 2.0 * AXIAL_CURVE)
    inverse2 = inverse * inverse
    c_cross = inverse2 * (VISCOSITY / dtheta)
    r_low = turn_cells / (2.0 * math.pi) + (lane * 0 + band * 32).astype(jnp.float32) + 0.5
    r_high = r_low + 31.0
    edge_c = (0.5 * (r_low - 1.0) / r_low, -0.5 * (r_high + 1.0) / r_high)
    edge_l = ((r_low - 0.5) / r_low, (r_high + 0.5) / r_high)
    zero = jnp.zeros((TILE, LANES), jnp.float32)
    c_in = jnp.where(inner == 0, zero, c_in)
    l_in = jnp.where(inner == 0, zero, l_in)
    c_out = jnp.where(inner == 31, zero, c_out)
    l_out = jnp.where(inner == 31, zero, l_out)

    def pack(tiles_of, a, slot):
        group = a // quarter
        for f in range(5):
            low, high = halo_out[slot, 0, f], halo_out[slot, 1, f]
            for t in range(tiles):
                w, tile_index = tiles_of[t][f], a * 4 + t
                low = jnp.where(inner == tile_index, pltpu.roll(w, tile_index + 97, axis=1), low)
                high = jnp.where(inner == tile_index, pltpu.roll(w, tile_index, axis=1), high)
                moved = pltpu.roll(w, (32 * group + 32) % 128, axis=1)
                rows = pl.ds(pl.multiple_of((a % quarter) * 32 + t * 8, 8), 8)
                plane_out[slot, f, rows, :] = jnp.where(part == group, moved, plane_out[slot, f, rows, :])
            halo_out[slot, 0, f], halo_out[slot, 1, f] = low, high

    def wrap(which, a, tiles_of):
        @pl.when(a == 0)
        def _():
            for f in range(5):
                prim[which, f, turn_cells + 8:turn_cells + 16, :] = tiles_of[0][f]

        @pl.when(a == az_count - 1)
        def _():
            for f in range(5):
                prim[which, f, 0:8, :] = tiles_of[tiles - 1][f]

    def neighbour_copies(slot):
        copies = []
        for side, to in ((0, (band + 1) % chips), (1, (band + chips - 1) % chips)):
            copies.append(pltpu.make_async_remote_copy(
                src_ref=halo_out.at[slot, side],
                dst_ref=halo_in.at[slot, side],
                send_sem=sh.at[slot, side],
                recv_sem=rh.at[slot, side],
                device_id=band_id(to),
                device_id_type=PEER,
            ))
        copies.append(pltpu.make_async_remote_copy(
            src_ref=plane_out.at[slot],
            dst_ref=plane_in.at[slot],
            send_sem=sp.at[slot],
            recv_sem=rp.at[slot],
            device_id=(1 - row, ax, az),
            device_id_type=PEER,
        ))
        return copies

    quarter = az_count // 4
    drag = (0.0, VISCOSITY, VISCOSITY, VISCOSITY, CONDUCTION)

    def flux(w, d):
        rho, vt, vr, vz, temp = w
        m = rho * w[1 + d]
        terms = [m, m * vt, m * vr, m * vz,
                 m * (3.5 * temp + 0.5 * (vt * vt + vr * vr + vz * vz))]
        terms[1 + d] = terms[1 + d] + rho * temp
        return terms

    def inside(a, step):
        which = step % 2
        keep, fresh = RUNGE_KUTTA[step]
        for t in range(tiles):
            row0 = a * 32 + t * 8
            mid, tl, th, rl, rr, zl, zh = [], [], [], [], [], [], []
            for f in range(5):
                c = prim[which, f, pl.ds(pl.multiple_of(row0 + 8, 8), 8), :]
                mid.append(c)
                tl.append(prim[which, f, pl.ds(row0 + 7, 8), :])
                th.append(prim[which, f, pl.ds(row0 + 9, 8), :])
                rl.append(pltpu.roll(c, 1, axis=1))
                rr.append(pltpu.roll(c, 127, axis=1))
                zl.append(jnp.where(part == 0, c, pltpu.roll(c, 32, axis=1)))
                zh.append(jnp.where(part == 3, zero, pltpu.roll(c, 96, axis=1)))
            ftl, fth = flux(tl, 0), flux(th, 0)
            frl, frh = flux(rl, 1), flux(rr, 1)
            fzl, fzh = flux(zl, 2), flux(zh, 2)
            total = [
                c_turn * (ftl[f] - fth[f]) + (c_in * frl[f] - c_out * frh[f]) + (fzl[f] - fzh[f])
                for f in range(5)
            ]

            def lap(n):
                return (l_turn * (th[n] + tl[n]) + (l_out * rr[n] + l_in * rl[n])
                        + AXIAL_CURVE * (zh[n] + zl[n]) - l_mid * mid[n])

            rho, vt, vr, vz, temp = mid
            total[1] = (total[1] - rho * vt * vr * inverse
                        + VISCOSITY * (lap(1) - vt * inverse2) + c_cross * (th[2] - tl[2]))
            total[2] = (total[2] + rho * (vt * vt + temp) * inverse
                        + VISCOSITY * (lap(2) - vr * inverse2) - c_cross * (th[1] - tl[1]))
            total[3] = total[3] + VISCOSITY * lap(3)
            total[4] = total[4] + CONDUCTION * lap(4)
            rows = pl.ds(pl.multiple_of(row0, 8), 8)
            for f in range(5):
                value = fresh * (now[f, rows, :] + TIME_STEP * total[f])
                if keep:
                    value = value + keep * base[f, rows, :]
                now[f, rows, :] = value

    def unpack(a):
        tiles_of = []
        for t in range(tiles):
            h, i = t // 2, t % 2
            w = []
            for f in range(5):
                c0 = recv1[a, f, 8 * i:8 * i + 8, :]
                c1 = recv1[az_count + a, f, 8 * i:8 * i + 8, :]
                if h == 0:
                    w.append(jnp.where(part < 2, c0, pltpu.roll(c1, 64, axis=1)))
                else:
                    w.append(jnp.where(part < 2, pltpu.roll(c0, 64, axis=1), c1))
            rho, vt, vr, vz, temp = w
            rows = pl.ds(pl.multiple_of(a * 32 + t * 8, 8), 8)
            rows_pad = pl.ds(pl.multiple_of(a * 32 + t * 8 + 8, 8), 8)
            state = (rho, rho * vt, rho * vr, rho * vz,
                     rho * (temp / (HEAT_RATIO - 1.0) + 0.5 * (vt * vt + vr * vr + vz * vz)))
            for f in range(5):
                base[f, rows, :] = state[f]
                now[f, rows, :] = state[f]
                prim[0, f, rows_pad, :] = w[f]
            tiles_of.append(w)
        wrap(0, a, tiles_of)
        pack(tiles_of, a, 0)

    def arrive(j, carry):
        a = (az + spread(j, half)) % az_count
        for x in range(2):
            flat = x * az_count + a

            @pl.when(flat != me)
            def _():
                pltpu.make_async_remote_copy(
                    src_ref=send1.at[flat],
                    dst_ref=recv1.at[flat],
                    send_sem=s1.at[flat],
                    recv_sem=r1.at[flat],
                    device_id=chip_id(flat),
                    device_id_type=PEER,
                ).wait_recv()

        unpack(a)

        @pl.when(j >= 2)
        def _():
            inside((az + spread(j - 2, half)) % az_count, 0)

        return carry

    lax.fori_loop(0, az_count, arrive, 0)

    def second_copy(flat):
        return pltpu.make_async_remote_copy(
            src_ref=send2.at[flat],
            dst_ref=recv2.at[band],
            send_sem=s2.at[flat],
            recv_sem=r2.at[band],
            device_id=chip_id(flat),
            device_id_type=PEER,
        )

    signs = (1.0, -1.0, -1.0, -1.0, 1.0)
    for step in range(3):
        copies = neighbour_copies(step)
        for copy in copies:
            copy.start()
        if step == 0:
            def rest(j, carry):
                inside((az + spread(j + az_count - 2, half)) % az_count, 0)
                return carry

            lax.fori_loop(0, 2, rest, 0)
        else:
            def sweep(a, carry, step=step):
                inside((az + spread(a, half)) % az_count, step)
                return carry

            lax.fori_loop(0, az_count if step == 1 else half, sweep, 0)
        for copy in copies:
            copy.wait()
        weight = TIME_STEP * RUNGE_KUTTA[step][1]
        walls = (band == 0, band == chips - 1)
        for side in range(2):
            w = [
                jnp.where(walls[side], signs[f] * halo_out[step, 1 - side, f], halo_in[step, side, f])
                for f in range(5)
            ]
            terms = flux(w, 1)
            for f in range(5):
                value = edge_c[side] * terms[f]
                if f:
                    value = value + drag[f] * edge_l[side] * w[f]
                halo[side, f] = weight * value

        def slide(n, carry, step=step, weight=weight):
            rows = pl.ds(pl.multiple_of(n * 8, 8), 8)
            w = [plane_in[step, f, rows, :] for f in range(5)]
            w[3] = -w[3]
            terms = flux(w, 2)
            for f in range(5):
                value = -terms[f]
                if f:
                    value = value + (AXIAL_CURVE * drag[f]) * w[f]
                value = weight * value
                for g in range(4):
                    moved = pltpu.roll(value, 96 - 32 * g, axis=1) if g != 3 else value
                    place = 32 * quarter * g + n * 8
                    ghost[f, pl.ds(pl.multiple_of(place, 8), 8), :] = moved
                    ghost[f, pl.ds(pl.multiple_of(turn_cells + place, 8), 8), :] = moved
            return carry

        lax.fori_loop(0, 4 * quarter, slide, 0)
        shift = off_ref[step]
        shift = jnp.where(row == 0, shift, turn_cells - shift)

        def edges(j, carry, step=step, shift=shift):
            which = step % 2
            a = j if step < 2 else (az + spread(j, half)) % az_count
            if step == 2:
                @pl.when(j >= half)
                def _():
                    inside(a, step)

            states, prims = [], []
            for t in range(tiles):
                tile_index = a * 4 + t
                row0 = a * 32 + t * 8
                rows = pl.ds(pl.multiple_of(row0, 8), 8)
                state = []
                for f in range(5):
                    low = pltpu.roll(halo[0, f], 128 - tile_index, axis=1)
                    high = pltpu.roll(halo[1, f], 128 + 31 - tile_index, axis=1)
                    extra = jnp.where(inner == 0, low, jnp.where(inner == 31, high, zero))
                    extra = extra + jnp.where(part == 3, ghost[f, pl.ds(row0 + shift, 8), :], zero)
                    state.append(now[f, rows, :] + extra)
                if step < 2:
                    inv = 1.0 / state[0]
                    vt, vr, vz = state[1] * inv, state[2] * inv, state[3] * inv
                    press = (HEAT_RATIO - 1.0) * (
                        state[4] - 0.5 * (state[1] * vt + state[2] * vr + state[3] * vz))
                    w = [state[0], vt, vr, vz, press * inv]
                    rows_pad = pl.ds(pl.multiple_of(row0 + 8, 8), 8)
                    for f in range(5):
                        now[f, rows, :] = state[f]
                        prim[1 - which, f, rows_pad, :] = w[f]
                    prims.append(w)
                else:
                    states.append(state)
            if step < 2:
                wrap(1 - which, a, prims)
                pack(prims, a, step + 1)
                return carry
            for f in range(5):
                for i in range(2):
                    upper, lower = states[i][f], states[2 + i][f]
                    send2[a, f, 8 * i:8 * i + 8, :] = jnp.where(part < 2, upper, pltpu.roll(lower, 64, axis=1))
                    send2[az_count + a, f, 8 * i:8 * i + 8, :] = jnp.where(
                        part < 2, pltpu.roll(upper, 64, axis=1), lower)
            for x in range(2):
                flat = x * az_count + a

                @pl.when(flat != me)
                def _():
                    second_copy(flat).start()

                @pl.when(flat == me)
                def _():
                    recv2[band] = send2[me]
            return carry

        lax.fori_loop(0, az_count, edges, 0)

    for col in range(4):
        for sub in range(4):
            from_band = 4 * col + sub
            from_ax, from_az = chip_of(from_band, wide)
            flat = from_ax * az_count + from_az

            @pl.when(flat != me)
            def _():
                pltpu.make_async_remote_copy(
                    src_ref=send2.at[flat],
                    dst_ref=recv2.at[from_band],
                    send_sem=s2.at[flat],
                    recv_sem=r2.at[from_band],
                    device_id=chip_id(flat),
                    device_id_type=PEER,
                ).wait_recv()

        for f in range(5):
            for i in range(2):
                source = [recv2[4 * col + sub, f, 8 * i:8 * i + 8, :] for sub in range(4)]
                for q in range(4):
                    h, k = q // 2, q % 2
                    mixed = None
                    for sub in range(4):
                        turn = (32 * (sub - q)) % 128
                        moved = pltpu.roll(source[sub], turn, axis=1) if turn else source[sub]
                        mixed = moved if mixed is None else jnp.where(part == sub, moved, mixed)
                    out_ref[0, f, k, 16 * h + 8 * i:16 * h + 8 * i + 8, 128 * col:128 * col + 128] = mixed

    for flat in others():
        first_copy(flat).wait_send()
        second_copy(flat).wait_send()


def banded(az_count, density, velocity, pressure, offsets):
    chips = 2 * az_count
    cells = 32 * az_count
    f32 = jnp.float32
    dma = pltpu.SemaphoreType.DMA
    anywhere = pl.BlockSpec(memory_space=pl.ANY)
    return pl.pallas_call(
        functools.partial(kernel, az_count),
        out_shape=jax.ShapeDtypeStruct((1, 5) + density.shape[1:], f32),
        in_specs=[anywhere] * 4,
        out_specs=pl.BlockSpec(memory_space=pltpu.VMEM),
        scratch_shapes=[
            pltpu.SMEM(offsets.shape, jnp.int32),
            pltpu.VMEM(density.shape, f32),
            pltpu.VMEM(velocity.shape, f32),
            pltpu.VMEM(pressure.shape, f32),
            pltpu.VMEM((chips, 5, 16, LANES), f32),
            pltpu.VMEM((chips, 5, 16, LANES), f32),
            pltpu.VMEM((chips, 5, 16, LANES), f32),
            pltpu.VMEM((chips, 5, 16, LANES), f32),
            pltpu.VMEM((5, cells, LANES), f32),
            pltpu.VMEM((5, cells, LANES), f32),
            pltpu.VMEM((2, 5, cells + 16, LANES), f32),
            pltpu.VMEM((3, 2, 5, TILE, LANES), f32),
            pltpu.VMEM((3, 2, 5, TILE, LANES), f32),
            pltpu.VMEM((2, 5, TILE, LANES), f32),
            pltpu.VMEM((3, 5, cells // 4, LANES), f32),
            pltpu.VMEM((3, 5, cells // 4, LANES), f32),
            pltpu.VMEM((5, 2 * cells + 8, LANES), f32),
            dma((chips,)), dma((chips,)), dma((chips,)), dma((chips,)),
            dma((3, 2)), dma((3, 2)), dma((3,)), dma((3,)), dma((4,)),
        ],
        compiler_params=pltpu.CompilerParams(
            collective_id=0, has_side_effects=True, vmem_limit_bytes=56 * 2**20
        ),
    )(offsets, density, velocity, pressure)


def whole_step(density, velocity, pressure, offsets):
    ax_count, az_count = lax.axis_size("ax"), lax.axis_size("az")
    if ax_count == 2 and az_count == 8 and density.shape == (1, 2, 32, 512):
        return banded(az_count, density, velocity, pressure, offsets)
    return body(density, velocity, pressure, offsets)


def solution(mesh):
    placed = (
        P("row", "ax", "az", None),
        P("row", None, "ax", "az", None),
        P("row", "ax", "az", None),
        P(),
    )
    return jax.shard_map(
        whole_step,
        mesh=mesh,
        in_specs=placed,
        out_specs=P("row", None, "ax", "az", None),
        check_vma=False,
    )
```

```python
import functools
import math

import jax
import jax.numpy as jnp
from jax import lax
from jax.experimental import pallas as pl
from jax.experimental.pallas import tpu as pltpu
from jax.sharding import PartitionSpec as P

HEAT_RATIO = 1.4
VISCOSITY = 0.8
CONDUCTION = 0.6
TIME_STEP = 0.1
AXIAL_FLUX = 1.0
AXIAL_CURVE = 4.0


def partner_2(value, axis, bit):
    mask = 2**bit
    pairs = [(source, source ^ mask) for source in range(lax.axis_size(axis))]
    return lax.ppermute(value, axis, pairs)


def padded(cells, sides, width, closed):
    for axis, dim in sides:
        count = lax.axis_size(axis)
        ends = count if closed else count - 1
        head = lax.slice_in_dim(cells, 0, width, axis=dim)
        tail = lax.slice_in_dim(cells, cells.shape[dim] - width, cells.shape[dim], axis=dim)
        cells = jnp.concatenate(
            [
                lax.ppermute(tail, axis, [(i, (i + 1) % count) for i in range(ends)]),
                cells,
                lax.ppermute(head, axis, [((i + 1) % count, i) for i in range(ends)]),
            ],
            axis=dim,
        )
    return cells


def conserved(density, velocity, pressure):
    momentum = density[:, None] * velocity
    energy = pressure / (HEAT_RATIO - 1.0) + 0.5 * density * jnp.sum(velocity * velocity, axis=1)
    return jnp.concatenate([density[:, None], momentum, energy[:, None]], axis=1)


def primitive(state):
    vel_theta = state[:, 1] / state[:, 0]
    vel_radial = state[:, 2] / state[:, 0]
    vel_axial = state[:, 3] / state[:, 0]
    press = (HEAT_RATIO - 1.0) * (
        state[:, 4]
        - 0.5 * (state[:, 1] * vel_theta + state[:, 2] * vel_radial + state[:, 3] * vel_axial)
    )
    return (vel_theta, vel_radial, vel_axial, press / state[:, 0], press)


def fluxes(state, values, direction):
    normal_vel = values[direction]
    press = values[4]
    flux_terms = [
        state[:, 0] * normal_vel,
        state[:, 1] * normal_vel,
        state[:, 2] * normal_vel,
        state[:, 3] * normal_vel,
        (state[:, 4] + press) * normal_vel,
    ]
    flux_terms[1 + direction] = flux_terms[1 + direction] + press
    return flux_terms


def extended(state, values_c, lower, upper, axis_pos):
    values_lo = primitive(lower)
    values_hi = primitive(upper)
    ext_state = jnp.concatenate([lower, state, upper], axis=axis_pos)
    ext_values = tuple(
        (
            jnp.concatenate([values_lo[k], values_c[k], values_hi[k]], axis=axis_pos - 1)
            for k in range(5)
        )
    )
    return (ext_state, ext_values)


def side_slices(items, axis_pos):
    size_now = items[0].shape[axis_pos] - 2
    lows = [lax.slice_in_dim(item, 0, size_now, axis=axis_pos) for item in items]
    highs = [lax.slice_in_dim(item, 2, size_now + 2, axis=axis_pos) for item in items]
    return (lows, highs)


def tendency(state, theta_ghosts, radial_ghosts, axial_ghosts, radius, dtheta):
    values_c = primitive(state)
    directions = [(theta_ghosts, 3), (radial_ghosts, 4), (axial_ghosts, 2)]
    flux_lo = []
    flux_hi = []
    value_lo = []
    value_hi = []
    for direction_index in range(3):
        ghosts, axis_pos = directions[direction_index]
        ext_state, ext_values = extended(state, values_c, ghosts[0], ghosts[1], axis_pos)
        flux_all = fluxes(ext_state, ext_values, direction_index)
        lows, highs = side_slices(flux_all, axis_pos - 1)
        flux_lo.append(lows)
        flux_hi.append(highs)
        vlows, vhighs = side_slices(list(ext_values), axis_pos - 1)
        value_lo.append(vlows)
        value_hi.append(vhighs)
    result = []
    for field_index in range(5):
        divergence = -(flux_hi[0][field_index] - flux_lo[0][field_index]) / (2.0 * radius * dtheta)
        divergence = divergence - (
            (radius + 1.0) * flux_hi[1][field_index] - (radius - 1.0) * flux_lo[1][field_index]
        ) / (2.0 * radius)
        divergence = divergence - AXIAL_FLUX * (flux_hi[2][field_index] - flux_lo[2][field_index])
        result.append(divergence)

    def viscous(which):
        center = values_c[which]
        beside_all = (value_hi[0][which] - 2.0 * center + value_lo[0][which]) / (
            radius * dtheta
        ) ** 2
        across = (
            (radius + 0.5) * (value_hi[1][which] - center)
            - (radius - 0.5) * (center - value_lo[1][which])
        ) / radius
        return (
            beside_all
            + across
            + AXIAL_CURVE * (value_hi[2][which] - 2.0 * center + value_lo[2][which])
        )

    density_now = state[:, 0]
    result[1] = (
        result[1]
        - density_now * values_c[0] * values_c[1] / radius
        + VISCOSITY
        * (
            viscous(0)
            - values_c[0] / radius**2
            + (value_hi[0][1] - value_lo[0][1]) / (radius**2 * dtheta)
        )
    )
    result[2] = (
        result[2]
        + (density_now * values_c[0] * values_c[0] + values_c[4]) / radius
        + VISCOSITY
        * (
            viscous(1)
            - values_c[1] / radius**2
            - (value_hi[0][0] - value_lo[0][0]) / (radius**2 * dtheta)
        )
    )
    result[3] = result[3] + VISCOSITY * viscous(2)
    result[4] = result[4] + CONDUCTION * viscous(3)
    return jnp.stack(result, axis=1)


def body(density, velocity, pressure, offsets):
    state0 = conserved(density, velocity, pressure)
    tile_cells = state0.shape[3]
    radial_cells = state0.shape[4]
    cycle_size = lax.axis_size("az")
    cycle_cells = tile_cells * cycle_size
    dtheta = 2.0 * math.pi / cycle_cells
    radius = cycle_cells / (2.0 * math.pi) + jnp.arange(radial_cells, dtype=jnp.float32) + 0.5
    at_outer = lax.axis_index("ax") == 0
    at_plane = lax.axis_index("ax") == lax.axis_size("ax") - 1
    is_rotor = lax.axis_index("row") == 0
    axial_sign = jnp.array([1.0, 1.0, 1.0, -1.0, 1.0], dtype=jnp.float32).reshape(5, 1, 1)
    wall_sign = jnp.array([1.0, -1.0, -1.0, -1.0, 1.0], dtype=jnp.float32).reshape(5, 1, 1, 1)

    def rotate_plane(partner, turn_cells):
        band = lax.all_to_all(partner, "az", split_axis=2, concat_axis=1, tiled=True)
        doubled = jnp.concatenate([band, band], axis=1)
        rolled = lax.dynamic_slice_in_dim(doubled, turn_cells, cycle_cells, 1)
        return lax.all_to_all(rolled, "az", split_axis=1, concat_axis=2, tiled=True)

    def full_rate(state, shift):
        top_plane = state[0, :, -1] * axial_sign
        partner = partner_2(top_plane, "row", 0)
        turn_cells = jnp.where(is_rotor, shift, (cycle_cells - shift) % cycle_cells)
        ghost_plane = rotate_plane(partner, turn_cells)
        cycle_pad = padded(state, (("az", 3),), 1, True)
        theta_lo = cycle_pad[:, :, :, :1]
        theta_hi = cycle_pad[:, :, :, -1:]
        plane_pad = padded(state, (("ax", 2),), 1, False)
        lower_ghost = plane_pad[:, :, :1]
        upper_ghost = plane_pad[:, :, -1:]
        lower_ghost = jnp.where(at_outer, state[:, :, :1], lower_ghost)
        upper_ghost = jnp.where(at_plane, ghost_plane[None, :, None], upper_ghost)
        radial_lo = state[..., :1] * wall_sign
        radial_hi = state[..., -1:] * wall_sign
        return tendency(
            state,
            (theta_lo, theta_hi),
            (radial_lo, radial_hi),
            (lower_ghost, upper_ghost),
            radius,
            dtheta,
        )

    state1 = state0 + TIME_STEP * full_rate(state0, offsets[0])
    state2 = 0.75 * state0 + 0.25 * (state1 + TIME_STEP * full_rate(state1, offsets[1]))
    return state0 / 3.0 + 2.0 / 3.0 * (state2 + TIME_STEP * full_rate(state2, offsets[2]))


LANES = 128
TILE = 8
PEER = pl.DeviceIdType.MESH
RUNGE_KUTTA = ((0.0, 1.0), (0.75, 0.25), (1.0 / 3.0, 2.0 / 3.0))


def band_of(ax, az, wide):
    deep, side = az // 2, az % 2
    column = side + ax * (3 - 2 * side)
    return column * wide + deep + (column % 2) * (wide - 1 - 2 * deep)


def chip_of(band, wide):
    column, step = band // wide, band % wide
    ax = column // 2
    side = (column + ax) % 2
    deep = step + (column % 2) * (wide - 1 - 2 * step)
    return ax, deep * 2 + side


def spread(j, half):
    return half + (j % 2) * ((j + 1) // 2) - (1 - j % 2) * (j // 2)


def kernel(
    az_count,
    off_hbm, den_hbm, vel_hbm, pre_hbm, out_ref,
    off_ref, den_ref, vel_ref, pre_ref,
    send1, recv1, send2, recv2, base, now, prim, halo_out, halo_in, halo, plane_out, plane_in, ghost,
    s1, r1, s2, r2, sh, rh, sp, rp, s_in,
):
    chips = 2 * az_count
    half = az_count // 2
    wide = az_count // 2
    turn_cells = 32 * az_count
    tiles = 4
    row = lax.axis_index("row")
    ax = lax.axis_index("ax")
    az = lax.axis_index("az")
    me = ax * az_count + az
    band = band_of(ax, az, wide)

    def chip_id(flat):
        return (row, flat // az_count, flat % az_count)

    def band_id(which):
        return (row,) + chip_of(which, wide)

    loads = [
        pltpu.make_async_copy(src, dst, s_in.at[n])
        for n, (src, dst) in enumerate((
            (den_hbm, den_ref), (pre_hbm, pre_ref), (vel_hbm, vel_ref), (off_hbm, off_ref)))
    ]
    for load in loads:
        load.start()
    barrier = pltpu.get_barrier_semaphore()
    for i in range(1, chips):
        pl.semaphore_signal(barrier, inc=1, device_id=chip_id((me + i) % chips), device_id_type=PEER)
    pl.semaphore_signal(barrier, inc=1, device_id=(1 - row, ax, az), device_id_type=PEER)

    lane = lax.broadcasted_iota(jnp.int32, (TILE, LANES), 1)
    part = lane // 32
    inner = lane % 32

    for load in loads:
        load.wait()

    for f in range(5):
        for i in range(2):
            for col in range(4):
                source = []
                for h in range(2):
                    for k in range(2):
                        rows = pl.ds(16 * h + 8 * i, 8)
                        cols = pl.ds(128 * col, 128)
                        if f == 0:
                            tile = den_ref[0, k, rows, cols]
                        elif f == 4:
                            tile = pre_ref[0, k, rows, cols] / den_ref[0, k, rows, cols]
                        else:
                            tile = vel_ref[0, f - 1, k, rows, cols]
                        source.append(tile)
                for sub in range(4):
                    mixed = None
                    for q in range(4):
                        turn = (32 * (q - sub)) % 128
                        moved = pltpu.roll(source[q], turn, axis=1) if turn else source[q]
                        mixed = moved if mixed is None else jnp.where(part == q, moved, mixed)
                    send1[4 * col + sub, f, 8 * i:8 * i + 8, :] = mixed

    pl.semaphore_wait(barrier, chips)

    def first_copy(flat):
        return pltpu.make_async_remote_copy(
            src_ref=send1.at[band_of(flat // az_count, flat % az_count, wide)],
            dst_ref=recv1.at[me],
            send_sem=s1.at[flat],
            recv_sem=r1.at[me],
            device_id=chip_id(flat),
            device_id_type=PEER,
        )

    def others():
        for j in range(az_count):
            for x in range(2):
                offset = spread(j, half) % az_count
                if offset or x:
                    yield ((ax + x) % 2) * az_count + (az + az_count - offset) % az_count

    for flat in others():
        first_copy(flat).start()
    recv1[me] = send1[band]

    dtheta = 2.0 * math.pi / turn_cells
    radius = turn_cells / (2.0 * math.pi) + (band * 32 + inner).astype(jnp.float32) + 0.5
    inverse = 1.0 / radius
    c_turn = inverse * (0.5 / dtheta)
    l_turn = (inverse * (1.0 / dtheta)) * (inverse * (1.0 / dtheta))
    l_mid = 2.0 * l_turn + (2.0 + 2.0 * AXIAL_CURVE)
    inverse2 = inverse * inverse
    c_cross = inverse2 * (VISCOSITY / dtheta)
    r_low = turn_cells / (2.0 * math.pi) + (lane * 0 + band * 32).astype(jnp.float32) + 0.5
    r_high = r_low + 31.0
    edge_c = (0.5 * (r_low - 1.0) / r_low, -0.5 * (r_high + 1.0) / r_high)
    edge_l = ((r_low - 0.5) / r_low, (r_high + 0.5) / r_high)
    zero = jnp.zeros((TILE, LANES), jnp.float32)
    give_next = jnp.where(inner == 31, zero, 0.5 * radius / (radius + 1.0))
    give_last = jnp.where(inner == 0, zero, -0.5 * radius / (radius - 1.0))
    drag_next = jnp.where(inner == 31, zero, (radius + 0.5) / (radius + 1.0))
    drag_last = jnp.where(inner == 0, zero, (radius - 0.5) / (radius - 1.0))

    def pack(tiles_of, a, slot):
        group = a // quarter
        for f in range(5):
            low, high = halo_out[slot, 0, f], halo_out[slot, 1, f]
            for t in range(tiles):
                w, tile_index = tiles_of[t][f], a * 4 + t
                low = jnp.where(inner == tile_index, pltpu.roll(w, tile_index + 97, axis=1), low)
                high = jnp.where(inner == tile_index, pltpu.roll(w, tile_index, axis=1), high)
                moved = pltpu.roll(w, (32 * group + 32) % 128, axis=1)
                rows = pl.ds(pl.multiple_of((a % quarter) * 32 + t * 8, 8), 8)
                plane_out[slot, f, rows, :] = jnp.where(part == group, moved, plane_out[slot, f, rows, :])
            halo_out[slot, 0, f], halo_out[slot, 1, f] = low, high

    def wrap(which, a, tiles_of):
        @pl.when(a == 0)
        def _():
            for f in range(5):
                prim[which, f, turn_cells + 8:turn_cells + 16, :] = tiles_of[0][f]

        @pl.when(a == az_count - 1)
        def _():
            for f in range(5):
                prim[which, f, 0:8, :] = tiles_of[tiles - 1][f]

    def neighbour_copies(slot):
        copies = []
        for side, to in ((0, (band + 1) % chips), (1, (band + chips - 1) % chips)):
            copies.append(pltpu.make_async_remote_copy(
                src_ref=halo_out.at[slot, side],
                dst_ref=halo_in.at[slot, side],
                send_sem=sh.at[slot, side],
                recv_sem=rh.at[slot, side],
                device_id=band_id(to),
                device_id_type=PEER,
            ))
        copies.append(pltpu.make_async_remote_copy(
            src_ref=plane_out.at[slot],
            dst_ref=plane_in.at[slot],
            send_sem=sp.at[slot],
            recv_sem=rp.at[slot],
            device_id=(1 - row, ax, az),
            device_id_type=PEER,
        ))
        return copies

    quarter = az_count // 4
    drag = (0.0, VISCOSITY, VISCOSITY, VISCOSITY, CONDUCTION)

    def flux(w, d):
        rho, vt, vr, vz, temp = w
        m = rho * w[1 + d]
        terms = [m, m * vt, m * vr, m * vz,
                 m * (3.5 * temp + 0.5 * (vt * vt + vr * vr + vz * vz))]
        terms[1 + d] = terms[1 + d] + rho * temp
        return terms

    def inside(a, step):
        which = step % 2
        keep, fresh = RUNGE_KUTTA[step]
        for t in range(tiles):
            row0 = a * 32 + t * 8
            mid = [prim[which, f, pl.ds(pl.multiple_of(row0 + 8, 8), 8), :] for f in range(5)]
            rho, vt, vr, vz, temp = mid
            heat = 3.5 * temp + 0.5 * (vt * vt + vr * vr + vz * vz)
            press = rho * temp
            spin = rho * vt
            total = [
                None,
                -inverse * (spin * vr) - (VISCOSITY * (l_mid + inverse2)) * vt,
                inverse * (spin * vt + press) - (VISCOSITY * (l_mid + inverse2)) * vr,
                -(VISCOSITY * l_mid) * vz,
                -(CONDUCTION * l_mid) * temp,
            ]
            m = rho * vz
            terms = [m, m * vt, m * vr, m * vz + press, m * heat]
            for f in range(5):
                up, down = terms[f], -terms[f]
                if f:
                    worn = (AXIAL_CURVE * drag[f]) * mid[f]
                    up, down = worn + terms[f], worn - terms[f]
                value = (jnp.where(part == 0, up, pltpu.roll(up, 32, axis=1))
                         + jnp.where(part == 3, zero, pltpu.roll(down, 96, axis=1)))
                total[f] = value if total[f] is None else total[f] + value
            m = rho * vr
            terms = [m, m * vt, m * vr + press, m * vz, m * heat]
            for f in range(5):
                out, back = give_next * terms[f], give_last * terms[f]
                if f:
                    worn = drag[f] * mid[f]
                    out, back = out + drag_next * worn, back + drag_last * worn
                total[f] = total[f] + pltpu.roll(out, 1, axis=1) + pltpu.roll(back, 127, axis=1)
            tl = [prim[which, f, pl.ds(row0 + 7, 8), :] for f in range(5)]
            th = [prim[which, f, pl.ds(row0 + 9, 8), :] for f in range(5)]
            ftl, fth = flux(tl, 0), flux(th, 0)
            for f in range(5):
                total[f] = total[f] + c_turn * (ftl[f] - fth[f])
                if f:
                    total[f] = total[f] + (drag[f] * l_turn) * (th[f] + tl[f])
            total[1] = total[1] + c_cross * (th[2] - tl[2])
            total[2] = total[2] - c_cross * (th[1] - tl[1])
            rows = pl.ds(pl.multiple_of(row0, 8), 8)
            for f in range(5):
                value = fresh * now[f, rows, :] + (fresh * TIME_STEP) * total[f]
                if keep:
                    value = value + keep * base[f, rows, :]
                now[f, rows, :] = value

    def unpack(a):
        tiles_of = []
        for t in range(tiles):
            h, i = t // 2, t % 2
            w = []
            for f in range(5):
                c0 = recv1[a, f, 8 * i:8 * i + 8, :]
                c1 = recv1[az_count + a, f, 8 * i:8 * i + 8, :]
                if h == 0:
                    w.append(jnp.where(part < 2, c0, pltpu.roll(c1, 64, axis=1)))
                else:
                    w.append(jnp.where(part < 2, pltpu.roll(c0, 64, axis=1), c1))
            rho, vt, vr, vz, temp = w
            rows = pl.ds(pl.multiple_of(a * 32 + t * 8, 8), 8)
            rows_pad = pl.ds(pl.multiple_of(a * 32 + t * 8 + 8, 8), 8)
            state = (rho, rho * vt, rho * vr, rho * vz,
                     rho * (temp / (HEAT_RATIO - 1.0) + 0.5 * (vt * vt + vr * vr + vz * vz)))
            for f in range(5):
                base[f, rows, :] = state[f]
                now[f, rows, :] = state[f]
                prim[0, f, rows_pad, :] = w[f]
            tiles_of.append(w)
        wrap(0, a, tiles_of)
        pack(tiles_of, a, 0)

    def arrive(j, carry):
        a = (az + spread(j, half)) % az_count
        for x in range(2):
            flat = x * az_count + a

            @pl.when(flat != me)
            def _():
                pltpu.make_async_remote_copy(
                    src_ref=send1.at[flat],
                    dst_ref=recv1.at[flat],
                    send_sem=s1.at[flat],
                    recv_sem=r1.at[flat],
                    device_id=chip_id(flat),
                    device_id_type=PEER,
                ).wait_recv()

        unpack(a)

        @pl.when(j >= 2)
        def _():
            inside((az + spread(j - 2, half)) % az_count, 0)

        return carry

    lax.fori_loop(0, az_count, arrive, 0)

    def second_copy(flat):
        return pltpu.make_async_remote_copy(
            src_ref=send2.at[flat],
            dst_ref=recv2.at[band],
            send_sem=s2.at[flat],
            recv_sem=r2.at[band],
            device_id=chip_id(flat),
            device_id_type=PEER,
        )

    signs = (1.0, -1.0, -1.0, -1.0, 1.0)
    for step in range(3):
        copies = neighbour_copies(step)
        for copy in copies:
            copy.start()
        if step == 0:
            def rest(j, carry):
                inside((az + spread(j + az_count - 2, half)) % az_count, 0)
                return carry

            lax.fori_loop(0, 2, rest, 0, unroll=2)
        else:
            def sweep(a, carry, step=step):
                inside((az + spread(a, half)) % az_count, step)
                return carry

            lax.fori_loop(0, az_count if step == 1 else half, sweep, 0, unroll=2)
        for copy in copies:
            copy.wait()
        weight = TIME_STEP * RUNGE_KUTTA[step][1]
        walls = (band == 0, band == chips - 1)
        for side in range(2):
            w = [
                jnp.where(walls[side], signs[f] * halo_out[step, 1 - side, f], halo_in[step, side, f])
                for f in range(5)
            ]
            terms = flux(w, 1)
            for f in range(5):
                value = edge_c[side] * terms[f]
                if f:
                    value = value + drag[f] * edge_l[side] * w[f]
                halo[side, f] = weight * value

        def slide(n, carry, step=step, weight=weight):
            rows = pl.ds(pl.multiple_of(n * 8, 8), 8)
            w = [plane_in[step, f, rows, :] for f in range(5)]
            w[3] = -w[3]
            terms = flux(w, 2)
            for f in range(5):
                value = -terms[f]
                if f:
                    value = value + (AXIAL_CURVE * drag[f]) * w[f]
                value = weight * value
                for g in range(4):
                    moved = pltpu.roll(value, 96 - 32 * g, axis=1) if g != 3 else value
                    place = 32 * quarter * g + n * 8
                    ghost[f, pl.ds(pl.multiple_of(place, 8), 8), :] = moved
                    ghost[f, pl.ds(pl.multiple_of(turn_cells + place, 8), 8), :] = moved
            return carry

        lax.fori_loop(0, 4 * quarter, slide, 0, unroll=4)
        shift = off_ref[step]
        shift = jnp.where(row == 0, shift, turn_cells - shift)

        def edges(j, carry, step=step, shift=shift):
            which = step % 2
            a = j if step < 2 else (az + spread(j, half)) % az_count
            if step == 2:
                @pl.when(j >= half)
                def _():
                    inside(a, step)

            states, prims = [], []
            for t in range(tiles):
                tile_index = a * 4 + t
                row0 = a * 32 + t * 8
                rows = pl.ds(pl.multiple_of(row0, 8), 8)
                state = []
                for f in range(5):
                    low = pltpu.roll(halo[0, f], 128 - tile_index, axis=1)
                    high = pltpu.roll(halo[1, f], 128 + 31 - tile_index, axis=1)
                    extra = jnp.where(inner == 0, low, jnp.where(inner == 31, high, zero))
                    extra = extra + jnp.where(part == 3, ghost[f, pl.ds(row0 + shift, 8), :], zero)
                    state.append(now[f, rows, :] + extra)
                if step < 2:
                    inv = 1.0 / state[0]
                    vt, vr, vz = state[1] * inv, state[2] * inv, state[3] * inv
                    press = (HEAT_RATIO - 1.0) * (
                        state[4] - 0.5 * (state[1] * vt + state[2] * vr + state[3] * vz))
                    w = [state[0], vt, vr, vz, press * inv]
                    rows_pad = pl.ds(pl.multiple_of(row0 + 8, 8), 8)
                    for f in range(5):
                        now[f, rows, :] = state[f]
                        prim[1 - which, f, rows_pad, :] = w[f]
                    prims.append(w)
                else:
                    states.append(state)
            if step < 2:
                wrap(1 - which, a, prims)
                pack(prims, a, step + 1)
                return carry
            for f in range(5):
                for i in range(2):
                    upper, lower = states[i][f], states[2 + i][f]
                    send2[a, f, 8 * i:8 * i + 8, :] = jnp.where(part < 2, upper, pltpu.roll(lower, 64, axis=1))
                    send2[az_count + a, f, 8 * i:8 * i + 8, :] = jnp.where(
                        part < 2, pltpu.roll(upper, 64, axis=1), lower)
            for x in range(2):
                flat = x * az_count + a

                @pl.when(flat != me)
                def _():
                    second_copy(flat).start()

                @pl.when(flat == me)
                def _():
                    recv2[band] = send2[me]
            return carry

        lax.fori_loop(0, az_count, edges, 0, unroll=1 if step == 2 else 2)

    for col in range(4):
        for sub in range(4):
            from_band = 4 * col + sub
            from_ax, from_az = chip_of(from_band, wide)
            flat = from_ax * az_count + from_az

            @pl.when(flat != me)
            def _():
                pltpu.make_async_remote_copy(
                    src_ref=send2.at[flat],
                    dst_ref=recv2.at[from_band],
                    send_sem=s2.at[flat],
                    recv_sem=r2.at[from_band],
                    device_id=chip_id(flat),
                    device_id_type=PEER,
                ).wait_recv()

        for f in range(5):
            for i in range(2):
                source = [recv2[4 * col + sub, f, 8 * i:8 * i + 8, :] for sub in range(4)]
                for q in range(4):
                    h, k = q // 2, q % 2
                    mixed = None
                    for sub in range(4):
                        turn = (32 * (sub - q)) % 128
                        moved = pltpu.roll(source[sub], turn, axis=1) if turn else source[sub]
                        mixed = moved if mixed is None else jnp.where(part == sub, moved, mixed)
                    out_ref[0, f, k, 16 * h + 8 * i:16 * h + 8 * i + 8, 128 * col:128 * col + 128] = mixed

    for flat in others():
        first_copy(flat).wait_send()
        second_copy(flat).wait_send()


def banded(az_count, density, velocity, pressure, offsets):
    chips = 2 * az_count
    cells = 32 * az_count
    f32 = jnp.float32
    dma = pltpu.SemaphoreType.DMA
    anywhere = pl.BlockSpec(memory_space=pltpu.HBM)
    return pl.pallas_call(
        functools.partial(kernel, az_count),
        out_shape=jax.ShapeDtypeStruct((1, 5) + density.shape[1:], f32),
        in_specs=[anywhere] * 4,
        out_specs=pl.BlockSpec(memory_space=pltpu.VMEM),
        scratch_shapes=[
            pltpu.SMEM(offsets.shape, jnp.int32),
            pltpu.VMEM(density.shape, f32),
            pltpu.VMEM(velocity.shape, f32),
            pltpu.VMEM(pressure.shape, f32),
            pltpu.VMEM((chips, 5, 16, LANES), f32),
            pltpu.VMEM((chips, 5, 16, LANES), f32),
            pltpu.VMEM((chips, 5, 16, LANES), f32),
            pltpu.VMEM((chips, 5, 16, LANES), f32),
            pltpu.VMEM((5, cells, LANES), f32),
            pltpu.VMEM((5, cells, LANES), f32),
            pltpu.VMEM((2, 5, cells + 16, LANES), f32),
            pltpu.VMEM((3, 2, 5, TILE, LANES), f32),
            pltpu.VMEM((3, 2, 5, TILE, LANES), f32),
            pltpu.VMEM((2, 5, TILE, LANES), f32),
            pltpu.VMEM((3, 5, cells // 4, LANES), f32),
            pltpu.VMEM((3, 5, cells // 4, LANES), f32),
            pltpu.VMEM((5, 2 * cells + 8, LANES), f32),
            dma((chips,)), dma((chips,)), dma((chips,)), dma((chips,)),
            dma((3, 2)), dma((3, 2)), dma((3,)), dma((3,)), dma((4,)),
        ],
        compiler_params=pltpu.CompilerParams(
            collective_id=0, has_side_effects=True, vmem_limit_bytes=56 * 2**20
        ),
    )(offsets, density, velocity, pressure)


def whole_step(density, velocity, pressure, offsets):
    ax_count, az_count = lax.axis_size("ax"), lax.axis_size("az")
    if ax_count == 2 and az_count == 8 and density.shape == (1, 2, 32, 512):
        return banded(az_count, density, velocity, pressure, offsets)
    return body(density, velocity, pressure, offsets)


def solution(mesh):
    placed = (
        P("row", "ax", "az", None),
        P("row", None, "ax", "az", None),
        P("row", "ax", "az", None),
        P(),
    )
    return jax.shard_map(
        whole_step,
        mesh=mesh,
        in_specs=placed,
        out_specs=P("row", None, "ax", "az", None),
        check_vma=False,
    )
```

```python
import functools
import math

import jax
import jax.numpy as jnp
from jax import lax
from jax.experimental import pallas as pl
from jax.experimental.pallas import tpu as pltpu
from jax.sharding import PartitionSpec as P

HEAT_RATIO = 1.4
VISCOSITY = 0.8
CONDUCTION = 0.6
TIME_STEP = 0.1
AXIAL_FLUX = 1.0
AXIAL_CURVE = 4.0


def partner_2(value, axis, bit):
    mask = 2**bit
    pairs = [(source, source ^ mask) for source in range(lax.axis_size(axis))]
    return lax.ppermute(value, axis, pairs)


def padded(cells, sides, width, closed):
    for axis, dim in sides:
        count = lax.axis_size(axis)
        ends = count if closed else count - 1
        head = lax.slice_in_dim(cells, 0, width, axis=dim)
        tail = lax.slice_in_dim(cells, cells.shape[dim] - width, cells.shape[dim], axis=dim)
        cells = jnp.concatenate(
            [
                lax.ppermute(tail, axis, [(i, (i + 1) % count) for i in range(ends)]),
                cells,
                lax.ppermute(head, axis, [((i + 1) % count, i) for i in range(ends)]),
            ],
            axis=dim,
        )
    return cells


def conserved(density, velocity, pressure):
    momentum = density[:, None] * velocity
    energy = pressure / (HEAT_RATIO - 1.0) + 0.5 * density * jnp.sum(velocity * velocity, axis=1)
    return jnp.concatenate([density[:, None], momentum, energy[:, None]], axis=1)


def primitive(state):
    vel_theta = state[:, 1] / state[:, 0]
    vel_radial = state[:, 2] / state[:, 0]
    vel_axial = state[:, 3] / state[:, 0]
    press = (HEAT_RATIO - 1.0) * (
        state[:, 4]
        - 0.5 * (state[:, 1] * vel_theta + state[:, 2] * vel_radial + state[:, 3] * vel_axial)
    )
    return (vel_theta, vel_radial, vel_axial, press / state[:, 0], press)


def fluxes(state, values, direction):
    normal_vel = values[direction]
    press = values[4]
    flux_terms = [
        state[:, 0] * normal_vel,
        state[:, 1] * normal_vel,
        state[:, 2] * normal_vel,
        state[:, 3] * normal_vel,
        (state[:, 4] + press) * normal_vel,
    ]
    flux_terms[1 + direction] = flux_terms[1 + direction] + press
    return flux_terms


def extended(state, values_c, lower, upper, axis_pos):
    values_lo = primitive(lower)
    values_hi = primitive(upper)
    ext_state = jnp.concatenate([lower, state, upper], axis=axis_pos)
    ext_values = tuple(
        (
            jnp.concatenate([values_lo[k], values_c[k], values_hi[k]], axis=axis_pos - 1)
            for k in range(5)
        )
    )
    return (ext_state, ext_values)


def side_slices(items, axis_pos):
    size_now = items[0].shape[axis_pos] - 2
    lows = [lax.slice_in_dim(item, 0, size_now, axis=axis_pos) for item in items]
    highs = [lax.slice_in_dim(item, 2, size_now + 2, axis=axis_pos) for item in items]
    return (lows, highs)


def tendency(state, theta_ghosts, radial_ghosts, axial_ghosts, radius, dtheta):
    values_c = primitive(state)
    directions = [(theta_ghosts, 3), (radial_ghosts, 4), (axial_ghosts, 2)]
    flux_lo = []
    flux_hi = []
    value_lo = []
    value_hi = []
    for direction_index in range(3):
        ghosts, axis_pos = directions[direction_index]
        ext_state, ext_values = extended(state, values_c, ghosts[0], ghosts[1], axis_pos)
        flux_all = fluxes(ext_state, ext_values, direction_index)
        lows, highs = side_slices(flux_all, axis_pos - 1)
        flux_lo.append(lows)
        flux_hi.append(highs)
        vlows, vhighs = side_slices(list(ext_values), axis_pos - 1)
        value_lo.append(vlows)
        value_hi.append(vhighs)
    result = []
    for field_index in range(5):
        divergence = -(flux_hi[0][field_index] - flux_lo[0][field_index]) / (2.0 * radius * dtheta)
        divergence = divergence - (
            (radius + 1.0) * flux_hi[1][field_index] - (radius - 1.0) * flux_lo[1][field_index]
        ) / (2.0 * radius)
        divergence = divergence - AXIAL_FLUX * (flux_hi[2][field_index] - flux_lo[2][field_index])
        result.append(divergence)

    def viscous(which):
        center = values_c[which]
        beside_all = (value_hi[0][which] - 2.0 * center + value_lo[0][which]) / (
            radius * dtheta
        ) ** 2
        across = (
            (radius + 0.5) * (value_hi[1][which] - center)
            - (radius - 0.5) * (center - value_lo[1][which])
        ) / radius
        return (
            beside_all
            + across
            + AXIAL_CURVE * (value_hi[2][which] - 2.0 * center + value_lo[2][which])
        )

    density_now = state[:, 0]
    result[1] = (
        result[1]
        - density_now * values_c[0] * values_c[1] / radius
        + VISCOSITY
        * (
            viscous(0)
            - values_c[0] / radius**2
            + (value_hi[0][1] - value_lo[0][1]) / (radius**2 * dtheta)
        )
    )
    result[2] = (
        result[2]
        + (density_now * values_c[0] * values_c[0] + values_c[4]) / radius
        + VISCOSITY
        * (
            viscous(1)
            - values_c[1] / radius**2
            - (value_hi[0][0] - value_lo[0][0]) / (radius**2 * dtheta)
        )
    )
    result[3] = result[3] + VISCOSITY * viscous(2)
    result[4] = result[4] + CONDUCTION * viscous(3)
    return jnp.stack(result, axis=1)


def body(density, velocity, pressure, offsets):
    state0 = conserved(density, velocity, pressure)
    tile_cells = state0.shape[3]
    radial_cells = state0.shape[4]
    cycle_size = lax.axis_size("az")
    cycle_cells = tile_cells * cycle_size
    dtheta = 2.0 * math.pi / cycle_cells
    radius = cycle_cells / (2.0 * math.pi) + jnp.arange(radial_cells, dtype=jnp.float32) + 0.5
    at_outer = lax.axis_index("ax") == 0
    at_plane = lax.axis_index("ax") == lax.axis_size("ax") - 1
    is_rotor = lax.axis_index("row") == 0
    axial_sign = jnp.array([1.0, 1.0, 1.0, -1.0, 1.0], dtype=jnp.float32).reshape(5, 1, 1)
    wall_sign = jnp.array([1.0, -1.0, -1.0, -1.0, 1.0], dtype=jnp.float32).reshape(5, 1, 1, 1)

    def rotate_plane(partner, turn_cells):
        band = lax.all_to_all(partner, "az", split_axis=2, concat_axis=1, tiled=True)
        doubled = jnp.concatenate([band, band], axis=1)
        rolled = lax.dynamic_slice_in_dim(doubled, turn_cells, cycle_cells, 1)
        return lax.all_to_all(rolled, "az", split_axis=1, concat_axis=2, tiled=True)

    def full_rate(state, shift):
        top_plane = state[0, :, -1] * axial_sign
        partner = partner_2(top_plane, "row", 0)
        turn_cells = jnp.where(is_rotor, shift, (cycle_cells - shift) % cycle_cells)
        ghost_plane = rotate_plane(partner, turn_cells)
        cycle_pad = padded(state, (("az", 3),), 1, True)
        theta_lo = cycle_pad[:, :, :, :1]
        theta_hi = cycle_pad[:, :, :, -1:]
        plane_pad = padded(state, (("ax", 2),), 1, False)
        lower_ghost = plane_pad[:, :, :1]
        upper_ghost = plane_pad[:, :, -1:]
        lower_ghost = jnp.where(at_outer, state[:, :, :1], lower_ghost)
        upper_ghost = jnp.where(at_plane, ghost_plane[None, :, None], upper_ghost)
        radial_lo = state[..., :1] * wall_sign
        radial_hi = state[..., -1:] * wall_sign
        return tendency(
            state,
            (theta_lo, theta_hi),
            (radial_lo, radial_hi),
            (lower_ghost, upper_ghost),
            radius,
            dtheta,
        )

    state1 = state0 + TIME_STEP * full_rate(state0, offsets[0])
    state2 = 0.75 * state0 + 0.25 * (state1 + TIME_STEP * full_rate(state1, offsets[1]))
    return state0 / 3.0 + 2.0 / 3.0 * (state2 + TIME_STEP * full_rate(state2, offsets[2]))


LANES = 128
TILE = 8
PEER = pl.DeviceIdType.MESH
RUNGE_KUTTA = ((0.0, 1.0), (0.75, 0.25), (1.0 / 3.0, 2.0 / 3.0))


def band_of(ax, az, wide):
    deep, side = az // 2, az % 2
    column = side + ax * (3 - 2 * side)
    return column * wide + deep + (column % 2) * (wide - 1 - 2 * deep)


def chip_of(band, wide):
    column, step = band // wide, band % wide
    ax = column // 2
    side = (column + ax) % 2
    deep = step + (column % 2) * (wide - 1 - 2 * step)
    return ax, deep * 2 + side


def kernel(
    az_count,
    off_hbm, den_hbm, vel_hbm, pre_hbm, out_ref,
    off_ref, den_ref, vel_ref, pre_ref,
    send1, relay1, recv1, send2, relay2, recv2, base, now, prim, halo_out, halo_in, halo, plane_out, plane_in, ghost,
    sz1, rz1, sf1, r1, sz2, rz2, sf2, r2, sh, rh, sp, rp, s_in,
):
    chips = 2 * az_count
    half = az_count // 2
    wide = az_count // 2
    turn_cells = 32 * az_count
    tiles = 4
    row = lax.axis_index("row")
    ax = lax.axis_index("ax")
    az = lax.axis_index("az")
    level, corner = az // 2, 2 * (az % 2) + ax
    band = band_of(ax, az, wide)

    def place(to_level, to_corner):
        return (row, to_corner % 2, 2 * to_level + to_corner // 2)

    def band_id(which):
        return (row,) + chip_of(which, wide)

    loads = [
        pltpu.make_async_copy(src, dst, s_in.at[n])
        for n, (src, dst) in enumerate((
            (den_hbm, den_ref), (pre_hbm, pre_ref), (vel_hbm, vel_ref), (off_hbm, off_ref)))
    ]
    for load in loads:
        load.start()
    barrier = pltpu.get_barrier_semaphore()
    for i in range(1, wide):
        pl.semaphore_signal(barrier, inc=1, device_id=place((level + i) % wide, corner), device_id_type=PEER)
    for i in range(1, 4):
        pl.semaphore_signal(barrier, inc=1, device_id=place(level, (corner + i) % 4), device_id_type=PEER)
    pl.semaphore_signal(barrier, inc=1, device_id=(1 - row, ax, az), device_id_type=PEER)

    lane = lax.broadcasted_iota(jnp.int32, (TILE, LANES), 1)
    part = lane // 32
    inner = lane % 32

    for load in loads:
        load.wait()

    for f in range(5):
        for i in range(2):
            for col in range(4):
                source = []
                for h in range(2):
                    for k in range(2):
                        rows = pl.ds(16 * h + 8 * i, 8)
                        cols = pl.ds(128 * col, 128)
                        if f == 0:
                            tile = den_ref[0, k, rows, cols]
                        elif f == 4:
                            tile = pre_ref[0, k, rows, cols] / den_ref[0, k, rows, cols]
                        else:
                            tile = vel_ref[0, f - 1, k, rows, cols]
                        source.append(tile)
                for sub in range(4):
                    mixed = None
                    for q in range(4):
                        turn = (32 * (q - sub)) % 128
                        moved = pltpu.roll(source[q], turn, axis=1) if turn else source[q]
                        mixed = moved if mixed is None else jnp.where(part == q, moved, mixed)
                    to_ax, to_az = chip_of(4 * col + sub, wide)
                    send1[2 * to_az + to_ax, f, 8 * i:8 * i + 8, :] = mixed

    pl.semaphore_wait(barrier, wide + 3)

    def remote(src, dst, send_sem, recv_sem, to_level, to_corner):
        return pltpu.make_async_remote_copy(
            src_ref=src, dst_ref=dst, send_sem=send_sem, recv_sem=recv_sem,
            device_id=place(to_level, to_corner), device_id_type=PEER)

    def along1(to):
        return remote(send1.at[pl.ds(4 * to, 4)], relay1.at[level], sz1.at[to], rz1.at[level], to, corner)

    def across1(source, of_level, to):
        return remote(source, recv1.at[4 * of_level + corner], sf1.at[of_level, to],
                      r1.at[4 * of_level + corner], level, to)

    for k in range(1, wide):
        along1((level + wide - k) % wide).start()
    for i in range(1, 4):
        to = (corner + i) % 4
        across1(send1.at[4 * level + to], level, to).start()
    recv1[4 * level + corner] = send1[4 * level + corner]

    dtheta = 2.0 * math.pi / turn_cells
    radius = turn_cells / (2.0 * math.pi) + (band * 32 + inner).astype(jnp.float32) + 0.5
    inverse = 1.0 / radius
    c_turn = inverse * (0.5 / dtheta)
    l_turn = (inverse * (1.0 / dtheta)) * (inverse * (1.0 / dtheta))
    l_mid = 2.0 * l_turn + (2.0 + 2.0 * AXIAL_CURVE)
    inverse2 = inverse * inverse
    c_cross = inverse2 * (VISCOSITY / dtheta)
    r_low = turn_cells / (2.0 * math.pi) + (lane * 0 + band * 32).astype(jnp.float32) + 0.5
    r_high = r_low + 31.0
    edge_c = (0.5 * (r_low - 1.0) / r_low, -0.5 * (r_high + 1.0) / r_high)
    edge_l = ((r_low - 0.5) / r_low, (r_high + 0.5) / r_high)
    zero = jnp.zeros((TILE, LANES), jnp.float32)
    give_next = jnp.where(inner == 31, zero, 0.5 * radius / (radius + 1.0))
    give_last = jnp.where(inner == 0, zero, -0.5 * radius / (radius - 1.0))
    drag_next = jnp.where(inner == 31, zero, (radius + 0.5) / (radius + 1.0))
    drag_last = jnp.where(inner == 0, zero, (radius - 0.5) / (radius - 1.0))

    def pack(tiles_of, a, slot):
        group = a // quarter
        for f in range(5):
            low, high = halo_out[slot, 0, f], halo_out[slot, 1, f]
            for t in range(tiles):
                w, tile_index = tiles_of[t][f], a * 4 + t
                low = jnp.where(inner == tile_index, pltpu.roll(w, tile_index + 97, axis=1), low)
                high = jnp.where(inner == tile_index, pltpu.roll(w, tile_index, axis=1), high)
                moved = pltpu.roll(w, (32 * group + 32) % 128, axis=1)
                rows = pl.ds(pl.multiple_of((a % quarter) * 32 + t * 8, 8), 8)
                plane_out[slot, f, rows, :] = jnp.where(part == group, moved, plane_out[slot, f, rows, :])
            halo_out[slot, 0, f], halo_out[slot, 1, f] = low, high

    def wrap(which, a, tiles_of):
        @pl.when(a == 0)
        def _():
            for f in range(5):
                prim[which, f, turn_cells + 8:turn_cells + 16, :] = tiles_of[0][f]

        @pl.when(a == az_count - 1)
        def _():
            for f in range(5):
                prim[which, f, 0:8, :] = tiles_of[tiles - 1][f]

    def neighbour_copies(slot):
        copies = []
        for side, to in ((0, (band + 1) % chips), (1, (band + chips - 1) % chips)):
            copies.append(pltpu.make_async_remote_copy(
                src_ref=halo_out.at[slot, side],
                dst_ref=halo_in.at[slot, side],
                send_sem=sh.at[slot, side],
                recv_sem=rh.at[slot, side],
                device_id=band_id(to),
                device_id_type=PEER,
            ))
        copies.append(pltpu.make_async_remote_copy(
            src_ref=plane_out.at[slot],
            dst_ref=plane_in.at[slot],
            send_sem=sp.at[slot],
            recv_sem=rp.at[slot],
            device_id=(1 - row, ax, az),
            device_id_type=PEER,
        ))
        return copies

    quarter = az_count // 4
    drag = (0.0, VISCOSITY, VISCOSITY, VISCOSITY, CONDUCTION)

    def flux(w, d):
        rho, vt, vr, vz, temp = w
        m = rho * w[1 + d]
        terms = [m, m * vt, m * vr, m * vz,
                 m * (3.5 * temp + 0.5 * (vt * vt + vr * vr + vz * vz))]
        terms[1 + d] = terms[1 + d] + rho * temp
        return terms

    def inside(a, step):
        which = step % 2
        keep, fresh = RUNGE_KUTTA[step]
        for t in range(tiles):
            row0 = a * 32 + t * 8
            mid = [prim[which, f, pl.ds(pl.multiple_of(row0 + 8, 8), 8), :] for f in range(5)]
            rho, vt, vr, vz, temp = mid
            heat = 3.5 * temp + 0.5 * (vt * vt + vr * vr + vz * vz)
            press = rho * temp
            spin = rho * vt
            total = [
                None,
                -inverse * (spin * vr) - (VISCOSITY * (l_mid + inverse2)) * vt,
                inverse * (spin * vt + press) - (VISCOSITY * (l_mid + inverse2)) * vr,
                -(VISCOSITY * l_mid) * vz,
                -(CONDUCTION * l_mid) * temp,
            ]
            m = rho * vz
            terms = [m, m * vt, m * vr, m * vz + press, m * heat]
            for f in range(5):
                up, down = terms[f], -terms[f]
                if f:
                    worn = (AXIAL_CURVE * drag[f]) * mid[f]
                    up, down = worn + terms[f], worn - terms[f]
                value = (jnp.where(part == 0, up, pltpu.roll(up, 32, axis=1))
                         + jnp.where(part == 3, zero, pltpu.roll(down, 96, axis=1)))
                total[f] = value if total[f] is None else total[f] + value
            m = rho * vr
            terms = [m, m * vt, m * vr + press, m * vz, m * heat]
            for f in range(5):
                out, back = give_next * terms[f], give_last * terms[f]
                if f:
                    worn = drag[f] * mid[f]
                    out, back = out + drag_next * worn, back + drag_last * worn
                total[f] = total[f] + pltpu.roll(out, 1, axis=1) + pltpu.roll(back, 127, axis=1)
            tl = [prim[which, f, pl.ds(row0 + 7, 8), :] for f in range(5)]
            th = [prim[which, f, pl.ds(row0 + 9, 8), :] for f in range(5)]
            ftl, fth = flux(tl, 0), flux(th, 0)
            for f in range(5):
                total[f] = total[f] + c_turn * (ftl[f] - fth[f])
                if f:
                    total[f] = total[f] + (drag[f] * l_turn) * (th[f] + tl[f])
            total[1] = total[1] + c_cross * (th[2] - tl[2])
            total[2] = total[2] - c_cross * (th[1] - tl[1])
            rows = pl.ds(pl.multiple_of(row0, 8), 8)
            for f in range(5):
                value = fresh * now[f, rows, :] + (fresh * TIME_STEP) * total[f]
                if keep:
                    value = value + keep * base[f, rows, :]
                now[f, rows, :] = value

    def unpack(a):
        tiles_of = []
        for t in range(tiles):
            h, i = t // 2, t % 2
            w = []
            for f in range(5):
                c0 = recv1[2 * a, f, 8 * i:8 * i + 8, :]
                c1 = recv1[2 * a + 1, f, 8 * i:8 * i + 8, :]
                if h == 0:
                    w.append(jnp.where(part < 2, c0, pltpu.roll(c1, 64, axis=1)))
                else:
                    w.append(jnp.where(part < 2, pltpu.roll(c0, 64, axis=1), c1))
            rho, vt, vr, vz, temp = w
            rows = pl.ds(pl.multiple_of(a * 32 + t * 8, 8), 8)
            rows_pad = pl.ds(pl.multiple_of(a * 32 + t * 8 + 8, 8), 8)
            state = (rho, rho * vt, rho * vr, rho * vz,
                     rho * (temp / (HEAT_RATIO - 1.0) + 0.5 * (vt * vt + vr * vr + vz * vz)))
            for f in range(5):
                base[f, rows, :] = state[f]
                now[f, rows, :] = state[f]
                prim[0, f, rows_pad, :] = w[f]
            tiles_of.append(w)
        wrap(0, a, tiles_of)
        pack(tiles_of, a, 0)

    def arrive(k, carry):
        @pl.when(k < wide)
        def _():
            of_level = (level + k) % wide
            remote(send1.at[pl.ds(4 * of_level, 4)], relay1.at[of_level], sz1.at[of_level],
                   rz1.at[of_level], of_level, corner).wait_recv()
            for i in range(1, 4):
                to = (corner + i) % 4
                across1(relay1.at[of_level, to], of_level, to).start()
            recv1[4 * of_level + corner] = relay1[of_level, corner]

        for n in range(2):
            j = 2 * (k - 1) + n
            a = (2 * level + j) % az_count
            for x in range(2):
                of_corner = 2 * (a % 2) + x

                @pl.when(of_corner != corner)
                def _():
                    slot = 2 * a + x
                    remote(send1.at[slot], recv1.at[slot], sf1.at[a // 2, of_corner], r1.at[slot],
                           level, of_corner).wait_recv()

            unpack(a)

            @pl.when(j >= 2)
            def _():
                inside((2 * level + j + az_count - 1) % az_count, 0)

        return carry

    lax.fori_loop(1, wide + 1, arrive, 0)

    def along2(a):
        return remote(send2.at[pl.ds(2 * a, 2)], relay2.at[level, pl.ds(2 * (a % 2), 2)], sz2.at[a],
                      rz2.at[level, a % 2], a // 2, corner)

    def across2(source, of_level, to):
        of_band = band_of(ax, 2 * of_level + az % 2, wide)
        return remote(source, recv2.at[of_band], sf2.at[of_level, to], r2.at[of_band], level, to)

    signs = (1.0, -1.0, -1.0, -1.0, 1.0)
    for step in range(3):
        copies = neighbour_copies(step)
        for copy in copies:
            copy.start()
        if step == 0:
            def rest(j, carry):
                inside((2 * level + az_count - 1 + j) % az_count, 0)
                return carry

            lax.fori_loop(0, 2, rest, 0, unroll=2)
        else:
            def sweep(a, carry, step=step):
                inside((2 * level + 2 + a) % az_count, step)
                return carry

            lax.fori_loop(0, az_count if step == 1 else half, sweep, 0, unroll=2)
        for copy in copies:
            copy.wait()
        weight = TIME_STEP * RUNGE_KUTTA[step][1]
        walls = (band == 0, band == chips - 1)
        for side in range(2):
            w = [
                jnp.where(walls[side], signs[f] * halo_out[step, 1 - side, f], halo_in[step, side, f])
                for f in range(5)
            ]
            terms = flux(w, 1)
            for f in range(5):
                value = edge_c[side] * terms[f]
                if f:
                    value = value + drag[f] * edge_l[side] * w[f]
                halo[side, f] = weight * value

        def slide(n, carry, step=step, weight=weight):
            rows = pl.ds(pl.multiple_of(n * 8, 8), 8)
            w = [plane_in[step, f, rows, :] for f in range(5)]
            w[3] = -w[3]
            terms = flux(w, 2)
            for f in range(5):
                value = -terms[f]
                if f:
                    value = value + (AXIAL_CURVE * drag[f]) * w[f]
                value = weight * value
                for g in range(4):
                    moved = pltpu.roll(value, 96 - 32 * g, axis=1) if g != 3 else value
                    place = 32 * quarter * g + n * 8
                    ghost[f, pl.ds(pl.multiple_of(place, 8), 8), :] = moved
                    ghost[f, pl.ds(pl.multiple_of(turn_cells + place, 8), 8), :] = moved
            return carry

        lax.fori_loop(0, 4 * quarter, slide, 0, unroll=4)
        shift = off_ref[step]
        shift = jnp.where(row == 0, shift, turn_cells - shift)

        def edges(j, carry, step=step, shift=shift):
            which = step % 2
            a = j if step < 2 else (2 * level + 2 + j) % az_count
            if step == 2:
                @pl.when(j >= half)
                def _():
                    inside(a, step)

            states, prims = [], []
            for t in range(tiles):
                tile_index = a * 4 + t
                row0 = a * 32 + t * 8
                rows = pl.ds(pl.multiple_of(row0, 8), 8)
                state = []
                for f in range(5):
                    low = pltpu.roll(halo[0, f], 128 - tile_index, axis=1)
                    high = pltpu.roll(halo[1, f], 128 + 31 - tile_index, axis=1)
                    extra = jnp.where(inner == 0, low, jnp.where(inner == 31, high, zero))
                    extra = extra + jnp.where(part == 3, ghost[f, pl.ds(row0 + shift, 8), :], zero)
                    state.append(now[f, rows, :] + extra)
                if step < 2:
                    inv = 1.0 / state[0]
                    vt, vr, vz = state[1] * inv, state[2] * inv, state[3] * inv
                    press = (HEAT_RATIO - 1.0) * (
                        state[4] - 0.5 * (state[1] * vt + state[2] * vr + state[3] * vz))
                    w = [state[0], vt, vr, vz, press * inv]
                    rows_pad = pl.ds(pl.multiple_of(row0 + 8, 8), 8)
                    for f in range(5):
                        now[f, rows, :] = state[f]
                        prim[1 - which, f, rows_pad, :] = w[f]
                    prims.append(w)
                else:
                    states.append(state)
            if step < 2:
                wrap(1 - which, a, prims)
                pack(prims, a, step + 1)
                return carry
            for f in range(5):
                for i in range(2):
                    upper, lower = states[i][f], states[2 + i][f]
                    send2[2 * a, f, 8 * i:8 * i + 8, :] = jnp.where(part < 2, upper, pltpu.roll(lower, 64, axis=1))
                    send2[2 * a + 1, f, 8 * i:8 * i + 8, :] = jnp.where(
                        part < 2, pltpu.roll(upper, 64, axis=1), lower)
            @pl.when(a // 2 != level)
            def _():
                along2(a).start()

            for x in range(2):
                to = 2 * (a % 2) + x

                @pl.when((a // 2 == level) & (to != corner))
                def _():
                    across2(send2.at[2 * a + x], level, to).start()

                @pl.when((a // 2 == level) & (to == corner))
                def _():
                    recv2[band] = send2[2 * a + x]
            return carry

        lax.fori_loop(0, az_count, edges, 0, unroll=1 if step == 2 else 2)

    def pass_on(k, carry):
        of_level = (level + wide - k) % wide
        for n in range(2):
            remote(send2.at[pl.ds(0, 2)], relay2.at[of_level, pl.ds(2 * n, 2)], sz2.at[0],
                   rz2.at[of_level, n], of_level, corner).wait_recv()
            for x in range(2):
                to = 2 * n + x

                @pl.when(to != corner)
                def _():
                    across2(relay2.at[of_level, to], of_level, to).start()

                @pl.when(to == corner)
                def _():
                    recv2[band_of(ax, 2 * of_level + az % 2, wide)] = relay2[of_level, to]

        return carry

    lax.fori_loop(1, wide, pass_on, 0)

    for col in range(4):
        for sub in range(4):
            from_band = 4 * col + sub
            from_ax, from_az = chip_of(from_band, wide)
            of_corner = 2 * (from_az % 2) + from_ax

            @pl.when(of_corner != corner)
            def _():
                remote(send2.at[0], recv2.at[from_band], sf2.at[from_az // 2, of_corner],
                       r2.at[from_band], level, of_corner).wait_recv()

        for f in range(5):
            for i in range(2):
                source = [recv2[4 * col + sub, f, 8 * i:8 * i + 8, :] for sub in range(4)]
                for q in range(4):
                    h, k = q // 2, q % 2
                    mixed = None
                    for sub in range(4):
                        turn = (32 * (sub - q)) % 128
                        moved = pltpu.roll(source[sub], turn, axis=1) if turn else source[sub]
                        mixed = moved if mixed is None else jnp.where(part == sub, moved, mixed)
                    out_ref[0, f, k, 16 * h + 8 * i:16 * h + 8 * i + 8, 128 * col:128 * col + 128] = mixed

    for k in range(1, wide):
        to = (level + k) % wide
        along1(to).wait_send()
        for n in range(2):
            along2(2 * to + n).wait_send()
    for of_level in range(wide):
        for i in range(1, 4):
            to = (corner + i) % 4
            across1(send1.at[0], of_level, to).wait_send()
            across2(send2.at[0], of_level, to).wait_send()


def banded(az_count, density, velocity, pressure, offsets):
    chips = 2 * az_count
    cells = 32 * az_count
    f32 = jnp.float32
    dma = pltpu.SemaphoreType.DMA
    anywhere = pl.BlockSpec(memory_space=pltpu.HBM)
    return pl.pallas_call(
        functools.partial(kernel, az_count),
        out_shape=jax.ShapeDtypeStruct((1, 5) + density.shape[1:], f32),
        in_specs=[anywhere] * 4,
        out_specs=pl.BlockSpec(memory_space=pltpu.VMEM),
        scratch_shapes=[
            pltpu.SMEM(offsets.shape, jnp.int32),
            pltpu.VMEM(density.shape, f32),
            pltpu.VMEM(velocity.shape, f32),
            pltpu.VMEM(pressure.shape, f32),
            pltpu.VMEM((chips, 5, 16, LANES), f32),
            pltpu.VMEM((az_count // 2, 4, 5, 16, LANES), f32),
            pltpu.VMEM((chips, 5, 16, LANES), f32),
            pltpu.VMEM((chips, 5, 16, LANES), f32),
            pltpu.VMEM((az_count // 2, 4, 5, 16, LANES), f32),
            pltpu.VMEM((chips, 5, 16, LANES), f32),
            pltpu.VMEM((5, cells, LANES), f32),
            pltpu.VMEM((5, cells, LANES), f32),
            pltpu.VMEM((2, 5, cells + 16, LANES), f32),
            pltpu.VMEM((3, 2, 5, TILE, LANES), f32),
            pltpu.VMEM((3, 2, 5, TILE, LANES), f32),
            pltpu.VMEM((2, 5, TILE, LANES), f32),
            pltpu.VMEM((3, 5, cells // 4, LANES), f32),
            pltpu.VMEM((3, 5, cells // 4, LANES), f32),
            pltpu.VMEM((5, 2 * cells + 8, LANES), f32),
            dma((4,)), dma((4,)), dma((4, 4)), dma((chips,)),
            dma((az_count,)), dma((4, 2)), dma((4, 4)), dma((chips,)),
            dma((3, 2)), dma((3, 2)), dma((3,)), dma((3,)), dma((4,)),
        ],
        compiler_params=pltpu.CompilerParams(
            collective_id=0, has_side_effects=True, vmem_limit_bytes=56 * 2**20
        ),
    )(offsets, density, velocity, pressure)


def whole_step(density, velocity, pressure, offsets):
    ax_count, az_count = lax.axis_size("ax"), lax.axis_size("az")
    if ax_count == 2 and az_count == 8 and density.shape == (1, 2, 32, 512):
        return banded(az_count, density, velocity, pressure, offsets)
    return body(density, velocity, pressure, offsets)


def solution(mesh):
    placed = (
        P("row", "ax", "az", None),
        P("row", None, "ax", "az", None),
        P("row", "ax", "az", None),
        P(),
    )
    return jax.shard_map(
        whole_step,
        mesh=mesh,
        in_specs=placed,
        out_specs=P("row", None, "ax", "az", None),
        check_vma=False,
    )
```

```python
import functools
import math

import jax
import jax.numpy as jnp
from jax import lax
from jax.experimental import pallas as pl
from jax.experimental.pallas import tpu as pltpu
from jax.sharding import PartitionSpec as P

HEAT_RATIO = 1.4
VISCOSITY = 0.8
CONDUCTION = 0.6
TIME_STEP = 0.1
AXIAL_FLUX = 1.0
AXIAL_CURVE = 4.0


def partner_2(value, axis, bit):
    mask = 2**bit
    pairs = [(source, source ^ mask) for source in range(lax.axis_size(axis))]
    return lax.ppermute(value, axis, pairs)


def padded(cells, sides, width, closed):
    for axis, dim in sides:
        count = lax.axis_size(axis)
        ends = count if closed else count - 1
        head = lax.slice_in_dim(cells, 0, width, axis=dim)
        tail = lax.slice_in_dim(cells, cells.shape[dim] - width, cells.shape[dim], axis=dim)
        cells = jnp.concatenate(
            [
                lax.ppermute(tail, axis, [(i, (i + 1) % count) for i in range(ends)]),
                cells,
                lax.ppermute(head, axis, [((i + 1) % count, i) for i in range(ends)]),
            ],
            axis=dim,
        )
    return cells


def conserved(density, velocity, pressure):
    momentum = density[:, None] * velocity
    energy = pressure / (HEAT_RATIO - 1.0) + 0.5 * density * jnp.sum(velocity * velocity, axis=1)
    return jnp.concatenate([density[:, None], momentum, energy[:, None]], axis=1)


def primitive(state):
    vel_theta = state[:, 1] / state[:, 0]
    vel_radial = state[:, 2] / state[:, 0]
    vel_axial = state[:, 3] / state[:, 0]
    press = (HEAT_RATIO - 1.0) * (
        state[:, 4]
        - 0.5 * (state[:, 1] * vel_theta + state[:, 2] * vel_radial + state[:, 3] * vel_axial)
    )
    return (vel_theta, vel_radial, vel_axial, press / state[:, 0], press)


def fluxes(state, values, direction):
    normal_vel = values[direction]
    press = values[4]
    flux_terms = [
        state[:, 0] * normal_vel,
        state[:, 1] * normal_vel,
        state[:, 2] * normal_vel,
        state[:, 3] * normal_vel,
        (state[:, 4] + press) * normal_vel,
    ]
    flux_terms[1 + direction] = flux_terms[1 + direction] + press
    return flux_terms


def extended(state, values_c, lower, upper, axis_pos):
    values_lo = primitive(lower)
    values_hi = primitive(upper)
    ext_state = jnp.concatenate([lower, state, upper], axis=axis_pos)
    ext_values = tuple(
        (
            jnp.concatenate([values_lo[k], values_c[k], values_hi[k]], axis=axis_pos - 1)
            for k in range(5)
        )
    )
    return (ext_state, ext_values)


def side_slices(items, axis_pos):
    size_now = items[0].shape[axis_pos] - 2
    lows = [lax.slice_in_dim(item, 0, size_now, axis=axis_pos) for item in items]
    highs = [lax.slice_in_dim(item, 2, size_now + 2, axis=axis_pos) for item in items]
    return (lows, highs)


def tendency(state, theta_ghosts, radial_ghosts, axial_ghosts, radius, dtheta):
    values_c = primitive(state)
    directions = [(theta_ghosts, 3), (radial_ghosts, 4), (axial_ghosts, 2)]
    flux_lo = []
    flux_hi = []
    value_lo = []
    value_hi = []
    for direction_index in range(3):
        ghosts, axis_pos = directions[direction_index]
        ext_state, ext_values = extended(state, values_c, ghosts[0], ghosts[1], axis_pos)
        flux_all = fluxes(ext_state, ext_values, direction_index)
        lows, highs = side_slices(flux_all, axis_pos - 1)
        flux_lo.append(lows)
        flux_hi.append(highs)
        vlows, vhighs = side_slices(list(ext_values), axis_pos - 1)
        value_lo.append(vlows)
        value_hi.append(vhighs)
    result = []
    for field_index in range(5):
        divergence = -(flux_hi[0][field_index] - flux_lo[0][field_index]) / (2.0 * radius * dtheta)
        divergence = divergence - (
            (radius + 1.0) * flux_hi[1][field_index] - (radius - 1.0) * flux_lo[1][field_index]
        ) / (2.0 * radius)
        divergence = divergence - AXIAL_FLUX * (flux_hi[2][field_index] - flux_lo[2][field_index])
        result.append(divergence)

    def viscous(which):
        center = values_c[which]
        beside_all = (value_hi[0][which] - 2.0 * center + value_lo[0][which]) / (
            radius * dtheta
        ) ** 2
        across = (
            (radius + 0.5) * (value_hi[1][which] - center)
            - (radius - 0.5) * (center - value_lo[1][which])
        ) / radius
        return (
            beside_all
            + across
            + AXIAL_CURVE * (value_hi[2][which] - 2.0 * center + value_lo[2][which])
        )

    density_now = state[:, 0]
    result[1] = (
        result[1]
        - density_now * values_c[0] * values_c[1] / radius
        + VISCOSITY
        * (
            viscous(0)
            - values_c[0] / radius**2
            + (value_hi[0][1] - value_lo[0][1]) / (radius**2 * dtheta)
        )
    )
    result[2] = (
        result[2]
        + (density_now * values_c[0] * values_c[0] + values_c[4]) / radius
        + VISCOSITY
        * (
            viscous(1)
            - values_c[1] / radius**2
            - (value_hi[0][0] - value_lo[0][0]) / (radius**2 * dtheta)
        )
    )
    result[3] = result[3] + VISCOSITY * viscous(2)
    result[4] = result[4] + CONDUCTION * viscous(3)
    return jnp.stack(result, axis=1)


def body(density, velocity, pressure, offsets):
    state0 = conserved(density, velocity, pressure)
    tile_cells = state0.shape[3]
    radial_cells = state0.shape[4]
    cycle_size = lax.axis_size("az")
    cycle_cells = tile_cells * cycle_size
    dtheta = 2.0 * math.pi / cycle_cells
    radius = cycle_cells / (2.0 * math.pi) + jnp.arange(radial_cells, dtype=jnp.float32) + 0.5
    at_outer = lax.axis_index("ax") == 0
    at_plane = lax.axis_index("ax") == lax.axis_size("ax") - 1
    is_rotor = lax.axis_index("row") == 0
    axial_sign = jnp.array([1.0, 1.0, 1.0, -1.0, 1.0], dtype=jnp.float32).reshape(5, 1, 1)
    wall_sign = jnp.array([1.0, -1.0, -1.0, -1.0, 1.0], dtype=jnp.float32).reshape(5, 1, 1, 1)

    def rotate_plane(partner, turn_cells):
        band = lax.all_to_all(partner, "az", split_axis=2, concat_axis=1, tiled=True)
        doubled = jnp.concatenate([band, band], axis=1)
        rolled = lax.dynamic_slice_in_dim(doubled, turn_cells, cycle_cells, 1)
        return lax.all_to_all(rolled, "az", split_axis=1, concat_axis=2, tiled=True)

    def full_rate(state, shift):
        top_plane = state[0, :, -1] * axial_sign
        partner = partner_2(top_plane, "row", 0)
        turn_cells = jnp.where(is_rotor, shift, (cycle_cells - shift) % cycle_cells)
        ghost_plane = rotate_plane(partner, turn_cells)
        cycle_pad = padded(state, (("az", 3),), 1, True)
        theta_lo = cycle_pad[:, :, :, :1]
        theta_hi = cycle_pad[:, :, :, -1:]
        plane_pad = padded(state, (("ax", 2),), 1, False)
        lower_ghost = plane_pad[:, :, :1]
        upper_ghost = plane_pad[:, :, -1:]
        lower_ghost = jnp.where(at_outer, state[:, :, :1], lower_ghost)
        upper_ghost = jnp.where(at_plane, ghost_plane[None, :, None], upper_ghost)
        radial_lo = state[..., :1] * wall_sign
        radial_hi = state[..., -1:] * wall_sign
        return tendency(
            state,
            (theta_lo, theta_hi),
            (radial_lo, radial_hi),
            (lower_ghost, upper_ghost),
            radius,
            dtheta,
        )

    state1 = state0 + TIME_STEP * full_rate(state0, offsets[0])
    state2 = 0.75 * state0 + 0.25 * (state1 + TIME_STEP * full_rate(state1, offsets[1]))
    return state0 / 3.0 + 2.0 / 3.0 * (state2 + TIME_STEP * full_rate(state2, offsets[2]))


LANES = 128
TILE = 8
PEER = pl.DeviceIdType.MESH
RUNGE_KUTTA = ((0.0, 1.0), (0.75, 0.25), (1.0, 2.0))


def band_of(ax, az, wide):
    deep, side = az // 2, az % 2
    column = side + ax * (3 - 2 * side)
    return column * wide + deep + (column % 2) * (wide - 1 - 2 * deep)


def chip_of(band, wide):
    column, step = band // wide, band % wide
    ax = column // 2
    side = (column + ax) % 2
    deep = step + (column % 2) * (wide - 1 - 2 * step)
    return ax, deep * 2 + side


def spread(j, half):
    return half + (j % 2) * ((j + 1) // 2) - (1 - j % 2) * (j // 2)


def kernel(
    az_count,
    off_hbm, den_hbm, vel_hbm, pre_hbm, out_hbm,
    off_ref, den_ref, vel_ref, pre_ref, out_ref,
    send1, recv1, send2, recv2, base, now, prim, halo_out, halo_in, halo, plane_out, plane_in, ghost,
    s1, r1, s2, r2, sh, rh, sp, rp, s_in, s_out,
):
    chips = 2 * az_count
    half = az_count // 2
    wide = az_count // 2
    turn_cells = 32 * az_count
    tiles = 4
    row = lax.axis_index("row")
    ax = lax.axis_index("ax")
    az = lax.axis_index("az")
    me = ax * az_count + az
    band = band_of(ax, az, wide)

    def chip_id(flat):
        return (row, flat // az_count, flat % az_count)

    def band_id(which):
        return (row,) + chip_of(which, wide)

    loads = [
        pltpu.make_async_copy(src, dst, s_in.at[n])
        for n, (src, dst) in enumerate((
            (den_hbm, den_ref), (pre_hbm, pre_ref), (vel_hbm, vel_ref), (off_hbm, off_ref)))
    ]
    for load in loads:
        load.start()
    barrier = pltpu.get_barrier_semaphore()
    for i in range(1, chips):
        pl.semaphore_signal(barrier, inc=1, device_id=chip_id((me + i) % chips), device_id_type=PEER)
    pl.semaphore_signal(barrier, inc=1, device_id=(1 - row, ax, az), device_id_type=PEER)

    lane = lax.broadcasted_iota(jnp.int32, (TILE, LANES), 1)
    part = lane // 32
    inner = lane % 32

    for load in loads:
        load.wait()

    for f in range(5):
        for i in range(2):
            for col in range(4):
                source = []
                for h in range(2):
                    for k in range(2):
                        rows = pl.ds(16 * h + 8 * i, 8)
                        cols = pl.ds(128 * col, 128)
                        if f == 0:
                            tile = den_ref[0, k, rows, cols]
                        elif f == 4:
                            tile = pre_ref[0, k, rows, cols] / den_ref[0, k, rows, cols]
                        else:
                            tile = vel_ref[0, f - 1, k, rows, cols]
                        source.append(tile)
                for sub in range(4):
                    mixed = None
                    for q in range(4):
                        turn = (32 * (q - sub)) % 128
                        moved = pltpu.roll(source[q], turn, axis=1) if turn else source[q]
                        mixed = moved if mixed is None else jnp.where(part == q, moved, mixed)
                    send1[4 * col + sub, f, 8 * i:8 * i + 8, :] = mixed

    pl.semaphore_wait(barrier, chips)

    def first_copy(flat):
        return pltpu.make_async_remote_copy(
            src_ref=send1.at[band_of(flat // az_count, flat % az_count, wide)],
            dst_ref=recv1.at[me],
            send_sem=s1.at[flat],
            recv_sem=r1.at[me],
            device_id=chip_id(flat),
            device_id_type=PEER,
        )

    def others():
        for j in range(az_count):
            for x in range(2):
                offset = spread(j, half) % az_count
                if offset or x:
                    yield ((ax + x) % 2) * az_count + (az + az_count - offset) % az_count

    for flat in others():
        first_copy(flat).start()
    recv1[me] = send1[band]

    dtheta = 2.0 * math.pi / turn_cells
    radius = turn_cells / (2.0 * math.pi) + (band * 32 + inner).astype(jnp.float32) + 0.5
    inverse = 1.0 / radius
    c_turn = inverse * (0.5 / dtheta)
    l_turn = (inverse * (1.0 / dtheta)) * (inverse * (1.0 / dtheta))
    l_mid = 2.0 * l_turn + (2.0 + 2.0 * AXIAL_CURVE)
    inverse2 = inverse * inverse
    c_cross = inverse2 * (VISCOSITY / dtheta)
    r_low = turn_cells / (2.0 * math.pi) + (lane * 0 + band * 32).astype(jnp.float32) + 0.5
    r_high = r_low + 31.0
    edge_c = (0.5 * (r_low - 1.0) / r_low, -0.5 * (r_high + 1.0) / r_high)
    edge_l = ((r_low - 0.5) / r_low, (r_high + 0.5) / r_high)
    zero = jnp.zeros((TILE, LANES), jnp.float32)
    give_next = jnp.where(inner == 31, zero, 0.5 * radius / (radius + 1.0))
    give_last = jnp.where(inner == 0, zero, -0.5 * radius / (radius - 1.0))
    drag_next = jnp.where(inner == 31, zero, (radius + 0.5) / (radius + 1.0))
    drag_last = jnp.where(inner == 0, zero, (radius - 0.5) / (radius - 1.0))

    def pack(tiles_of, a, slot):
        group = a // quarter
        for f in range(5):
            low, high = halo_out[slot, 0, f], halo_out[slot, 1, f]
            for t in range(tiles):
                w, tile_index = tiles_of[t][f], a * 4 + t
                low = jnp.where(inner == tile_index, pltpu.roll(w, tile_index + 97, axis=1), low)
                high = jnp.where(inner == tile_index, pltpu.roll(w, tile_index, axis=1), high)
                moved = pltpu.roll(w, (32 * group + 32) % 128, axis=1)
                rows = pl.ds(pl.multiple_of((a % quarter) * 32 + t * 8, 8), 8)
                plane_out[slot, f, rows, :] = jnp.where(part == group, moved, plane_out[slot, f, rows, :])
            halo_out[slot, 0, f], halo_out[slot, 1, f] = low, high

    def wrap(which, a, tiles_of):
        @pl.when(a == 0)
        def _():
            for f in range(5):
                prim[which, f, turn_cells + 8:turn_cells + 16, :] = tiles_of[0][f]

        @pl.when(a == az_count - 1)
        def _():
            for f in range(5):
                prim[which, f, 0:8, :] = tiles_of[tiles - 1][f]

    def neighbour_copies(slot):
        copies = []
        for side, to in ((0, (band + 1) % chips), (1, (band + chips - 1) % chips)):
            copies.append(pltpu.make_async_remote_copy(
                src_ref=halo_out.at[slot, side],
                dst_ref=halo_in.at[slot, side],
                send_sem=sh.at[slot, side],
                recv_sem=rh.at[slot, side],
                device_id=band_id(to),
                device_id_type=PEER,
            ))
        copies.append(pltpu.make_async_remote_copy(
            src_ref=plane_out.at[slot],
            dst_ref=plane_in.at[slot],
            send_sem=sp.at[slot],
            recv_sem=rp.at[slot],
            device_id=(1 - row, ax, az),
            device_id_type=PEER,
        ))
        return copies

    quarter = az_count // 4
    drag = (0.0, VISCOSITY, VISCOSITY, VISCOSITY, CONDUCTION)

    def flux(w, d):
        rho, vt, vr, vz, temp = w
        m = rho * w[1 + d]
        terms = [m, m * vt, m * vr, m * vz,
                 m * (3.5 * temp + 0.5 * (vt * vt + vr * vr + vz * vz))]
        terms[1 + d] = terms[1 + d] + rho * temp
        return terms

    def inside(a, step):
        which = step % 2
        keep, fresh = RUNGE_KUTTA[step]
        for t in range(tiles):
            row0 = a * 32 + t * 8
            mid = [prim[which, f, pl.ds(pl.multiple_of(row0 + 8, 8), 8), :] for f in range(5)]
            rho, vt, vr, vz, temp = mid
            heat = 3.5 * temp + 0.5 * (vt * vt + vr * vr + vz * vz)
            press = rho * temp
            spin = rho * vt
            total = [
                None,
                -inverse * (spin * vr) - (VISCOSITY * (l_mid + inverse2)) * vt,
                inverse * (spin * vt + press) - (VISCOSITY * (l_mid + inverse2)) * vr,
                -(VISCOSITY * l_mid) * vz,
                -(CONDUCTION * l_mid) * temp,
            ]
            m = rho * vz
            terms = [m, m * vt, m * vr, m * vz + press, m * heat]
            for f in range(5):
                up, down = terms[f], -terms[f]
                if f:
                    worn = (AXIAL_CURVE * drag[f]) * mid[f]
                    up, down = worn + terms[f], worn - terms[f]
                value = (jnp.where(part == 0, up, pltpu.roll(up, 32, axis=1))
                         + jnp.where(part == 3, zero, pltpu.roll(down, 96, axis=1)))
                total[f] = value if total[f] is None else total[f] + value
            m = rho * vr
            terms = [m, m * vt, m * vr + press, m * vz, m * heat]
            for f in range(5):
                out, back = give_next * terms[f], give_last * terms[f]
                if f:
                    worn = drag[f] * mid[f]
                    out, back = out + drag_next * worn, back + drag_last * worn
                total[f] = total[f] + pltpu.roll(out, 1, axis=1) + pltpu.roll(back, 127, axis=1)
            tl = [prim[which, f, pl.ds(row0 + 7, 8), :] for f in range(5)]
            th = [prim[which, f, pl.ds(row0 + 9, 8), :] for f in range(5)]
            ftl, fth = flux(tl, 0), flux(th, 0)
            for f in range(5):
                total[f] = total[f] + c_turn * (ftl[f] - fth[f])
                if f:
                    total[f] = total[f] + (drag[f] * l_turn) * (th[f] + tl[f])
            total[1] = total[1] + c_cross * (th[2] - tl[2])
            total[2] = total[2] - c_cross * (th[1] - tl[1])
            rows = pl.ds(pl.multiple_of(row0, 8), 8)
            for f in range(5):
                value = fresh * now[f, rows, :] + (fresh * TIME_STEP) * total[f]
                if keep:
                    value = value + keep * base[f, rows, :]
                now[f, rows, :] = value

    def unpack(a):
        tiles_of = []
        for t in range(tiles):
            h, i = t // 2, t % 2
            w = []
            for f in range(5):
                c0 = recv1[a, f, 8 * i:8 * i + 8, :]
                c1 = recv1[az_count + a, f, 8 * i:8 * i + 8, :]
                if h == 0:
                    w.append(jnp.where(part < 2, c0, pltpu.roll(c1, 64, axis=1)))
                else:
                    w.append(jnp.where(part < 2, pltpu.roll(c0, 64, axis=1), c1))
            rho, vt, vr, vz, temp = w
            rows = pl.ds(pl.multiple_of(a * 32 + t * 8, 8), 8)
            rows_pad = pl.ds(pl.multiple_of(a * 32 + t * 8 + 8, 8), 8)
            state = (rho, rho * vt, rho * vr, rho * vz,
                     rho * (temp / (HEAT_RATIO - 1.0) + 0.5 * (vt * vt + vr * vr + vz * vz)))
            for f in range(5):
                base[f, rows, :] = state[f]
                now[f, rows, :] = state[f]
                prim[0, f, rows_pad, :] = w[f]
            tiles_of.append(w)
        wrap(0, a, tiles_of)
        pack(tiles_of, a, 0)

    def arrive(j, carry):
        a = (az + spread(j, half)) % az_count
        for x in range(2):
            flat = x * az_count + a

            @pl.when(flat != me)
            def _():
                pltpu.make_async_remote_copy(
                    src_ref=send1.at[flat],
                    dst_ref=recv1.at[flat],
                    send_sem=s1.at[flat],
                    recv_sem=r1.at[flat],
                    device_id=chip_id(flat),
                    device_id_type=PEER,
                ).wait_recv()

        unpack(a)

        @pl.when(j >= 2)
        def _():
            inside((az + spread(j - 2, half)) % az_count, 0)

        return carry

    lax.fori_loop(0, az_count, arrive, 0)

    def second_copy(flat):
        return pltpu.make_async_remote_copy(
            src_ref=send2.at[flat],
            dst_ref=recv2.at[band],
            send_sem=s2.at[flat],
            recv_sem=r2.at[band],
            device_id=chip_id(flat),
            device_id_type=PEER,
        )

    signs = (1.0, -1.0, -1.0, -1.0, 1.0)
    for step in range(3):
        copies = neighbour_copies(step)
        for copy in copies:
            copy.start()
        if step == 0:
            def rest(j, carry):
                inside((az + spread(j + az_count - 2, half)) % az_count, 0)
                return carry

            lax.fori_loop(0, 2, rest, 0, unroll=2)
        else:
            def sweep(a, carry, step=step):
                inside((az + spread(a, half)) % az_count, step)
                return carry

            lax.fori_loop(0, az_count if step == 1 else half, sweep, 0, unroll=2)
        for copy in copies:
            copy.wait()
        weight = TIME_STEP * RUNGE_KUTTA[step][1]
        walls = (band == 0, band == chips - 1)
        for side in range(2):
            w = [
                jnp.where(walls[side], signs[f] * halo_out[step, 1 - side, f], halo_in[step, side, f])
                for f in range(5)
            ]
            terms = flux(w, 1)
            for f in range(5):
                value = edge_c[side] * terms[f]
                if f:
                    value = value + drag[f] * edge_l[side] * w[f]
                halo[side, f] = weight * value

        def slide(n, carry, step=step, weight=weight):
            rows = pl.ds(pl.multiple_of(n * 8, 8), 8)
            w = [plane_in[step, f, rows, :] for f in range(5)]
            w[3] = -w[3]
            terms = flux(w, 2)
            for f in range(5):
                value = -terms[f]
                if f:
                    value = value + (AXIAL_CURVE * drag[f]) * w[f]
                value = weight * value
                for g in range(4):
                    moved = pltpu.roll(value, 96 - 32 * g, axis=1) if g != 3 else value
                    place = 32 * quarter * g + n * 8
                    ghost[f, pl.ds(pl.multiple_of(place, 8), 8), :] = moved
                    ghost[f, pl.ds(pl.multiple_of(turn_cells + place, 8), 8), :] = moved
            return carry

        lax.fori_loop(0, 4 * quarter, slide, 0, unroll=4)
        shift = off_ref[step]
        shift = jnp.where(row == 0, shift, turn_cells - shift)

        def edges(j, carry, step=step, shift=shift):
            which = step % 2
            a = j if step < 2 else (az + spread(j, half)) % az_count
            if step == 2:
                @pl.when(j >= half)
                def _():
                    inside(a, step)

            states, prims = [], []
            for t in range(tiles):
                tile_index = a * 4 + t
                row0 = a * 32 + t * 8
                rows = pl.ds(pl.multiple_of(row0, 8), 8)
                state = []
                for f in range(5):
                    low = pltpu.roll(halo[0, f], 128 - tile_index, axis=1)
                    high = pltpu.roll(halo[1, f], 128 + 31 - tile_index, axis=1)
                    extra = jnp.where(inner == 0, low, jnp.where(inner == 31, high, zero))
                    extra = extra + jnp.where(part == 3, ghost[f, pl.ds(row0 + shift, 8), :], zero)
                    state.append(now[f, rows, :] + extra)
                if step < 2:
                    inv = 1.0 / state[0]
                    vt, vr, vz = state[1] * inv, state[2] * inv, state[3] * inv
                    press = (HEAT_RATIO - 1.0) * (
                        state[4] - 0.5 * (state[1] * vt + state[2] * vr + state[3] * vz))
                    w = [state[0], vt, vr, vz, press * inv]
                    rows_pad = pl.ds(pl.multiple_of(row0 + 8, 8), 8)
                    for f in range(5):
                        now[f, rows, :] = state[f]
                        prim[1 - which, f, rows_pad, :] = w[f]
                    prims.append(w)
                else:
                    states.append(state)
            if step < 2:
                wrap(1 - which, a, prims)
                pack(prims, a, step + 1)
                return carry
            for f in range(5):
                for i in range(2):
                    upper, lower = states[i][f], states[2 + i][f]
                    send2[a, f, 8 * i:8 * i + 8, :] = jnp.where(part < 2, upper, pltpu.roll(lower, 64, axis=1))
                    send2[az_count + a, f, 8 * i:8 * i + 8, :] = jnp.where(
                        part < 2, pltpu.roll(upper, 64, axis=1), lower)
            for x in range(2):
                flat = x * az_count + a

                @pl.when(flat != me)
                def _():
                    second_copy(flat).start()

                @pl.when(flat == me)
                def _():
                    recv2[band] = send2[me]
            return carry

        lax.fori_loop(0, az_count, edges, 0, unroll=1 if step == 2 else 2)

    stores = []
    for col in range(4):
        for sub in range(4):
            from_band = 4 * col + sub
            from_ax, from_az = chip_of(from_band, wide)
            flat = from_ax * az_count + from_az

            @pl.when(flat != me)
            def _():
                pltpu.make_async_remote_copy(
                    src_ref=send2.at[flat],
                    dst_ref=recv2.at[from_band],
                    send_sem=s2.at[flat],
                    recv_sem=r2.at[from_band],
                    device_id=chip_id(flat),
                    device_id_type=PEER,
                ).wait_recv()

        for f in range(5):
            for i in range(2):
                source = [recv2[4 * col + sub, f, 8 * i:8 * i + 8, :] for sub in range(4)]
                for q in range(4):
                    h, k = q // 2, q % 2
                    mixed = None
                    for sub in range(4):
                        turn = (32 * (sub - q)) % 128
                        moved = pltpu.roll(source[sub], turn, axis=1) if turn else source[sub]
                        mixed = moved if mixed is None else jnp.where(part == sub, moved, mixed)
                    out_ref[col, f, k, 16 * h + 8 * i:16 * h + 8 * i + 8, :] = mixed

        store = pltpu.make_async_copy(
            out_ref.at[col], out_hbm.at[0, :, :, :, pl.ds(128 * col, 128)], s_out.at[col])
        store.start()
        stores.append(store)

    for flat in others():
        first_copy(flat).wait_send()
        second_copy(flat).wait_send()
    for store in stores:
        store.wait()


def banded(az_count, density, velocity, pressure, offsets):
    chips = 2 * az_count
    cells = 32 * az_count
    f32 = jnp.float32
    dma = pltpu.SemaphoreType.DMA
    anywhere = pl.BlockSpec(memory_space=pltpu.HBM)
    return pl.pallas_call(
        functools.partial(kernel, az_count),
        out_shape=jax.ShapeDtypeStruct((1, 5) + density.shape[1:], f32),
        in_specs=[anywhere] * 4,
        out_specs=anywhere,
        scratch_shapes=[
            pltpu.SMEM(offsets.shape, jnp.int32),
            pltpu.VMEM(density.shape, f32),
            pltpu.VMEM(velocity.shape, f32),
            pltpu.VMEM(pressure.shape, f32),
            pltpu.VMEM((4, 5, 2, 32, LANES), f32),
            pltpu.VMEM((chips, 5, 16, LANES), f32),
            pltpu.VMEM((chips, 5, 16, LANES), f32),
            pltpu.VMEM((chips, 5, 16, LANES), f32),
            pltpu.VMEM((chips, 5, 16, LANES), f32),
            pltpu.VMEM((5, cells, LANES), f32),
            pltpu.VMEM((5, cells, LANES), f32),
            pltpu.VMEM((2, 5, cells + 16, LANES), f32),
            pltpu.VMEM((3, 2, 5, TILE, LANES), f32),
            pltpu.VMEM((3, 2, 5, TILE, LANES), f32),
            pltpu.VMEM((2, 5, TILE, LANES), f32),
            pltpu.VMEM((3, 5, cells // 4, LANES), f32),
            pltpu.VMEM((3, 5, cells // 4, LANES), f32),
            pltpu.VMEM((5, 2 * cells + 8, LANES), f32),
            dma((chips,)), dma((chips,)), dma((chips,)), dma((chips,)),
            dma((3, 2)), dma((3, 2)), dma((3,)), dma((3,)), dma((4,)), dma((4,)),
        ],
        compiler_params=pltpu.CompilerParams(
            collective_id=0, has_side_effects=True, vmem_limit_bytes=56 * 2**20
        ),
    )(offsets, density, velocity, pressure)


def whole_step(density, velocity, pressure, offsets):
    ax_count, az_count = lax.axis_size("ax"), lax.axis_size("az")
    if ax_count == 2 and az_count == 8 and density.shape == (1, 2, 32, 512):
        return banded(az_count, density, velocity, pressure, offsets) * (1.0 / 3.0)
    return body(density, velocity, pressure, offsets)


def solution(mesh):
    placed = (
        P("row", "ax", "az", None),
        P("row", None, "ax", "az", None),
        P("row", "ax", "az", None),
        P(),
    )
    return jax.shard_map(
        whole_step,
        mesh=mesh,
        in_specs=placed,
        out_specs=P("row", None, "ax", "az", None),
        check_vma=False,
    )
```

```python
import functools
import math

import jax
import jax.numpy as jnp
from jax import lax
from jax.experimental import pallas as pl
from jax.experimental.pallas import tpu as pltpu
from jax.sharding import PartitionSpec as P

HEAT_RATIO = 1.4
VISCOSITY = 0.8
CONDUCTION = 0.6
TIME_STEP = 0.1
AXIAL_FLUX = 1.0
AXIAL_CURVE = 4.0


def partner_2(value, axis, bit):
    mask = 2**bit
    pairs = [(source, source ^ mask) for source in range(lax.axis_size(axis))]
    return lax.ppermute(value, axis, pairs)


def padded(cells, sides, width, closed):
    for axis, dim in sides:
        count = lax.axis_size(axis)
        ends = count if closed else count - 1
        head = lax.slice_in_dim(cells, 0, width, axis=dim)
        tail = lax.slice_in_dim(cells, cells.shape[dim] - width, cells.shape[dim], axis=dim)
        cells = jnp.concatenate(
            [
                lax.ppermute(tail, axis, [(i, (i + 1) % count) for i in range(ends)]),
                cells,
                lax.ppermute(head, axis, [((i + 1) % count, i) for i in range(ends)]),
            ],
            axis=dim,
        )
    return cells


def conserved(density, velocity, pressure):
    momentum = density[:, None] * velocity
    energy = pressure / (HEAT_RATIO - 1.0) + 0.5 * density * jnp.sum(velocity * velocity, axis=1)
    return jnp.concatenate([density[:, None], momentum, energy[:, None]], axis=1)


def primitive(state):
    vel_theta = state[:, 1] / state[:, 0]
    vel_radial = state[:, 2] / state[:, 0]
    vel_axial = state[:, 3] / state[:, 0]
    press = (HEAT_RATIO - 1.0) * (
        state[:, 4]
        - 0.5 * (state[:, 1] * vel_theta + state[:, 2] * vel_radial + state[:, 3] * vel_axial)
    )
    return (vel_theta, vel_radial, vel_axial, press / state[:, 0], press)


def fluxes(state, values, direction):
    normal_vel = values[direction]
    press = values[4]
    flux_terms = [
        state[:, 0] * normal_vel,
        state[:, 1] * normal_vel,
        state[:, 2] * normal_vel,
        state[:, 3] * normal_vel,
        (state[:, 4] + press) * normal_vel,
    ]
    flux_terms[1 + direction] = flux_terms[1 + direction] + press
    return flux_terms


def extended(state, values_c, lower, upper, axis_pos):
    values_lo = primitive(lower)
    values_hi = primitive(upper)
    ext_state = jnp.concatenate([lower, state, upper], axis=axis_pos)
    ext_values = tuple(
        (
            jnp.concatenate([values_lo[k], values_c[k], values_hi[k]], axis=axis_pos - 1)
            for k in range(5)
        )
    )
    return (ext_state, ext_values)


def side_slices(items, axis_pos):
    size_now = items[0].shape[axis_pos] - 2
    lows = [lax.slice_in_dim(item, 0, size_now, axis=axis_pos) for item in items]
    highs = [lax.slice_in_dim(item, 2, size_now + 2, axis=axis_pos) for item in items]
    return (lows, highs)


def tendency(state, theta_ghosts, radial_ghosts, axial_ghosts, radius, dtheta):
    values_c = primitive(state)
    directions = [(theta_ghosts, 3), (radial_ghosts, 4), (axial_ghosts, 2)]
    flux_lo = []
    flux_hi = []
    value_lo = []
    value_hi = []
    for direction_index in range(3):
        ghosts, axis_pos = directions[direction_index]
        ext_state, ext_values = extended(state, values_c, ghosts[0], ghosts[1], axis_pos)
        flux_all = fluxes(ext_state, ext_values, direction_index)
        lows, highs = side_slices(flux_all, axis_pos - 1)
        flux_lo.append(lows)
        flux_hi.append(highs)
        vlows, vhighs = side_slices(list(ext_values), axis_pos - 1)
        value_lo.append(vlows)
        value_hi.append(vhighs)
    result = []
    for field_index in range(5):
        divergence = -(flux_hi[0][field_index] - flux_lo[0][field_index]) / (2.0 * radius * dtheta)
        divergence = divergence - (
            (radius + 1.0) * flux_hi[1][field_index] - (radius - 1.0) * flux_lo[1][field_index]
        ) / (2.0 * radius)
        divergence = divergence - AXIAL_FLUX * (flux_hi[2][field_index] - flux_lo[2][field_index])
        result.append(divergence)

    def viscous(which):
        center = values_c[which]
        beside_all = (value_hi[0][which] - 2.0 * center + value_lo[0][which]) / (
            radius * dtheta
        ) ** 2
        across = (
            (radius + 0.5) * (value_hi[1][which] - center)
            - (radius - 0.5) * (center - value_lo[1][which])
        ) / radius
        return (
            beside_all
            + across
            + AXIAL_CURVE * (value_hi[2][which] - 2.0 * center + value_lo[2][which])
        )

    density_now = state[:, 0]
    result[1] = (
        result[1]
        - density_now * values_c[0] * values_c[1] / radius
        + VISCOSITY
        * (
            viscous(0)
            - values_c[0] / radius**2
            + (value_hi[0][1] - value_lo[0][1]) / (radius**2 * dtheta)
        )
    )
    result[2] = (
        result[2]
        + (density_now * values_c[0] * values_c[0] + values_c[4]) / radius
        + VISCOSITY
        * (
            viscous(1)
            - values_c[1] / radius**2
            - (value_hi[0][0] - value_lo[0][0]) / (radius**2 * dtheta)
        )
    )
    result[3] = result[3] + VISCOSITY * viscous(2)
    result[4] = result[4] + CONDUCTION * viscous(3)
    return jnp.stack(result, axis=1)


def body(density, velocity, pressure, offsets):
    state0 = conserved(density, velocity, pressure)
    tile_cells = state0.shape[3]
    radial_cells = state0.shape[4]
    cycle_size = lax.axis_size("az")
    cycle_cells = tile_cells * cycle_size
    dtheta = 2.0 * math.pi / cycle_cells
    radius = cycle_cells / (2.0 * math.pi) + jnp.arange(radial_cells, dtype=jnp.float32) + 0.5
    at_outer = lax.axis_index("ax") == 0
    at_plane = lax.axis_index("ax") == lax.axis_size("ax") - 1
    is_rotor = lax.axis_index("row") == 0
    axial_sign = jnp.array([1.0, 1.0, 1.0, -1.0, 1.0], dtype=jnp.float32).reshape(5, 1, 1)
    wall_sign = jnp.array([1.0, -1.0, -1.0, -1.0, 1.0], dtype=jnp.float32).reshape(5, 1, 1, 1)

    def rotate_plane(partner, turn_cells):
        band = lax.all_to_all(partner, "az", split_axis=2, concat_axis=1, tiled=True)
        doubled = jnp.concatenate([band, band], axis=1)
        rolled = lax.dynamic_slice_in_dim(doubled, turn_cells, cycle_cells, 1)
        return lax.all_to_all(rolled, "az", split_axis=1, concat_axis=2, tiled=True)

    def full_rate(state, shift):
        top_plane = state[0, :, -1] * axial_sign
        partner = partner_2(top_plane, "row", 0)
        turn_cells = jnp.where(is_rotor, shift, (cycle_cells - shift) % cycle_cells)
        ghost_plane = rotate_plane(partner, turn_cells)
        cycle_pad = padded(state, (("az", 3),), 1, True)
        theta_lo = cycle_pad[:, :, :, :1]
        theta_hi = cycle_pad[:, :, :, -1:]
        plane_pad = padded(state, (("ax", 2),), 1, False)
        lower_ghost = plane_pad[:, :, :1]
        upper_ghost = plane_pad[:, :, -1:]
        lower_ghost = jnp.where(at_outer, state[:, :, :1], lower_ghost)
        upper_ghost = jnp.where(at_plane, ghost_plane[None, :, None], upper_ghost)
        radial_lo = state[..., :1] * wall_sign
        radial_hi = state[..., -1:] * wall_sign
        return tendency(
            state,
            (theta_lo, theta_hi),
            (radial_lo, radial_hi),
            (lower_ghost, upper_ghost),
            radius,
            dtheta,
        )

    state1 = state0 + TIME_STEP * full_rate(state0, offsets[0])
    state2 = 0.75 * state0 + 0.25 * (state1 + TIME_STEP * full_rate(state1, offsets[1]))
    return state0 / 3.0 + 2.0 / 3.0 * (state2 + TIME_STEP * full_rate(state2, offsets[2]))


LANES = 128
TILE = 8
PEER = pl.DeviceIdType.MESH
RUNGE_KUTTA = ((0.0, 1.0), (0.75, 0.25), (1.0, 2.0))


def band_of(ax, az, wide):
    deep, side = az // 2, az % 2
    column = side + ax * (3 - 2 * side)
    return column * wide + deep + (column % 2) * (wide - 1 - 2 * deep)


def chip_of(band, wide):
    column, step = band // wide, band % wide
    ax = column // 2
    side = (column + ax) % 2
    deep = step + (column % 2) * (wide - 1 - 2 * step)
    return ax, deep * 2 + side


def spread(j, half):
    return half + (j % 2) * ((j + 1) // 2) - (1 - j % 2) * (j // 2)


def kernel(
    az_count,
    off_hbm, den_hbm, vel_hbm, pre_hbm, out_hbm,
    off_ref, den_ref, vel_ref, pre_ref, out_ref,
    send1, recv1, send2, recv2, base, now, prim, halo_out, halo_in, halo, plane_out, plane_in, ghost,
    s1, r1, s2, r2, sh, rh, sp, rp, s_in, s_out,
):
    chips = 2 * az_count
    half = az_count // 2
    wide = az_count // 2
    turn_cells = 32 * az_count
    tiles = 4
    row = lax.axis_index("row")
    ax = lax.axis_index("ax")
    az = lax.axis_index("az")
    me = ax * az_count + az
    band = band_of(ax, az, wide)

    def chip_id(flat):
        return (row, flat // az_count, flat % az_count)

    def band_id(which):
        return (row,) + chip_of(which, wide)

    loads = [
        pltpu.make_async_copy(src, dst, s_in.at[n])
        for n, (src, dst) in enumerate((
            (den_hbm, den_ref), (pre_hbm, pre_ref), (vel_hbm, vel_ref), (off_hbm, off_ref)))
    ]
    for load in loads:
        load.start()
    barrier = pltpu.get_barrier_semaphore()
    for i in range(1, chips):
        pl.semaphore_signal(barrier, inc=1, device_id=chip_id((me + i) % chips), device_id_type=PEER)
    pl.semaphore_signal(barrier, inc=1, device_id=(1 - row, ax, az), device_id_type=PEER)

    lane = lax.broadcasted_iota(jnp.int32, (TILE, LANES), 1)
    part = lane // 32
    inner = lane % 32

    for load in loads:
        load.wait()

    for f in range(5):
        for i in range(2):
            for col in range(4):
                source = []
                for h in range(2):
                    for k in range(2):
                        rows = pl.ds(16 * h + 8 * i, 8)
                        cols = pl.ds(128 * col, 128)
                        if f == 0:
                            tile = den_ref[0, k, rows, cols]
                        elif f == 4:
                            tile = pre_ref[0, k, rows, cols] / den_ref[0, k, rows, cols]
                        else:
                            tile = vel_ref[0, f - 1, k, rows, cols]
                        source.append(tile)
                for sub in range(4):
                    mixed = None
                    for q in range(4):
                        turn = (32 * (q - sub)) % 128
                        moved = pltpu.roll(source[q], turn, axis=1) if turn else source[q]
                        mixed = moved if mixed is None else jnp.where(part == q, moved, mixed)
                    send1[4 * col + sub, f, 8 * i:8 * i + 8, :] = mixed

    pl.semaphore_wait(barrier, chips)

    def first_copy(flat):
        return pltpu.make_async_remote_copy(
            src_ref=send1.at[band_of(flat // az_count, flat % az_count, wide)],
            dst_ref=recv1.at[me],
            send_sem=s1.at[flat],
            recv_sem=r1.at[me],
            device_id=chip_id(flat),
            device_id_type=PEER,
        )

    def others():
        for j in range(az_count):
            for x in range(2):
                offset = spread(j, half) % az_count
                if offset or x:
                    yield ((ax + x) % 2) * az_count + (az + az_count - offset) % az_count

    for flat in others():
        first_copy(flat).start()
    recv1[me] = send1[band]

    dtheta = 2.0 * math.pi / turn_cells
    radius = turn_cells / (2.0 * math.pi) + (band * 32 + inner).astype(jnp.float32) + 0.5
    inverse = 1.0 / radius
    c_turn = inverse * (0.5 / dtheta)
    l_turn = (inverse * (1.0 / dtheta)) * (inverse * (1.0 / dtheta))
    l_mid = 2.0 * l_turn + (2.0 + 2.0 * AXIAL_CURVE)
    inverse2 = inverse * inverse
    c_cross = inverse2 * (VISCOSITY / dtheta)
    r_low = turn_cells / (2.0 * math.pi) + (lane * 0 + band * 32).astype(jnp.float32) + 0.5
    r_high = r_low + 31.0
    edge_c = (0.5 * (r_low - 1.0) / r_low, -0.5 * (r_high + 1.0) / r_high)
    edge_l = ((r_low - 0.5) / r_low, (r_high + 0.5) / r_high)
    zero = jnp.zeros((TILE, LANES), jnp.float32)
    give_next = jnp.where(inner == 31, zero, 0.5 * radius / (radius + 1.0))
    give_last = jnp.where(inner == 0, zero, -0.5 * radius / (radius - 1.0))
    drag_next = jnp.where(inner == 31, zero, (radius + 0.5) / (radius + 1.0))
    drag_last = jnp.where(inner == 0, zero, (radius - 0.5) / (radius - 1.0))

    def pack(tiles_of, a, slot):
        group = a // quarter
        for f in range(5):
            low, high = halo_out[slot, 0, f], halo_out[slot, 1, f]
            for t in range(tiles):
                w, tile_index = tiles_of[t][f], a * 4 + t
                low = jnp.where(inner == tile_index, pltpu.roll(w, tile_index + 97, axis=1), low)
                high = jnp.where(inner == tile_index, pltpu.roll(w, tile_index, axis=1), high)
                moved = pltpu.roll(w, (32 * group + 32) % 128, axis=1)
                rows = pl.ds(pl.multiple_of((a % quarter) * 32 + t * 8, 8), 8)
                plane_out[slot, f, rows, :] = jnp.where(part == group, moved, plane_out[slot, f, rows, :])
            halo_out[slot, 0, f], halo_out[slot, 1, f] = low, high

    def wrap(which, a, tiles_of):
        @pl.when(a == 0)
        def _():
            for f in range(5):
                prim[which, f, turn_cells + 8:turn_cells + 16, :] = tiles_of[0][f]

        @pl.when(a == az_count - 1)
        def _():
            for f in range(5):
                prim[which, f, 0:8, :] = tiles_of[tiles - 1][f]

    def neighbour_copies(slot):
        copies = []
        for side, to in ((0, (band + 1) % chips), (1, (band + chips - 1) % chips)):
            copies.append(pltpu.make_async_remote_copy(
                src_ref=halo_out.at[slot, side],
                dst_ref=halo_in.at[slot, side],
                send_sem=sh.at[slot, side],
                recv_sem=rh.at[slot, side],
                device_id=band_id(to),
                device_id_type=PEER,
            ))
        copies.append(pltpu.make_async_remote_copy(
            src_ref=plane_out.at[slot],
            dst_ref=plane_in.at[slot],
            send_sem=sp.at[slot],
            recv_sem=rp.at[slot],
            device_id=(1 - row, ax, az),
            device_id_type=PEER,
        ))
        return copies

    quarter = az_count // 4
    drag = (0.0, VISCOSITY, VISCOSITY, VISCOSITY, CONDUCTION)

    def flux(w, d):
        rho, vt, vr, vz, temp = w
        m = rho * w[1 + d]
        terms = [m, m * vt, m * vr, m * vz,
                 m * (3.5 * temp + 0.5 * (vt * vt + vr * vr + vz * vz))]
        terms[1 + d] = terms[1 + d] + rho * temp
        return terms

    def inside(a, step):
        which = step % 2
        keep, fresh = RUNGE_KUTTA[step]
        for t in range(tiles):
            row0 = a * 32 + t * 8
            mid = [prim[which, f, pl.ds(pl.multiple_of(row0 + 8, 8), 8), :] for f in range(5)]
            rho, vt, vr, vz, temp = mid
            heat = 3.5 * temp + 0.5 * (vt * vt + vr * vr + vz * vz)
            press = rho * temp
            spin = rho * vt
            total = [
                None,
                -inverse * (spin * vr) - (VISCOSITY * (l_mid + inverse2)) * vt,
                inverse * (spin * vt + press) - (VISCOSITY * (l_mid + inverse2)) * vr,
                -(VISCOSITY * l_mid) * vz,
                -(CONDUCTION * l_mid) * temp,
            ]
            m = rho * vz
            terms = [m, m * vt, m * vr, m * vz + press, m * heat]
            for f in range(5):
                up, down = terms[f], -terms[f]
                if f:
                    worn = (AXIAL_CURVE * drag[f]) * mid[f]
                    up, down = worn + terms[f], worn - terms[f]
                value = (jnp.where(part == 0, up, pltpu.roll(up, 32, axis=1))
                         + jnp.where(part == 3, zero, pltpu.roll(down, 96, axis=1)))
                total[f] = value if total[f] is None else total[f] + value
            m = rho * vr
            terms = [m, m * vt, m * vr + press, m * vz, m * heat]
            for f in range(5):
                out, back = give_next * terms[f], give_last * terms[f]
                if f:
                    worn = drag[f] * mid[f]
                    out, back = out + drag_next * worn, back + drag_last * worn
                total[f] = total[f] + pltpu.roll(out, 1, axis=1) + pltpu.roll(back, 127, axis=1)
            tl = [prim[which, f, pl.ds(row0 + 7, 8), :] for f in range(5)]
            th = [prim[which, f, pl.ds(row0 + 9, 8), :] for f in range(5)]
            ftl, fth = flux(tl, 0), flux(th, 0)
            for f in range(5):
                total[f] = total[f] + c_turn * (ftl[f] - fth[f])
                if f:
                    total[f] = total[f] + (drag[f] * l_turn) * (th[f] + tl[f])
            total[1] = total[1] + c_cross * (th[2] - tl[2])
            total[2] = total[2] - c_cross * (th[1] - tl[1])
            rows = pl.ds(pl.multiple_of(row0, 8), 8)
            for f in range(5):
                value = fresh * now[f, rows, :] + (fresh * TIME_STEP) * total[f]
                if keep:
                    value = value + keep * base[f, rows, :]
                now[f, rows, :] = value

    def unpack(a):
        tiles_of = []
        for t in range(tiles):
            h, i = t // 2, t % 2
            w = []
            for f in range(5):
                c0 = recv1[a, f, 8 * i:8 * i + 8, :]
                c1 = recv1[az_count + a, f, 8 * i:8 * i + 8, :]
                if h == 0:
                    w.append(jnp.where(part < 2, c0, pltpu.roll(c1, 64, axis=1)))
                else:
                    w.append(jnp.where(part < 2, pltpu.roll(c0, 64, axis=1), c1))
            rho, vt, vr, vz, temp = w
            rows = pl.ds(pl.multiple_of(a * 32 + t * 8, 8), 8)
            rows_pad = pl.ds(pl.multiple_of(a * 32 + t * 8 + 8, 8), 8)
            state = (rho, rho * vt, rho * vr, rho * vz,
                     rho * (temp / (HEAT_RATIO - 1.0) + 0.5 * (vt * vt + vr * vr + vz * vz)))
            for f in range(5):
                base[f, rows, :] = state[f]
                now[f, rows, :] = state[f]
                prim[0, f, rows_pad, :] = w[f]
            tiles_of.append(w)
        wrap(0, a, tiles_of)
        pack(tiles_of, a, 0)

    def arrive(j, carry):
        a = (az + spread(j, az_count)) % az_count
        for x in range(2):
            flat = x * az_count + a

            @pl.when(flat != me)
            def _():
                pltpu.make_async_remote_copy(
                    src_ref=send1.at[flat],
                    dst_ref=recv1.at[flat],
                    send_sem=s1.at[flat],
                    recv_sem=r1.at[flat],
                    device_id=chip_id(flat),
                    device_id_type=PEER,
                ).wait_recv()

        unpack(a)

        @pl.when(j >= 2)
        def _():
            inside((az + spread(j - 2, az_count)) % az_count, 0)

        return carry

    lax.fori_loop(0, az_count, arrive, 0)

    def second_copy(flat):
        return pltpu.make_async_remote_copy(
            src_ref=send2.at[flat],
            dst_ref=recv2.at[band],
            send_sem=s2.at[flat],
            recv_sem=r2.at[band],
            device_id=chip_id(flat),
            device_id_type=PEER,
        )

    signs = (1.0, -1.0, -1.0, -1.0, 1.0)
    for step in range(3):
        copies = neighbour_copies(step)
        for copy in copies:
            copy.start()
        if step == 0:
            def rest(j, carry):
                inside((az + spread(j + az_count - 2, az_count)) % az_count, 0)
                return carry

            lax.fori_loop(0, 2, rest, 0, unroll=2)
        else:
            def sweep(a, carry, step=step):
                inside((az + spread(a, half)) % az_count, step)
                return carry

            lax.fori_loop(0, az_count if step == 1 else az_count - 2, sweep, 0, unroll=2)
        for copy in copies:
            copy.wait()
        weight = TIME_STEP * RUNGE_KUTTA[step][1]
        walls = (band == 0, band == chips - 1)
        for side in range(2):
            w = [
                jnp.where(walls[side], signs[f] * halo_out[step, 1 - side, f], halo_in[step, side, f])
                for f in range(5)
            ]
            terms = flux(w, 1)
            for f in range(5):
                value = edge_c[side] * terms[f]
                if f:
                    value = value + drag[f] * edge_l[side] * w[f]
                halo[side, f] = weight * value

        def slide(n, carry, step=step, weight=weight):
            rows = pl.ds(pl.multiple_of(n * 8, 8), 8)
            w = [plane_in[step, f, rows, :] for f in range(5)]
            w[3] = -w[3]
            terms = flux(w, 2)
            for f in range(5):
                value = -terms[f]
                if f:
                    value = value + (AXIAL_CURVE * drag[f]) * w[f]
                value = weight * value
                for g in range(4):
                    moved = pltpu.roll(value, 96 - 32 * g, axis=1) if g != 3 else value
                    place = 32 * quarter * g + n * 8
                    ghost[f, pl.ds(pl.multiple_of(place, 8), 8), :] = moved
                    ghost[f, pl.ds(pl.multiple_of(turn_cells + place, 8), 8), :] = moved
            return carry

        lax.fori_loop(0, 4 * quarter, slide, 0, unroll=4)
        shift = off_ref[step]
        shift = jnp.where(row == 0, shift, turn_cells - shift)

        def edges(j, carry, step=step, shift=shift):
            which = step % 2
            a = j if step < 2 else (az + spread(j, half)) % az_count
            if step == 2:
                @pl.when(j >= az_count - 2)
                def _():
                    inside(a, step)

            states, prims = [], []
            for t in range(tiles):
                tile_index = a * 4 + t
                row0 = a * 32 + t * 8
                rows = pl.ds(pl.multiple_of(row0, 8), 8)
                state = []
                for f in range(5):
                    low = pltpu.roll(halo[0, f], 128 - tile_index, axis=1)
                    high = pltpu.roll(halo[1, f], 128 + 31 - tile_index, axis=1)
                    extra = jnp.where(inner == 0, low, jnp.where(inner == 31, high, zero))
                    extra = extra + jnp.where(part == 3, ghost[f, pl.ds(row0 + shift, 8), :], zero)
                    state.append(now[f, rows, :] + extra)
                if step < 2:
                    inv = 1.0 / state[0]
                    vt, vr, vz = state[1] * inv, state[2] * inv, state[3] * inv
                    press = (HEAT_RATIO - 1.0) * (
                        state[4] - 0.5 * (state[1] * vt + state[2] * vr + state[3] * vz))
                    w = [state[0], vt, vr, vz, press * inv]
                    rows_pad = pl.ds(pl.multiple_of(row0 + 8, 8), 8)
                    for f in range(5):
                        now[f, rows, :] = state[f]
                        prim[1 - which, f, rows_pad, :] = w[f]
                    prims.append(w)
                else:
                    states.append(state)
            if step < 2:
                wrap(1 - which, a, prims)
                pack(prims, a, step + 1)
                return carry
            for f in range(5):
                for i in range(2):
                    upper, lower = states[i][f], states[2 + i][f]
                    send2[a, f, 8 * i:8 * i + 8, :] = jnp.where(part < 2, upper, pltpu.roll(lower, 64, axis=1))
                    send2[az_count + a, f, 8 * i:8 * i + 8, :] = jnp.where(
                        part < 2, pltpu.roll(upper, 64, axis=1), lower)
            for x in range(2):
                flat = x * az_count + a

                @pl.when(flat != me)
                def _():
                    second_copy(flat).start()

                @pl.when(flat == me)
                def _():
                    recv2[band] = send2[me]
            return carry

        lax.fori_loop(0, az_count, edges, 0, unroll=1 if step == 2 else 2)

    stores = []
    for col in range(4):
        for sub in range(4):
            from_band = 4 * col + sub
            from_ax, from_az = chip_of(from_band, wide)
            flat = from_ax * az_count + from_az

            @pl.when(flat != me)
            def _():
                pltpu.make_async_remote_copy(
                    src_ref=send2.at[flat],
                    dst_ref=recv2.at[from_band],
                    send_sem=s2.at[flat],
                    recv_sem=r2.at[from_band],
                    device_id=chip_id(flat),
                    device_id_type=PEER,
                ).wait_recv()

        for f in range(5):
            for i in range(2):
                source = [recv2[4 * col + sub, f, 8 * i:8 * i + 8, :] for sub in range(4)]
                for q in range(4):
                    h, k = q // 2, q % 2
                    mixed = None
                    for sub in range(4):
                        turn = (32 * (sub - q)) % 128
                        moved = pltpu.roll(source[sub], turn, axis=1) if turn else source[sub]
                        mixed = moved if mixed is None else jnp.where(part == sub, moved, mixed)
                    out_ref[col, f, k, 16 * h + 8 * i:16 * h + 8 * i + 8, :] = mixed

        store = pltpu.make_async_copy(
            out_ref.at[col], out_hbm.at[0, :, :, :, pl.ds(128 * col, 128)], s_out.at[col])
        store.start()
        stores.append(store)

    for flat in others():
        first_copy(flat).wait_send()
        second_copy(flat).wait_send()
    for store in stores:
        store.wait()


def banded(az_count, density, velocity, pressure, offsets):
    chips = 2 * az_count
    cells = 32 * az_count
    f32 = jnp.float32
    dma = pltpu.SemaphoreType.DMA
    anywhere = pl.BlockSpec(memory_space=pltpu.HBM)
    return pl.pallas_call(
        functools.partial(kernel, az_count),
        out_shape=jax.ShapeDtypeStruct((1, 5) + density.shape[1:], f32),
        in_specs=[anywhere] * 4,
        out_specs=anywhere,
        scratch_shapes=[
            pltpu.SMEM(offsets.shape, jnp.int32),
            pltpu.VMEM(density.shape, f32),
            pltpu.VMEM(velocity.shape, f32),
            pltpu.VMEM(pressure.shape, f32),
            pltpu.VMEM((4, 5, 2, 32, LANES), f32),
            pltpu.VMEM((chips, 5, 16, LANES), f32),
            pltpu.VMEM((chips, 5, 16, LANES), f32),
            pltpu.VMEM((chips, 5, 16, LANES), f32),
            pltpu.VMEM((chips, 5, 16, LANES), f32),
            pltpu.VMEM((5, cells, LANES), f32),
            pltpu.VMEM((5, cells, LANES), f32),
            pltpu.VMEM((2, 5, cells + 16, LANES), f32),
            pltpu.VMEM((3, 2, 5, TILE, LANES), f32),
            pltpu.VMEM((3, 2, 5, TILE, LANES), f32),
            pltpu.VMEM((2, 5, TILE, LANES), f32),
            pltpu.VMEM((3, 5, cells // 4, LANES), f32),
            pltpu.VMEM((3, 5, cells // 4, LANES), f32),
            pltpu.VMEM((5, 2 * cells + 8, LANES), f32),
            dma((chips,)), dma((chips,)), dma((chips,)), dma((chips,)),
            dma((3, 2)), dma((3, 2)), dma((3,)), dma((3,)), dma((4,)), dma((4,)),
        ],
        compiler_params=pltpu.CompilerParams(
            collective_id=0, has_side_effects=True, vmem_limit_bytes=56 * 2**20
        ),
    )(offsets, density, velocity, pressure)


def whole_step(density, velocity, pressure, offsets):
    ax_count, az_count = lax.axis_size("ax"), lax.axis_size("az")
    if ax_count == 2 and az_count == 8 and density.shape == (1, 2, 32, 512):
        return banded(az_count, density, velocity, pressure, offsets) * (1.0 / 3.0)
    return body(density, velocity, pressure, offsets)


def solution(mesh):
    placed = (
        P("row", "ax", "az", None),
        P("row", None, "ax", "az", None),
        P("row", "ax", "az", None),
        P(),
    )
    return jax.shard_map(
        whole_step,
        mesh=mesh,
        in_specs=placed,
        out_specs=P("row", None, "ax", "az", None),
        check_vma=False,
    )
```
